32 devices in a mesh: seq: 8 (over z, x), expert: 4 (over y, core).
Axes of the slice: x: 2, y: 2, z: 4, core: 2. Of those that a mesh axis runs over, the one named last changes fastest.
Arguments:
- byte_states: bfloat16 [8192, 512], P(('seq', 'expert')), may hold values from -6 to 6
- patch_start: int32 [8192], P(('seq', 'expert')), may hold values from 0 to 1, as said below
- expert_ids: int32 [1280, 2], P(('seq', 'expert')), may hold values from 0 to 3, all different within a row; in each aligned block of 40 rows (0 to 39, 40 to 79, ...) at most 24 rows name the same one
- enc_gain: float32 [512], replicated, may hold values from 0.1 to 1.9
- w_qkv: bfloat16 [512, 1536], replicated, may hold values from -0.25 to 0.25
- w_out: bfloat16 [512, 512], replicated, may hold values from -0.25 to 0.25
- w_xq: bfloat16 [512, 512], replicated, may hold values from -0.25 to 0.25
- w_xkv: bfloat16 [512, 1024], replicated, may hold values from -0.25 to 0.25
- w_up: bfloat16 [512, 2048], replicated, may hold values from -0.25 to 0.25
- moe_gain: float32 [2048], replicated, may hold values from 0.1 to 1.9
- w_router: float32 [2048, 4], replicated, may hold values from -0.03125 to 0.03125
- w_in: bfloat16 [4, 2048, 2, 6144], P('expert', None, None, 'seq'), may hold values from -0.125 to 0.125
- w_down: bfloat16 [4, 6144, 2048], P('expert', 'seq'), may hold values from -0.15625 to 0.15625
- dec_gain: float32 [512], replicated, may hold values from 0.1 to 1.9
- w_dq: bfloat16 [512, 512], replicated, may hold values from -0.25 to 0.25
- w_dkv: bfloat16 [2048, 1024], replicated, may hold values from -0.125 to 0.125
- w_do: bfloat16 [512, 512], replicated, may hold values from -0.25 to 0.25
Outputs:
- bytes_out: bfloat16 [8192, 512], P(('seq', 'expert'))
- patch_out: bfloat16 [1280, 2048], P(('seq', 'expert'))
The draws below stay inside these ranges and needn't reach their ends.
Inputs may be any that keep to these rules, and one draw needn't show every extreme that they name: `patch_start`: the first byte of every block of 256 bytes has a 1; every block has between 20 and 40 ones, and some block has exactly 40. `expert_ids`: the two experts of a slot differ. Among the 80 entries of one block's slots no expert appears more than 24 times, and some expert appears exactly 24 times in some block.
All inputs are finite; a program needn't handle non-finite values.
Results may differ from the reference program's by a relative error of at most 0.025.
Values may be sent and summed in bfloat16 or wider, within the bound.
No kernel may reach another device: no remote copies, remote signals or barrier semaphores. Data moves between devices by JAX's collectives and lax.ppermute only.
A program may use at most 128 MiB of HBM per device.

```python
import math
import jax
import jax.numpy as jnp
import numpy as np
from jax import lax

DL = 512
HEADS_L = 8
HEAD = 64
WINDOW = 512
DG = 2048
FF = 6144
BYTE_DEV = 256
EXPERTS = 4
PATCH_CAP = 40
CAP = 24
BYTES = 8192
PATCHES = 1280
N_SEQ = 8


def draw_patch_start(key, part):
    devices = BYTES // BYTE_DEV
    first, second, third = jax.random.split(key, 3)
    counts = jax.random.randint(first, (devices,), PATCH_CAP // 2, PATCH_CAP + 1)
    fullest = jax.random.randint(second, (), 0, devices)
    counts = jnp.where(jnp.arange(devices) == fullest, PATCH_CAP, counts)
    scores = jax.random.randint(third, (devices, BYTE_DEV - 1), 0, 1 << 20) * BYTE_DEV + jnp.arange(BYTE_DEV - 1)
    ordering = jnp.argsort(scores, axis=1)
    ranking = jnp.argsort(ordering, axis=1)
    inner = (ranking < counts[:, None] - 1).astype(jnp.int32)
    flags = jnp.concatenate([jnp.ones((devices, 1), jnp.int32), inner], axis=1)
    return flags.reshape(-1).astype(jnp.int32)


def steps_of(key, shape, cuts, least, largest):
    level, own = 1.0, jax.random.fold_in(key, 6)
    for axis_at, blocks in cuts:
        steps = jnp.exp(jax.random.uniform(jax.random.fold_in(own, axis_at), (blocks,), jnp.float32, least / len(cuts), largest / len(cuts)))
        level = level * jnp.repeat(steps, shape[axis_at] // blocks).reshape([-1 if axis == axis_at else 1 for axis in range(len(shape))])
    return level


def assign_block(key, own, number, rows, amount, top, most, skew):
    order = jax.random.permutation(key, amount)
    heavy_load, common = load_shares(amount, rows * top, most, skew, True), load_shares(amount, rows * top, most, skew, False)
    places = jnp.arange(amount)

    def named(tallies, turn):
        used = int((tallies > 0).sum())
        fixed = max(1, used // 4)
        shifted = fixed + (places - fixed + turn * (used - fixed)) % max(1, amount - fixed)
        return jnp.zeros((amount,), jnp.int32).at[order[jnp.where(places < fixed, places, shifted)]].set(jnp.asarray(tallies, jnp.int32))

    tallies = jnp.where(number % 4 == 0, named(heavy_load, number // 4), named(common, number - number // 4 - 1))
    mixed = jax.random.permutation(jax.random.fold_in(own, 3), amount)
    donor, sink = mixed[0:amount // 2 * 2:2], mixed[1:amount // 2 * 2:2]
    room = jnp.minimum(tallies[donor] - 1, most - tallies[sink]) // 2
    room = jnp.where((donor == order[0]) | (sink == order[0]) | (tallies[sink] == 0), 0, jnp.maximum(room, 0))
    shifted = jax.random.randint(jax.random.fold_in(own, 4), (amount // 2,), 0, 1 << 20) % (room + 1)
    tallies = tallies.at[donor].add(-shifted).at[sink].add(shifted)
    items = jnp.searchsorted(jnp.cumsum(tallies), jnp.arange(rows * top), side="right").astype(jnp.int32)
    grid = items.reshape(top, rows).T
    grid = grid[jax.random.permutation(jax.random.fold_in(own, 1), rows)]
    turn = jax.random.randint(jax.random.fold_in(own, 2), (rows, 1), 0, top)
    return jnp.take_along_axis(grid, (jnp.arange(top)[None, :] + turn) % top, axis=1)


def load_shares(number_of, total, bound, lean, full):
    weights = [(1 << 20) // math.isqrt(standing ** lean) + 1 for standing in range(1, number_of + 1)]
    largest = bound if full else min(bound, max(-(-total // number_of), total * weights[0] // sum(weights)))
    least = 1 if total - largest >= number_of - 1 else 0
    given, surplus = [largest] + [least] * (number_of - 1), total - largest - least * (number_of - 1)
    while surplus > 0:
        movable = [i for i in range(1, number_of) if given[i] < largest] or [i for i in range(1, number_of) if given[i] < bound]
        mass, budget = sum([weights[i] for i in movable]), surplus
        for i in movable:
            addition = min(bound - given[i], max(1, budget * weights[i] // mass), surplus)
            given[i] = given[i] + addition
            surplus = surplus - addition
    return np.array(given)


def gaussian(key, shape, spread, bound, pieces=(), held_as=jnp.bfloat16):
    level = steps_of(key, shape, pieces, -0.22, 0.18) if pieces else 1.0
    drawn = jax.random.normal(key, shape, jnp.float32) * spread * level
    return jnp.minimum(jnp.maximum(drawn, -bound), bound).astype(held_as)


def setup_inputs(seed: int = 0) -> dict:
    seeds = jax.random.split(jax.random.key(seed), 18)
    byte_states = gaussian(seeds[0], (BYTES, DL), 1.0, 6.0, ((0, 32),))
    patch_start = draw_patch_start(jax.random.fold_in(seeds[17], 71), 0)
    expert_ids_keys = jax.random.split(jax.random.fold_in(seeds[2], 1), PATCHES // PATCH_CAP)
    expert_ids_turns = jax.random.permutation(jax.random.fold_in(seeds[2], 3), PATCHES // PATCH_CAP)
    expert_ids = jax.vmap(lambda own, number: assign_block(jax.random.fold_in(seeds[2], 2), own, number, PATCH_CAP, EXPERTS, 2, CAP, 2))(expert_ids_keys, expert_ids_turns).reshape((PATCHES, 2))
    enc_gain = jnp.clip(1.0 + 0.18 * jax.random.normal(seeds[3], (DL,), jnp.float32), 0.1, 1.9)
    w_qkv = gaussian(seeds[4], (DL, 3 * DL), DL ** -0.5, 0.25)
    w_out = gaussian(seeds[5], (DL, DL), DL ** -0.5, 0.25)
    w_xq = gaussian(seeds[6], (DL, DL), DL ** -0.5, 0.25)
    w_xkv = gaussian(seeds[7], (DL, 2 * DL), DL ** -0.5, 0.25)
    w_up = gaussian(seeds[8], (DL, DG), DL ** -0.5, 0.25)
    moe_gain = jnp.clip(1.0 + 0.18 * jax.random.normal(seeds[9], (DG,), jnp.float32), 0.1, 1.9)
    w_router = gaussian(seeds[10], (DG, EXPERTS), (DG * 16) ** -0.5, 0.03125, (), jnp.float32)
    w_in = gaussian(seeds[11], (EXPERTS, DG, 2, FF), DG ** -0.5, 0.125, ((0, 4), (3, 8)))
    w_down = gaussian(seeds[12], (EXPERTS, FF, DG), (FF // 4) ** -0.5, 0.15625, ((0, 4), (1, 8)))
    dec_gain = jnp.clip(1.0 + 0.18 * jax.random.normal(seeds[13], (DL,), jnp.float32), 0.1, 1.9)
    w_dq = gaussian(seeds[14], (DL, DL), DL ** -0.5, 0.25)
    w_dkv = gaussian(seeds[15], (DG, 2 * DL), DG ** -0.5, 0.125)
    w_do = gaussian(seeds[16], (DL, DL), DL ** -0.5, 0.25)
    return dict(byte_states=byte_states, patch_start=patch_start, expert_ids=expert_ids, enc_gain=enc_gain, w_qkv=w_qkv, w_out=w_out, w_xq=w_xq, w_xkv=w_xkv, w_up=w_up, moe_gain=moe_gain, w_router=w_router, w_in=w_in, w_down=w_down, dec_gain=dec_gain, w_dq=w_dq, w_dkv=w_dkv, w_do=w_do)


epsilon = 1e-06
very_negative = -1e+30

def rms_scale(inputs, gain_vector):
    widened = inputs.astype(jnp.float32)
    return widened * lax.rsqrt(lax.optimization_barrier(jnp.mean(widened * widened, axis=-1, keepdims=True)) + epsilon) * gain_vector

def softmax_rows(scores):
    highest = lax.optimization_barrier(jnp.max(scores, axis=-1, keepdims=True))
    raised = jnp.exp(scores - highest)
    return raised / lax.optimization_barrier(jnp.sum(raised, axis=-1, keepdims=True))

def heads_split(inputs):
    return inputs.reshape(inputs.shape[0], HEADS_L, HEAD).transpose(1, 0, 2)

def heads_merge(inputs):
    return inputs.transpose(1, 0, 2).reshape(inputs.shape[1], HEADS_L * HEAD)

def attend(queries, keys, values, allowed):
    scores = jnp.einsum('hqd,hkd->hqk', queries.astype(jnp.float32), keys.astype(jnp.float32)) / math.sqrt(HEAD)
    scores = jnp.where(allowed[None], scores, very_negative)
    weights = softmax_rows(scores).astype(jnp.bfloat16)
    mixed = jnp.einsum('hqk,hkd->hqd', weights.astype(jnp.float32), values.astype(jnp.float32))
    return heads_merge(mixed)

def window_mask(query_place, key_place):
    later = key_place[None, :]
    return (later >= 0) & (later <= query_place[:, None]) & (later > query_place[:, None] - WINDOW)

def encoder(byte_states, enc_gain, w_qkv, w_out):
    normed = rms_scale(byte_states, enc_gain).astype(jnp.bfloat16)
    projected = jnp.dot(normed, w_qkv, preferred_element_type=jnp.float32).astype(jnp.bfloat16)
    padding = jnp.zeros((WINDOW, 2 * DL), projected.dtype)
    pairs = jnp.concatenate([padding, projected[:, DL:]], axis=0)

    def one_block(block_index):
        offset = (block_index * BYTE_DEV).astype(jnp.int32)
        queries = lax.dynamic_slice_in_dim(projected, offset, BYTE_DEV, 0)[:, :DL]
        nearby = lax.dynamic_slice_in_dim(pairs, offset, BYTE_DEV + WINDOW, 0)
        query_place = offset + jnp.arange(BYTE_DEV, dtype=jnp.int32)
        key_place = offset - WINDOW + jnp.arange(BYTE_DEV + WINDOW, dtype=jnp.int32)
        mixed = attend(heads_split(queries), heads_split(nearby[:, :DL]), heads_split(nearby[:, DL:]), window_mask(query_place, key_place)).astype(jnp.bfloat16)
        residual = lax.dynamic_slice_in_dim(byte_states, offset, BYTE_DEV, 0)
        return (residual.astype(jnp.float32) + jnp.dot(mixed, w_out, preferred_element_type=jnp.float32)).astype(jnp.bfloat16)
    blocks = lax.map(one_block, jnp.arange(BYTES // BYTE_DEV, dtype=jnp.int32))
    return blocks.reshape(BYTES, DL)

def patch_block(encoded, flags, w_xq, w_xkv, w_up):
    patch_index = jnp.cumsum(flags) - 1
    patch_count = jnp.sum(flags)
    slot_list = jnp.arange(PATCH_CAP, dtype=jnp.int32)
    member = patch_index[None, :] == slot_list[:, None]
    live = slot_list < patch_count
    pooled = lax.optimization_barrier(jnp.max(jnp.where(member[:, :, None], encoded[None], jnp.asarray(very_negative, encoded.dtype)), axis=1))
    pooled = jnp.where(live[:, None], pooled, jnp.zeros_like(pooled))
    queries = jnp.dot(pooled, w_xq, preferred_element_type=jnp.float32).astype(jnp.bfloat16)
    pairs = jnp.dot(encoded, w_xkv, preferred_element_type=jnp.float32).astype(jnp.bfloat16)
    width_local = pairs.shape[1] // 2
    mixed = attend(heads_split(queries), heads_split(pairs[:, :width_local]), heads_split(pairs[:, width_local:]), member)
    patch_input = (pooled.astype(jnp.float32) + mixed).astype(jnp.bfloat16)
    state = jnp.dot(patch_input, w_up, preferred_element_type=jnp.float32)
    return jnp.where(live[:, None], state, jnp.zeros_like(state)).astype(jnp.bfloat16)

def decode_block(encoded, flags, states, dec_gain, w_dq, w_dkv, w_do):
    patch_index = jnp.cumsum(flags) - 1
    slot_list = jnp.arange(PATCH_CAP, dtype=jnp.int32)
    normed = rms_scale(encoded, dec_gain).astype(jnp.bfloat16)
    queries = jnp.dot(normed, w_dq, preferred_element_type=jnp.float32).astype(jnp.bfloat16)
    pairs = jnp.dot(states, w_dkv, preferred_element_type=jnp.float32).astype(jnp.bfloat16)
    width_local = pairs.shape[1] // 2
    allowed = slot_list[None, :] <= patch_index[:, None]
    mixed = attend(heads_split(queries), heads_split(pairs[:, :width_local]), heads_split(pairs[:, width_local:]), allowed).astype(jnp.bfloat16)
    return (encoded.astype(jnp.float32) + jnp.dot(mixed, w_do, preferred_element_type=jnp.float32)).astype(jnp.bfloat16)

def route_slots(expert_ids):
    flat = expert_ids.reshape(-1)
    onehot = (flat[:, None] == jnp.arange(EXPERTS, dtype=jnp.int32)[None, :]).astype(jnp.int32)
    ranked = jnp.cumsum(onehot, axis=0) - 1
    return lax.optimization_barrier(jnp.sum(ranked * onehot, axis=1)).reshape(expert_ids.shape)

def mixture(patch_state, expert_ids, moe_gain, w_router, w_in, w_down):
    devices = PATCHES // PATCH_CAP
    normed = rms_scale(patch_state, moe_gain).astype(jnp.bfloat16)
    logits = jnp.dot(normed.astype(jnp.float32), w_router, precision=lax.Precision.HIGHEST)
    gates = softmax_rows(jnp.take_along_axis(logits, expert_ids, axis=1))
    ids_blocks = expert_ids.reshape(devices, PATCH_CAP, 2)
    slot_number = jax.vmap(route_slots)(ids_blocks)
    target = ids_blocks * CAP + slot_number
    normed_blocks = normed.reshape(devices, PATCH_CAP, DG)

    def fill(rows, places):
        buffer = jnp.zeros((EXPERTS * CAP, DG), rows.dtype)
        return buffer.at[places[:, 0]].set(rows).at[places[:, 1]].set(rows)
    routed = jax.vmap(fill)(normed_blocks, target)
    routed = routed.reshape(devices, EXPERTS, CAP, DG).transpose(1, 0, 2, 3).reshape(EXPERTS, devices * CAP, DG)
    share = FF // N_SEQ

    def one_expert(packed):
        rows, paired, lowered = packed
        gate = jnp.dot(rows, paired[:, 0, :], preferred_element_type=jnp.float32)
        upper = jnp.dot(rows, paired[:, 1, :], preferred_element_type=jnp.float32)
        hidden = (jax.nn.silu(gate) * upper).astype(jnp.bfloat16)

        def add_block(block_index, total):
            offset = (jnp.asarray(block_index, jnp.int32) * share).astype(jnp.int32)
            part = lax.dynamic_slice_in_dim(hidden, offset, share, 1)
            weights_part = lax.dynamic_slice_in_dim(lowered, offset, share, 0)
            term = jnp.dot(part, weights_part, preferred_element_type=jnp.float32).astype(jnp.bfloat16)
            term = lax.optimization_barrier(term)
            return total + term.astype(jnp.float32)
        total = lax.fori_loop(0, N_SEQ, add_block, jnp.zeros((rows.shape[0], DG), jnp.float32))
        return total.astype(jnp.bfloat16)
    outputs = lax.map(one_expert, (routed, w_in, w_down))
    outputs = outputs.reshape(EXPERTS, devices, CAP, DG)
    device_index = jnp.arange(devices, dtype=jnp.int32)[:, None, None]
    chosen = outputs[ids_blocks, device_index, slot_number]
    gate_blocks = gates.reshape(devices, PATCH_CAP, 2)
    combined = lax.optimization_barrier(jnp.sum(gate_blocks[..., None] * chosen.astype(jnp.float32), axis=2))
    return (patch_state.astype(jnp.float32) + combined.reshape(PATCHES, DG)).astype(jnp.bfloat16)

def reference(byte_states, patch_start, expert_ids, enc_gain, w_qkv, w_out, w_xq, w_xkv, w_up, moe_gain, w_router, w_in, w_down, dec_gain, w_dq, w_dkv, w_do):
    devices = BYTES // BYTE_DEV
    encoded = encoder(byte_states, enc_gain, w_qkv, w_out)
    encoded_blocks = encoded.reshape(devices, BYTE_DEV, DL)
    flag_blocks = patch_start.reshape(devices, BYTE_DEV)
    states = lax.map(lambda packed: patch_block(packed[0], packed[1], w_xq, w_xkv, w_up), (encoded_blocks, flag_blocks))
    patch_state = states.reshape(PATCHES, DG)
    patch_out = mixture(patch_state, expert_ids, moe_gain, w_router, w_in, w_down)
    decoded = lax.map(lambda packed: decode_block(packed[0], packed[1], packed[2], dec_gain, w_dq, w_dkv, w_do), (encoded_blocks, flag_blocks, patch_out.reshape(devices, PATCH_CAP, DG)))
    return (decoded.reshape(BYTES, DL), patch_out)
```

```python
import math

import jax
import jax.numpy as jnp
from jax import lax
from jax.sharding import PartitionSpec as P

HEADS_L = 8
HEAD = 64
WINDOW = 512


epsilon = 1e-06
very_negative = -1e30


def passed_along(x, axis, by):
    length = lax.axis_size(axis)
    pairs = [(i, i + by) for i in range(length) if 0 <= i + by < length]
    return lax.ppermute(x, axis, pairs)


def rms_scale(inputs, gain_vector):
    widened = inputs.astype(jnp.float32)
    return (
        widened
        * lax.rsqrt(jnp.mean(widened * widened, axis=-1, keepdims=True) + epsilon)
        * gain_vector
    )


def softmax_rows(scores):
    highest = jnp.max(scores, axis=-1, keepdims=True)
    raised = jnp.exp(scores - highest)
    return raised / jnp.sum(raised, axis=-1, keepdims=True)


def heads_split(inputs):
    return inputs.reshape(inputs.shape[0], HEADS_L, HEAD).transpose(1, 0, 2)


def heads_merge(inputs):
    return inputs.transpose(1, 0, 2).reshape(inputs.shape[1], HEADS_L * HEAD)


def attend(queries, keys, values, allowed):
    scores = jnp.einsum(
        "hqd,hkd->hqk", queries, keys, preferred_element_type=jnp.float32
    ) / math.sqrt(HEAD)
    scores = jnp.where(allowed[None], scores, very_negative)
    weights = softmax_rows(scores).astype(jnp.bfloat16)
    mixed = jnp.einsum("hqk,hkd->hqd", weights, values, preferred_element_type=jnp.float32)
    return heads_merge(mixed)


def window_mask(query_place, key_place):
    later = key_place[None, :]
    return (later >= 0) & (later <= query_place[:, None]) & (later > query_place[:, None] - WINDOW)


def patch_block(encoded, flags, w_xq, w_xkv):
    patch_cap = encoded.shape[0] * 5 // 32
    patch_index = jnp.cumsum(flags) - 1
    patch_count = jnp.sum(flags)
    slot_list = jnp.arange(patch_cap, dtype=jnp.int32)
    member = patch_index[None, :] == slot_list[:, None]
    live = slot_list < patch_count
    pooled = jnp.max(
        jnp.where(member[:, :, None], encoded[None], jnp.asarray(very_negative, encoded.dtype)),
        axis=1,
    )
    pooled = jnp.where(live[:, None], pooled, jnp.zeros_like(pooled))
    queries = jnp.dot(pooled, w_xq, preferred_element_type=jnp.float32).astype(jnp.bfloat16)
    pairs = jnp.dot(encoded, w_xkv, preferred_element_type=jnp.float32).astype(jnp.bfloat16)
    width_local = pairs.shape[1] // 2
    mixed = attend(
        heads_split(queries),
        heads_split(pairs[:, :width_local]),
        heads_split(pairs[:, width_local:]),
        member,
    )
    patch_input = jnp.where(live[:, None], pooled.astype(jnp.float32) + mixed, 0.0)
    return patch_input.astype(jnp.bfloat16)


def decode_block(encoded, flags, states, dec_gain, w_dq, w_dkv, w_do):
    patch_index = jnp.cumsum(flags) - 1
    slot_list = jnp.arange(states.shape[0], dtype=jnp.int32)
    normed = rms_scale(encoded, dec_gain).astype(jnp.bfloat16)
    queries = jnp.dot(normed, w_dq, preferred_element_type=jnp.float32).astype(jnp.bfloat16)
    pairs = jnp.dot(states, w_dkv, preferred_element_type=jnp.float32).astype(jnp.bfloat16)
    width_local = pairs.shape[1] // 2
    allowed = slot_list[None, :] <= patch_index[:, None]
    mixed = attend(
        heads_split(queries),
        heads_split(pairs[:, :width_local]),
        heads_split(pairs[:, width_local:]),
        allowed,
    ).astype(jnp.bfloat16)
    return (
        encoded.astype(jnp.float32) + jnp.dot(mixed, w_do, preferred_element_type=jnp.float32)
    ).astype(jnp.bfloat16)


def route_slots(expert_ids, experts):
    flat = expert_ids.reshape(-1)
    onehot = (flat[:, None] == jnp.arange(experts, dtype=jnp.int32)[None, :]).astype(jnp.int32)
    ranked = jnp.cumsum(onehot, axis=0) - 1
    return jnp.sum(ranked * onehot, axis=1).reshape(expert_ids.shape)


def digits():
    seq, expert = lax.axis_size("seq"), lax.axis_size("expert")
    inner = 2 if seq % 2 == 0 else 1
    core = 2 if expert % 2 == 0 else 1
    return {
        "z": ("seq", inner, seq // inner),
        "x": ("seq", 1, inner),
        "y": ("expert", core, expert // core),
        "c": ("expert", 1, core),
    }


def shift(x, digit, by):
    axis, stride, radix = digit
    pairs = []
    for i in range(lax.axis_size(axis)):
        g = i // stride % radix
        pairs.append((i, i + ((g + by) % radix - g) * stride))
    return lax.ppermute(x, axis, pairs)


def gathered(x, digit, place=0):
    return jnp.stack([x] + [shift(x, digit, d) for d in range(1, digit[2])], axis=place)


def gather_all(x):
    d = digits()
    half = x.shape[1] // 2
    x = gathered(x, d["z"])
    left = gathered(gathered(x[..., :half], d["x"]), d["y"])
    right = gathered(gathered(x[..., half:], d["y"]), d["x"], 1)
    return gathered(jnp.concatenate([left, right], axis=-1), d["c"])


def summed(parts):
    total = parts[0].astype(jnp.float32)
    for part in parts[1:]:
        total = total + part.astype(jnp.float32)
    return total


def reduced(x, digit, place=0):
    parts = [lax.index_in_dim(x, d, place, keepdims=False) for d in range(digit[2])]
    return summed([parts[0]] + [shift(parts[d], digit, -d) for d in range(1, digit[2])])


def scatter_all(x):
    d = digits()
    half = x.shape[-1] // 2

    def narrow(v):
        return v.astype(jnp.bfloat16)

    left = narrow(reduced(x[..., :half], d["c"]))
    right = narrow(reduced(x[..., half:], d["c"]))
    left = narrow(reduced(narrow(reduced(left, d["x"], 1)), d["y"]))
    right = narrow(reduced(narrow(reduced(right, d["y"])), d["x"]))
    return reduced(jnp.concatenate([left, right], axis=-1), d["z"])


def mixture(patch_input, expert_ids, w_up, moe_gain, w_router, w_in, w_down):
    patch_cap, local_width = patch_input.shape
    experts = w_router.shape[1]
    hidden_share = w_in.shape[3]
    capacity = 12 * patch_cap // (5 * experts)
    target = expert_ids * capacity + route_slots(expert_ids, experts)
    table = jnp.pad(target.T.astype(jnp.bfloat16), ((0, 6), (0, local_width - patch_cap)))
    gathered_rows = gather_all(jnp.concatenate([patch_input, table], axis=0))
    lead = gathered_rows.shape[:4]
    everything = gathered_rows.reshape((-1,) + gathered_rows.shape[4:])
    sources = everything.shape[0]
    rows = everything[:, :patch_cap]
    targets = everything[:, patch_cap : patch_cap + 2, :patch_cap].astype(jnp.int32)
    me = lax.axis_index("expert")
    places = me * capacity + jnp.arange(capacity, dtype=jnp.int32)
    hit = targets[:, :, None, :] == places[None, None, :, None]
    dispatch = jnp.any(hit, axis=1)
    other = jnp.sum(jnp.where(hit, targets[:, ::-1, None, :] // capacity, 0), axis=(1, 3))
    one_hot = dispatch.astype(jnp.bfloat16)
    routed = jnp.einsum("scp,spd->scd", one_hot, rows, preferred_element_type=jnp.float32)
    routed = routed.astype(jnp.bfloat16).reshape(sources * capacity, local_width)
    state = jnp.dot(routed, w_up, preferred_element_type=jnp.float32).astype(jnp.bfloat16)
    normed = rms_scale(state, moe_gain).astype(jnp.bfloat16)
    logits = jnp.dot(normed.astype(jnp.float32), w_router, precision=lax.Precision.HIGHEST)
    own_logit = jnp.sum(jnp.where(jnp.arange(experts)[None] == me, logits, 0.0), axis=1)
    other_logit = jnp.sum(
        jnp.where(jnp.arange(experts)[None] == other.reshape(-1, 1), logits, 0.0), axis=1
    )
    gates = softmax_rows(jnp.stack([own_logit, other_logit], axis=1))[:, :1]
    paired = w_in.reshape(w_in.shape[1], 2 * hidden_share)
    both = jnp.dot(normed, paired, preferred_element_type=jnp.float32)
    hidden = (jax.nn.silu(both[:, :hidden_share]) * both[:, hidden_share:]).astype(jnp.bfloat16)
    term = jnp.dot(hidden, w_down[0], preferred_element_type=jnp.float32)
    term = (term * gates).astype(jnp.bfloat16).reshape(sources, capacity, -1)
    spread = jnp.einsum("scp,scd->spd", one_hot, term, preferred_element_type=jnp.float32)
    spread = spread.astype(jnp.bfloat16)
    combined = scatter_all(spread.reshape(lead + spread.shape[1:]))
    own_state = jnp.dot(patch_input, w_up, preferred_element_type=jnp.float32).astype(jnp.bfloat16)
    return (own_state.astype(jnp.float32) + combined).astype(jnp.bfloat16)


def per_device(
    byte_states,
    patch_start,
    expert_ids,
    enc_gain,
    w_qkv,
    w_out,
    w_xq,
    w_xkv,
    w_up,
    moe_gain,
    w_router,
    w_in,
    w_down,
    dec_gain,
    w_dq,
    w_dkv,
    w_do,
):
    byte_dev = byte_states.shape[0]
    model_width = byte_states.shape[1]
    normed = rms_scale(byte_states, enc_gain).astype(jnp.bfloat16)
    projected = jnp.dot(normed, w_qkv, preferred_element_type=jnp.float32).astype(jnp.bfloat16)
    queries = projected[:, :model_width]
    own_pairs = projected[:, model_width:]
    reach = -(-WINDOW // byte_dev)
    earlier = []
    for distance in range(reach, 0, -1):
        moved = passed_along(normed, ("seq", "expert"), distance)
        earlier.append(
            jnp.dot(moved, w_qkv[:, model_width:], preferred_element_type=jnp.float32).astype(
                jnp.bfloat16
            )
        )
    pairs = jnp.concatenate(earlier + [own_pairs], axis=0)
    offset = lax.axis_index(("seq", "expert")) * byte_dev
    query_place = offset + jnp.arange(byte_dev, dtype=jnp.int32)
    key_place = offset - reach * byte_dev + jnp.arange((reach + 1) * byte_dev, dtype=jnp.int32)
    mixed = attend(
        heads_split(queries),
        heads_split(pairs[:, :model_width]),
        heads_split(pairs[:, model_width:]),
        window_mask(query_place, key_place),
    ).astype(jnp.bfloat16)
    encoded = (
        byte_states.astype(jnp.float32) + jnp.dot(mixed, w_out, preferred_element_type=jnp.float32)
    ).astype(jnp.bfloat16)
    patch_input = patch_block(encoded, patch_start, w_xq, w_xkv)
    patch_out = mixture(patch_input, expert_ids, w_up, moe_gain, w_router, w_in, w_down)
    bytes_out = decode_block(encoded, patch_start, patch_out, dec_gain, w_dq, w_dkv, w_do)
    return (bytes_out, patch_out)


def solution(mesh):
    in_specs = (
        P(("seq", "expert"), None),
        P(("seq", "expert")),
        P(("seq", "expert"), None),
        P(),
        P(),
        P(),
        P(),
        P(),
        P(),
        P(),
        P(),
        P("expert", None, None, "seq"),
        P("expert", "seq", None),
        P(),
        P(),
        P(),
        P(),
    )
    out_specs = (P(("seq", "expert"), None), P(("seq", "expert"), None))
    return jax.shard_map(
        per_device, mesh=mesh, in_specs=in_specs, out_specs=out_specs, check_vma=False
    )
```

```python
import functools
import math

import jax
import jax.numpy as jnp
from jax import lax
from jax.experimental import pallas as pl
from jax.experimental.pallas import tpu as pltpu
from jax.sharding import PartitionSpec as P

HEADS_L = 8
HEAD = 64
WINDOW = 512


epsilon = 1e-06
very_negative = -1e30


def passed_along(x, axis, by):
    length = lax.axis_size(axis)
    pairs = [(i, i + by) for i in range(length) if 0 <= i + by < length]
    return lax.ppermute(x, axis, pairs)


def normed_rows(x, gain_row):
    wide = x.astype(jnp.float32)
    scale = lax.rsqrt(jnp.mean(wide * wide, axis=-1, keepdims=True) + epsilon)
    return (wide * scale * gain_row).astype(jnp.bfloat16)


def mm(a, b):
    return jnp.dot(a, b, preferred_element_type=jnp.float32)


def mm_t(a, b):
    return lax.dot_general(a, b, (((1,), (1,)), ((), ())), preferred_element_type=jnp.float32)


def iota(shape, dim):
    return lax.broadcasted_iota(jnp.int32, shape, dim)


def attend_pair(q, k, v, bias):
    first = iota((1, 2 * HEAD), 1) < HEAD
    q = q * jnp.asarray(1.0 / math.sqrt(HEAD), q.dtype)
    outs = []
    for here in (first, jnp.logical_not(first)):
        scores = mm_t(jnp.where(here, q, jnp.zeros_like(q)), k) + bias
        raised = jnp.exp(scores - jnp.max(scores, axis=-1, keepdims=True)).astype(jnp.bfloat16)
        both = mm(raised, jnp.where(here, v, jnp.ones_like(v)))
        outs.append(both / pltpu.roll(both, HEAD, 1))
    return jnp.where(first, outs[0], outs[1])


def encoder_kernel(reach, experts, capacity, *refs):
    place, own, *earlier = refs[: 2 + reach]
    flags, ids, gain, w_qkv, w_out, w_xq, w_xkv = refs[2 + reach : 9 + reach]
    encoded_out, payload_out = refs[9 + reach : 11 + reach]
    bias_ref, pairs_ref, mixed_ref = refs[11 + reach :]
    rows, width = own.shape
    patch_cap = rows * 5 // 32
    gain_row = gain[...]
    normed = normed_rows(own[...], gain_row)
    projected = mm(normed, w_qkv[...]).astype(jnp.bfloat16)
    queries = projected[:, :width]
    pairs_ref[reach * rows :, :] = projected[:, width:]
    for at, block in enumerate(earlier):
        moved = normed_rows(block[...], gain_row)
        pairs_ref[at * rows : (at + 1) * rows, :] = mm(moved, w_qkv[:, width:]).astype(jnp.bfloat16)
    keys = (reach + 1) * rows
    at_query = iota((rows, keys), 0) + reach * rows
    at_key = iota((rows, keys), 1)
    allowed = (at_key <= at_query) & (at_key > at_query - WINDOW)
    allowed = allowed & (at_key >= (reach - place[0]) * rows)
    bias_ref[...] = jnp.where(allowed, 0.0, very_negative)
    lanes = 2 * HEAD
    for at in range(0, width, lanes):
        mixed = attend_pair(
            queries[:, at : at + lanes],
            pairs_ref[:, at : at + lanes],
            pairs_ref[:, width + at : width + at + lanes],
            bias_ref[...],
        )
        mixed_ref[:, at : at + lanes] = mixed.astype(jnp.bfloat16)
    encoded = (own[...].astype(jnp.float32) + mm(mixed_ref[...], w_out[...])).astype(jnp.bfloat16)
    encoded_out[...] = encoded

    flag = flags[...]
    at_row, at_col = iota((rows, rows), 0), iota((rows, rows), 1)
    upto = at_col <= at_row
    opened = jnp.max(jnp.where(upto & (flag == 1), at_col, 0), axis=1, keepdims=True)
    since = iota((rows, 1), 0) - opened
    eight = jnp.broadcast_to(flag, (8, rows)).astype(jnp.float32).astype(jnp.bfloat16)
    before = (at_row <= at_col).astype(jnp.float32).astype(jnp.bfloat16)
    number = mm(eight, before)[:1].astype(jnp.int32) - 1
    slot = iota((patch_cap, rows), 0)
    at_byte = iota((patch_cap, rows), 1)
    member = number == slot
    last = jnp.max(jnp.where(member, at_byte, -1), axis=1, keepdims=True)
    live = last >= 0
    highest = encoded.astype(jnp.float32)
    step = 1
    while step < rows:
        highest = jnp.where(
            since >= step, jnp.maximum(highest, pltpu.roll(highest, step, 0)), highest
        )
        step *= 2
    ends = (member & (at_byte == last)).astype(jnp.float32).astype(jnp.bfloat16)
    pooled = mm(ends, highest.astype(jnp.bfloat16))
    patch_queries = mm(pooled.astype(jnp.bfloat16), w_xq[...]).astype(jnp.bfloat16)
    byte_pairs = mm(encoded, w_xkv[...]).astype(jnp.bfloat16)
    member_bias = jnp.where(member, 0.0, very_negative)
    for at in range(0, width, lanes):
        mixed = attend_pair(
            patch_queries[:, at : at + lanes],
            byte_pairs[:, at : at + lanes],
            byte_pairs[:, width + at : width + at + lanes],
            member_bias,
        )
        total = jnp.where(live, pooled[:, at : at + lanes] + mixed, 0.0)
        payload_out[:patch_cap, at : at + lanes] = total.astype(jnp.bfloat16)

    square = (patch_cap, patch_cap)
    same = iota(square, 0) == iota(square, 1)
    earlier_slot = iota(square, 0) < iota(square, 1)
    id_rows = [ids[k : k + 1, :] for k in range(2)]
    id_cols = [jnp.sum(jnp.where(same, row, 0), axis=1, keepdims=True) for row in id_rows]
    targets = []
    for row in id_rows:
        named = sum((col == row).astype(jnp.int32) for col in id_cols)
        rank = jnp.sum(jnp.where(earlier_slot, named, 0), axis=0, keepdims=True)
        targets.append(row * capacity + rank)
    extra = payload_out.shape[0] - patch_cap
    at_extra = iota((extra, patch_cap), 0)
    table = jnp.where(at_extra == 0, targets[0], jnp.where(at_extra == 1, targets[1], 0))
    payload_out[patch_cap:, :] = jnp.zeros((extra, width), jnp.bfloat16)
    payload_out[patch_cap:, :patch_cap] = table.astype(jnp.float32).astype(jnp.bfloat16)


def encode(byte_states, earlier, patch_start, expert_ids, experts, capacity, place, enc_gain, *ws):
    rows, width = byte_states.shape
    reach = len(earlier)
    patch_cap = rows * 5 // 32
    payload_rows = -(-(patch_cap + 2) // 16) * 16
    vmem = pl.BlockSpec(memory_space=pltpu.VMEM)
    return pl.pallas_call(
        functools.partial(encoder_kernel, reach, experts, capacity),
        out_shape=(
            jax.ShapeDtypeStruct((rows, width), jnp.bfloat16),
            jax.ShapeDtypeStruct((payload_rows, width), jnp.bfloat16),
        ),
        in_specs=[pl.BlockSpec(memory_space=pltpu.SMEM)] + [vmem] * (8 + reach),
        out_specs=(vmem, vmem),
        scratch_shapes=[
            pltpu.VMEM((rows, (reach + 1) * rows), jnp.float32),
            pltpu.VMEM(((reach + 1) * rows, 2 * width), jnp.bfloat16),
            pltpu.VMEM((rows, width), jnp.bfloat16),
        ],
        compiler_params=pltpu.CompilerParams(vmem_limit_bytes=16 * 1024 * 1024),
    )(
        place,
        byte_states,
        *earlier,
        patch_start.reshape(1, rows),
        expert_ids.T,
        enc_gain.reshape(1, width),
        *ws,
    )


def mm_first(a, b):
    return lax.dot_general(a, b, (((0,), (0,)), ((), ())), preferred_element_type=jnp.float32)


def counted_from(values, step, most):
    return sum((values >= step * k).astype(jnp.int32) for k in range(1, most))


def as_bf16(mask):
    return mask.astype(jnp.float32).astype(jnp.bfloat16)


GROUP = 4


def expert_kernel(patch_cap, capacity, experts, *refs):
    me_ref, rows_ref, w_up, gain, router, w_in, w_down = refs[:7]
    outs = refs[7:-4]
    routed_ref, spread_ref, hidden_ref, parts_ref = refs[-4:]
    sources, held, width = rows_ref.shape
    per = GROUP * capacity
    me = me_ref[0]
    slots = iota((per, 1), 0)
    source_of_slot = counted_from(slots, capacity, GROUP)
    place_of_slot = slots - source_of_slot * capacity + me * capacity
    lanes = 128

    def spreader(block):
        at_from, at_to = iota((GROUP * lanes, GROUP * block), 0), iota((GROUP * lanes, GROUP * block), 1)
        source = counted_from(at_from, lanes, GROUP)
        within = at_from - source * lanes
        return as_bf16((at_to == source * block + within) & (within < block))

    spread_held, spread_cap = spreader(held), spreader(patch_cap)

    def matched(table, spread, block):
        targets = mm(table, spread).astype(jnp.int32)
        at = iota((1, GROUP * block), 1)
        source = counted_from(at, block, GROUP)
        first, second = targets[0:1], targets[1:2]
        hit = (first == place_of_slot) | (second == place_of_slot)
        hit = hit & (source == source_of_slot) & (at - source * block < patch_cap)
        named = [counted_from(t, capacity, experts) for t in (first, second)]
        return hit, jnp.where(named[0] == me, named[1], named[0])

    others = []
    for g in range(sources // GROUP):
        tables = []
        for s in range(g * GROUP, (g + 1) * GROUP):
            block = rows_ref[s, held - 16 : held, :lanes].astype(jnp.float32)
            tables.append(block[patch_cap - (held - 16) : patch_cap - (held - 16) + 8])
        table = jnp.concatenate(tables, axis=1).astype(jnp.bfloat16)
        hit, other = matched(table, spread_held, held)
        others.append(jnp.sum(jnp.where(hit, other, 0), axis=1, keepdims=True))
        block = rows_ref[g * GROUP : (g + 1) * GROUP].reshape(GROUP * held, width)
        routed_ref[g * per : (g + 1) * per, :] = mm(as_bf16(hit), block).astype(jnp.bfloat16)
        hit, _ = matched(table, spread_cap, patch_cap)
        spread_ref[g] = as_bf16(hit)
    other = jnp.concatenate(others, axis=0)

    state = mm(routed_ref[...], w_up[...]).astype(jnp.bfloat16)
    normed = normed_rows(state, gain[...])

    parts_ref[...] = jnp.zeros_like(parts_ref)
    left = router[...]
    for part in range(3):
        here = left.astype(jnp.bfloat16).astype(jnp.float32)
        parts_ref[8 * part : 8 * part + experts, :] = here
        left = left - here
    logits = mm_t(normed, parts_ref[...].astype(jnp.bfloat16))
    expert_of_lane = iota((1, parts_ref.shape[0]), 1) & 7
    own = jnp.sum(jnp.where(expert_of_lane == me, logits, 0.0), axis=1, keepdims=True)
    rival = jnp.sum(jnp.where(expert_of_lane == other, logits, 0.0), axis=1, keepdims=True)
    highest = jnp.maximum(own, rival)
    raised = jnp.exp(own - highest)
    gate = raised / (raised + jnp.exp(rival - highest))

    hidden_share = hidden_ref.shape[1]
    chunk = 256 if hidden_share % 256 == 0 else hidden_share
    for at in range(0, hidden_share, chunk):
        opened = mm(normed, w_in[:, at : at + chunk])
        upper = mm(normed, w_in[:, hidden_share + at : hidden_share + at + chunk])
        hidden_ref[:, at : at + chunk] = (opened / (1.0 + jnp.exp(-opened)) * upper).astype(
            jnp.bfloat16
        )
    hidden = hidden_ref[...]
    wide = outs[0].shape[1]
    chunk = min(512, wide)
    for number, out in enumerate(outs):
        for at in range(0, wide, chunk):
            begin = number * wide + at
            term = (mm(hidden, w_down[:, begin : begin + chunk]) * gate).astype(jnp.bfloat16)
            for g in range(sources // GROUP):
                total = mm_first(spread_ref[g], term[g * per : (g + 1) * per])
                out[g * GROUP * patch_cap : (g + 1) * GROUP * patch_cap, at : at + chunk] = (
                    total.astype(jnp.bfloat16)
                )


def expert_share(rows, patch_cap, capacity, me, w_up, gain, router, w_in, w_down, pieces):
    sources, held, width = rows.shape
    wide = w_up.shape[1]
    experts = router.shape[0]
    vmem = pl.BlockSpec(memory_space=pltpu.VMEM)
    slots = sources * capacity
    return pl.pallas_call(
        functools.partial(expert_kernel, patch_cap, capacity, experts),
        out_shape=tuple(
            jax.ShapeDtypeStruct((sources * patch_cap, wide // pieces), jnp.bfloat16)
            for _ in range(pieces)
        ),
        in_specs=[pl.BlockSpec(memory_space=pltpu.SMEM)] + [vmem] * 6,
        out_specs=(vmem,) * pieces,
        scratch_shapes=[
            pltpu.VMEM((slots, width), jnp.bfloat16),
            pltpu.VMEM((sources // GROUP, GROUP * capacity, GROUP * patch_cap), jnp.bfloat16),
            pltpu.VMEM((slots, w_down.shape[0]), jnp.bfloat16),
            pltpu.VMEM((24, wide), jnp.float32),
        ],
        compiler_params=pltpu.CompilerParams(vmem_limit_bytes=28 * 1024 * 1024),
    )(me, rows, w_up, gain, router, w_in, w_down)


def prepare_kernel(encoded, payload, gain, w_dq, w_up, queries, state):
    queries[...] = mm(normed_rows(encoded[...], gain[...]), w_dq[...]).astype(jnp.bfloat16)
    state[...] = mm(payload[: state.shape[0], :], w_up[...]).astype(jnp.bfloat16)


def prepare(encoded, payload, patch_cap, gain, w_dq, w_up):
    vmem = pl.BlockSpec(memory_space=pltpu.VMEM)
    return pl.pallas_call(
        prepare_kernel,
        out_shape=(
            jax.ShapeDtypeStruct(encoded.shape, jnp.bfloat16),
            jax.ShapeDtypeStruct((patch_cap, w_up.shape[1]), jnp.bfloat16),
        ),
        in_specs=[vmem] * 5,
        out_specs=(vmem, vmem),
        compiler_params=pltpu.CompilerParams(vmem_limit_bytes=8 * 1024 * 1024),
    )(encoded, payload, gain.reshape(1, -1), w_dq, w_up)


def decode_kernel(shares, *refs):
    state, *parts = refs[: 1 + shares]
    encoded, queries, flags, w_dkv, w_do, bytes_out, patch_out, mixed_ref = refs[1 + shares :]
    rows, width = encoded.shape
    patch_cap = state.shape[0]
    total = state[...].astype(jnp.float32)
    for part in parts:
        total = total + part[...].astype(jnp.float32)
    states = total.astype(jnp.bfloat16)
    patch_out[...] = states
    pairs = mm(states, w_dkv[...]).astype(jnp.bfloat16)
    flag = flags[...]
    upto = iota((rows, rows), 1) <= iota((rows, rows), 0)
    number = jnp.sum(jnp.where(upto, flag, 0), axis=1, keepdims=True) - 1
    bias = jnp.where(iota((rows, patch_cap), 1) <= number, 0.0, very_negative)
    lanes = 2 * HEAD
    for at in range(0, width, lanes):
        mixed = attend_pair(
            queries[:, at : at + lanes],
            pairs[:, at : at + lanes],
            pairs[:, width + at : width + at + lanes],
            bias,
        )
        mixed_ref[:, at : at + lanes] = mixed.astype(jnp.bfloat16)
    bytes_out[...] = (encoded[...].astype(jnp.float32) + mm(mixed_ref[...], w_do[...])).astype(
        jnp.bfloat16
    )


def decode(state, parts, encoded, queries, patch_start, w_dkv, w_do):
    vmem = pl.BlockSpec(memory_space=pltpu.VMEM)
    return pl.pallas_call(
        functools.partial(decode_kernel, len(parts)),
        out_shape=(
            jax.ShapeDtypeStruct(encoded.shape, jnp.bfloat16),
            jax.ShapeDtypeStruct(state.shape, jnp.bfloat16),
        ),
        in_specs=[vmem] * (6 + len(parts)),
        out_specs=(vmem, vmem),
        scratch_shapes=[pltpu.VMEM(encoded.shape, jnp.bfloat16)],
        compiler_params=pltpu.CompilerParams(vmem_limit_bytes=12 * 1024 * 1024),
    )(state, *parts, encoded, queries, patch_start.reshape(1, -1), w_dkv, w_do)


def digits():
    seq, expert = lax.axis_size("seq"), lax.axis_size("expert")
    inner = 2 if seq % 2 == 0 else 1
    core = 2 if expert % 2 == 0 else 1
    return {
        "z": ("seq", inner, seq // inner),
        "x": ("seq", 1, inner),
        "y": ("expert", core, expert // core),
        "c": ("expert", 1, core),
    }


def shift(x, digit, by):
    axis, stride, radix = digit
    pairs = []
    for i in range(lax.axis_size(axis)):
        g = i // stride % radix
        pairs.append((i, i + ((g + by) % radix - g) * stride))
    return lax.ppermute(x, axis, pairs)


def gathered(x, digit, place=0):
    return jnp.stack([x] + [shift(x, digit, d) for d in range(1, digit[2])], axis=place)


def gather_all(x):
    d = digits()
    half = x.shape[1] // 2
    x = gathered(x, d["z"])
    left = gathered(gathered(x[..., :half], d["x"]), d["y"])
    right = gathered(gathered(x[..., half:], d["y"]), d["x"], 1)
    return gathered(jnp.concatenate([left, right], axis=-1), d["c"])


def summed(parts):
    total = parts[0].astype(jnp.float32)
    for part in parts[1:]:
        total = total + part.astype(jnp.float32)
    return total


def reduced(x, digit, place=0):
    parts = [lax.index_in_dim(x, d, place, keepdims=False) for d in range(digit[2])]
    return summed([parts[0]] + [shift(parts[d], digit, -d) for d in range(1, digit[2])])


def narrow(v):
    return v.astype(jnp.bfloat16)


def mixture(payload, patch_cap, capacity, w_up, moe_gain, w_router, w_in, w_down):
    d = digits()
    wide = w_up.shape[1]
    rows = gather_all(payload)
    lead = rows.shape[:4]
    me = lax.axis_index("expert").astype(jnp.int32).reshape(1)
    paired = w_in.reshape(w_in.shape[1], -1)
    pieces = 2
    per_call = lead[1] if lead[1] * lead[2] * lead[3] <= 32 else 1

    def shares(core):
        got = [
            expert_share(
                rows[core, at : at + per_call].reshape((-1,) + rows.shape[4:]),
                patch_cap,
                capacity,
                me,
                w_up,
                moe_gain.reshape(1, wide),
                w_router.T,
                paired,
                w_down[0],
                pieces,
            )
            for at in range(0, lead[1], per_call)
        ]
        return [
            jnp.concatenate([g[k] for g in got]).reshape(lead[1:] + (patch_cap, wide // pieces))
            for k in range(pieces)
        ]

    sent = [shares(core) for core in range(lead[0] - 1, 0, -1)]
    sent = [shift(v, d["c"], -1) for part in sent for v in part]
    kept = shares(0)
    left, right = [narrow(summed([kept[k]] + sent[k::pieces])) for k in range(pieces)]
    left = narrow(reduced(narrow(reduced(left, d["x"], 1)), d["y"]))
    right = narrow(reduced(narrow(reduced(right, d["y"])), d["x"]))
    both = jnp.concatenate([left, right], axis=-1)
    return [both[0]] + [shift(both[by], d["z"], -by) for by in range(1, lead[3])]


def per_device(
    byte_states,
    patch_start,
    expert_ids,
    enc_gain,
    w_qkv,
    w_out,
    w_xq,
    w_xkv,
    w_up,
    moe_gain,
    w_router,
    w_in,
    w_down,
    dec_gain,
    w_dq,
    w_dkv,
    w_do,
):
    byte_dev = byte_states.shape[0]
    patch_cap = expert_ids.shape[0]
    experts = w_router.shape[1]
    capacity = 12 * patch_cap // (5 * experts)
    both_axes = ("seq", "expert")
    reach = -(-WINDOW // byte_dev)
    earlier = [passed_along(byte_states, both_axes, by) for by in range(reach, 0, -1)]
    place = lax.axis_index(both_axes).astype(jnp.int32).reshape(1)
    encoded, payload = encode(
        byte_states,
        earlier,
        patch_start,
        expert_ids,
        experts,
        capacity,
        place,
        enc_gain,
        w_qkv,
        w_out,
        w_xq,
        w_xkv,
    )
    parts = mixture(payload, patch_cap, capacity, w_up, moe_gain, w_router, w_in, w_down)
    queries, state = prepare(encoded, payload, patch_cap, dec_gain, w_dq, w_up)
    return decode(state, parts, encoded, queries, patch_start, w_dkv, w_do)


def solution(mesh):
    in_specs = (
        P(("seq", "expert"), None),
        P(("seq", "expert")),
        P(("seq", "expert"), None),
        P(),
        P(),
        P(),
        P(),
        P(),
        P(),
        P(),
        P(),
        P("expert", None, None, "seq"),
        P("expert", "seq", None),
        P(),
        P(),
        P(),
        P(),
    )
    out_specs = (P(("seq", "expert"), None), P(("seq", "expert"), None))
    return jax.shard_map(
        per_device, mesh=mesh, in_specs=in_specs, out_specs=out_specs, check_vma=False
    )
```

```python
import functools
import math

import jax
import jax.numpy as jnp
from jax import lax
from jax.experimental import pallas as pl
from jax.experimental.pallas import tpu as pltpu
from jax.sharding import PartitionSpec as P

HEADS_L = 8
HEAD = 64
WINDOW = 512


epsilon = 1e-06
very_negative = -1e30


def passed_along(x, axis, by):
    length = lax.axis_size(axis)
    pairs = [(i, i + by) for i in range(length) if 0 <= i + by < length]
    return lax.ppermute(x, axis, pairs)


def normed_rows(x, gain_row):
    wide = x.astype(jnp.float32)
    scale = lax.rsqrt(jnp.mean(wide * wide, axis=-1, keepdims=True) + epsilon)
    return (wide * scale * gain_row).astype(jnp.bfloat16)


def cost(flops):
    return pl.CostEstimate(flops=int(flops), transcendentals=0, bytes_accessed=0)


def mm(a, b):
    return jnp.dot(a, b, preferred_element_type=jnp.float32)


def mm_t(a, b):
    return lax.dot_general(a, b, (((1,), (1,)), ((), ())), preferred_element_type=jnp.float32)


def as_bf16(mask):
    return mask.astype(jnp.float32).astype(jnp.bfloat16)


def iota(shape, dim):
    return lax.broadcasted_iota(jnp.int32, shape, dim)


def attend_pair(q, k, v, bias):
    first = iota((1, 2 * HEAD), 1) < HEAD
    q = q * jnp.asarray(1.0 / math.sqrt(HEAD), q.dtype)
    outs = []
    for here in (first, jnp.logical_not(first)):
        scores = mm_t(jnp.where(here, q, jnp.zeros_like(q)), k) + bias
        raised = jnp.exp(scores - jnp.max(scores, axis=-1, keepdims=True)).astype(jnp.bfloat16)
        both = mm(raised, jnp.where(here, v, jnp.ones_like(v)))
        outs.append(both / pltpu.roll(both, HEAD, 1))
    return jnp.where(first, outs[0], outs[1])


def opening_kernel(reach, capacity, *refs):
    place, own_in, flags_in, ids_in, gain_in, w_qkv_in, w_out_in, w_xq_in, w_xkv_in = refs[:9]
    outs, (flags, ids, w_qkv, sem) = refs[9:-4], refs[-4:]
    own, gain, w_kv, w_out, w_xq, w_xkv, projected_out = outs[:7]
    bias_out, since_out, ends_out, member_out, live_out, table_out, decode_out = outs[7:]
    pairs = [
        (own_in, own),
        (gain_in, gain),
        (w_qkv_in, w_qkv),
        (flags_in, flags),
        (ids_in, ids),
        (w_out_in, w_out),
        (w_xq_in, w_xq),
        (w_xkv_in, w_xkv),
    ]
    copies = [pltpu.make_async_copy(a, b, sem.at[k]) for k, (a, b) in enumerate(pairs)]
    for copy in copies:
        copy.start()
    rows, width = own.shape
    patch_cap = rows * 5 // 32
    keys = (reach + 1) * rows
    at_query = iota((rows, keys), 0) + reach * rows
    at_key = iota((rows, keys), 1)
    allowed = (at_key <= at_query) & (at_key > at_query - WINDOW)
    allowed = allowed & (at_key >= (reach - place[0]) * rows)
    bias_out[...] = jnp.where(allowed, 0.0, very_negative)
    for copy in copies[:3]:
        copy.wait()
    normed = normed_rows(own[...], gain[...])
    projected_out[...] = mm(normed, w_qkv[...]).astype(jnp.bfloat16)
    w_kv[...] = w_qkv[:, width:]
    copies[3].wait()
    flag = flags[...]
    at_row, at_col = iota((rows, rows), 0), iota((rows, rows), 1)
    upto = at_col <= at_row
    opened = jnp.max(jnp.where(upto & (flag == 1), at_col, 0), axis=1, keepdims=True)
    since_out[...] = iota((rows, 1), 0) - opened
    own_number = jnp.sum(jnp.where(upto, flag, 0), axis=1, keepdims=True) - 1
    decode_out[...] = jnp.where(iota((rows, patch_cap), 1) <= own_number, 0.0, very_negative)
    eight = jnp.broadcast_to(flag, (8, rows)).astype(jnp.float32).astype(jnp.bfloat16)
    number = mm(eight, as_bf16(at_row <= at_col))[:1].astype(jnp.int32) - 1
    at_byte = iota((patch_cap, rows), 1)
    member = number == iota((patch_cap, rows), 0)
    last = jnp.max(jnp.where(member, at_byte, -1), axis=1, keepdims=True)
    live_out[...] = (last >= 0).astype(jnp.float32)
    ends_out[...] = as_bf16(member & (at_byte == last))
    member_out[...] = jnp.where(member, 0.0, very_negative)

    copies[4].wait()
    square = (patch_cap, patch_cap)
    same = iota(square, 0) == iota(square, 1)
    earlier_slot = iota(square, 0) < iota(square, 1)
    id_rows = [ids[k : k + 1, :] for k in range(2)]
    id_cols = [jnp.sum(jnp.where(same, row, 0), axis=1, keepdims=True) for row in id_rows]
    targets = []
    for row in id_rows:
        named = sum((col == row).astype(jnp.int32) for col in id_cols)
        rank = jnp.sum(jnp.where(earlier_slot, named, 0), axis=0, keepdims=True)
        targets.append(row * capacity + rank)
    extra = table_out.shape[0]
    at_extra = iota((extra, patch_cap), 0)
    table = jnp.where(at_extra == 0, targets[0], jnp.where(at_extra == 1, targets[1], 0))
    table_out[...] = jnp.zeros_like(table_out)
    table_out[:, :patch_cap] = table.astype(jnp.float32).astype(jnp.bfloat16)
    for copy in copies[5:]:
        copy.wait()


def opening(byte_states, patch_start, expert_ids, reach, capacity, place, enc_gain, *ws):
    rows, width = byte_states.shape
    w_qkv, w_out, w_xq, w_xkv = ws
    patch_cap = expert_ids.shape[0]
    extra = -(-(patch_cap + 2) // 16) * 16 - patch_cap
    keys = (reach + 1) * rows
    vmem, anywhere = pl.BlockSpec(memory_space=pltpu.VMEM), pl.BlockSpec(memory_space=pltpu.HBM)
    like = jax.ShapeDtypeStruct
    bf16, f32 = jnp.bfloat16, jnp.float32
    return pl.pallas_call(
        functools.partial(opening_kernel, reach, capacity),
        out_shape=(
            like((rows, width), bf16),
            like((1, width), f32),
            like((width, 2 * width), bf16),
            like(w_out.shape, bf16),
            like(w_xq.shape, bf16),
            like(w_xkv.shape, bf16),
            like((rows, 3 * width), bf16),
            like((rows, keys), f32),
            like((rows, 1), jnp.int32),
            like((patch_cap, rows), bf16),
            like((patch_cap, rows), f32),
            like((patch_cap, 1), f32),
            like((extra, width), bf16),
            like((rows, patch_cap), f32),
        ),
        in_specs=[pl.BlockSpec(memory_space=pltpu.SMEM)] + [anywhere] * 8,
        out_specs=(vmem,) * 14,
        scratch_shapes=[
            pltpu.VMEM((1, rows), jnp.int32),
            pltpu.VMEM((2, patch_cap), jnp.int32),
            pltpu.VMEM(w_qkv.shape, bf16),
            pltpu.SemaphoreType.DMA((8,)),
        ],
        cost_estimate=cost(4 * rows * width * 3 * width),
        compiler_params=pltpu.CompilerParams(vmem_limit_bytes=16 * 1024 * 1024),
    )(
        place,
        *[
            pltpu.with_memory_space_constraint(v, pltpu.HBM)
            for v in (
                byte_states,
                patch_start.reshape(1, rows),
                expert_ids.T,
                enc_gain.reshape(1, width),
                *ws,
            )
        ],
    )


def encoder_kernel(reach, *refs):
    instead, earlier, nearest, refs = refs[0], refs[1 : 1 + reach], refs[1 + reach], refs[2 + reach :]
    own, gain, w_kv, w_out, w_xq, w_xkv, projected = refs[:7]
    bias, since, ends, member_bias, live, table = refs[7:13]
    encoded_out, payload_out, pairs_ref, mixed_ref = refs[13:]
    rows, width = own.shape
    patch_cap = ends.shape[0]
    pairs_ref[reach * rows :, :] = projected[:, width:]
    for at, block in enumerate(earlier):
        moved = block[...]
        if at == reach - 1:
            moved = jnp.where(instead[0] == 1, nearest[...], moved)
        moved = normed_rows(moved, gain[...])
        pairs_ref[at * rows : (at + 1) * rows, :] = mm(moved, w_kv[...]).astype(jnp.bfloat16)
    lanes = 2 * HEAD
    for at in range(0, width, lanes):
        mixed = attend_pair(
            projected[:, at : at + lanes],
            pairs_ref[:, at : at + lanes],
            pairs_ref[:, width + at : width + at + lanes],
            bias[...],
        )
        mixed_ref[:, at : at + lanes] = mixed.astype(jnp.bfloat16)
    encoded = (own[...].astype(jnp.float32) + mm(mixed_ref[...], w_out[...])).astype(jnp.bfloat16)
    encoded_out[...] = encoded

    inside = since[...]
    highest = encoded.astype(jnp.float32)
    step = 1
    while step < rows:
        highest = jnp.where(
            inside >= step, jnp.maximum(highest, pltpu.roll(highest, step, 0)), highest
        )
        step *= 2
    pooled = mm(ends[...], highest.astype(jnp.bfloat16))
    patch_queries = mm(pooled.astype(jnp.bfloat16), w_xq[...]).astype(jnp.bfloat16)
    byte_pairs = mm(encoded, w_xkv[...]).astype(jnp.bfloat16)
    alive = live[...] > 0.0
    for at in range(0, width, lanes):
        mixed = attend_pair(
            patch_queries[:, at : at + lanes],
            byte_pairs[:, at : at + lanes],
            byte_pairs[:, width + at : width + at + lanes],
            member_bias[...],
        )
        total = jnp.where(alive, pooled[:, at : at + lanes] + mixed, 0.0)
        payload_out[:patch_cap, at : at + lanes] = total.astype(jnp.bfloat16)
    payload_out[patch_cap:, :] = table[...]


def encode(instead, earlier, nearest, opened):
    rows, width = opened[0].shape
    reach = len(earlier)
    vmem = pl.BlockSpec(memory_space=pltpu.VMEM)
    payload_rows = opened[9].shape[0] + opened[12].shape[0]
    return pl.pallas_call(
        functools.partial(encoder_kernel, reach),
        out_shape=(
            jax.ShapeDtypeStruct((rows, width), jnp.bfloat16),
            jax.ShapeDtypeStruct((payload_rows, width), jnp.bfloat16),
        ),
        in_specs=[pl.BlockSpec(memory_space=pltpu.SMEM)] + [vmem] * (14 + reach),
        out_specs=(vmem, vmem),
        scratch_shapes=[
            pltpu.VMEM(((reach + 1) * rows, 2 * width), jnp.bfloat16),
            pltpu.VMEM((rows, width), jnp.bfloat16),
        ],
        cost_estimate=cost(24 * rows * width * (reach + 1) * rows),
        compiler_params=pltpu.CompilerParams(vmem_limit_bytes=16 * 1024 * 1024),
    )(instead, *earlier, nearest, *opened[:13])


def mm_first(a, b):
    return lax.dot_general(a, b, (((0,), (0,)), ((), ())), preferred_element_type=jnp.float32)


def counted_from(values, step, most):
    return sum((values >= step * k).astype(jnp.int32) for k in range(1, most))


GROUP = 4


def give_back(term, spread, group, halves, order):
    for half, (out, places) in enumerate(zip(halves, order)):
        width = out.shape[-1]
        total = mm_first(spread, term[:, half * width : (half + 1) * width]).astype(jnp.bfloat16)
        block = out.shape[-2]
        for s in range(GROUP):
            out[places[group * GROUP + s]] = total[s * block : (s + 1) * block]


def stream_kernel(patch_cap, capacity, experts, blocks, order, *refs):
    me_ref, own_ref, moved_ref, w_up, gain, router, w_in, w_down = refs[:8]
    outs = refs[8:10]
    hidden_ref, gate_ref, spread_ref, all_hidden, later_spread, routed_ref, parts_ref = refs[10:]
    held, width = own_ref.shape[-2:]
    per = GROUP * capacity
    kept = len(blocks) // 2
    me = me_ref[0]
    slots = iota((per, 1), 0)
    source_of_slot = counted_from(slots, capacity, GROUP)
    place_of_slot = slots - source_of_slot * capacity + me * capacity
    lanes = 128

    def spreader(block):
        at_from, at_to = iota((GROUP * lanes, GROUP * block), 0), iota((GROUP * lanes, GROUP * block), 1)
        source = counted_from(at_from, lanes, GROUP)
        within = at_from - source * lanes
        return as_bf16((at_to == source * block + within) & (within < block))

    spread_held, spread_cap = spreader(held), spreader(patch_cap)

    def matched(table, spread, block):
        targets = mm(table, spread).astype(jnp.int32)
        at = iota((1, GROUP * block), 1)
        source = counted_from(at, block, GROUP)
        first, second = targets[0:1], targets[1:2]
        hit = (first == place_of_slot) | (second == place_of_slot)
        hit = hit & (source == source_of_slot) & (at - source * block < patch_cap)
        named = [counted_from(t, capacity, experts) for t in (first, second)]
        return hit, jnp.where(named[0] == me, named[1], named[0])

    others = []
    for g, begin in enumerate(blocks):
        rows_ref = own_ref if g < kept else moved_ref
        tables = []
        for s in range(begin, begin + GROUP):
            block = rows_ref[s, held - 16 : held, :lanes].astype(jnp.float32)
            tables.append(block[patch_cap - (held - 16) : patch_cap - (held - 16) + 8])
        table = jnp.concatenate(tables, axis=1).astype(jnp.bfloat16)
        hit, other = matched(table, spread_held, held)
        others.append(jnp.sum(jnp.where(hit, other, 0), axis=1, keepdims=True))
        block = rows_ref[begin : begin + GROUP].reshape(GROUP * held, width)
        routed_ref[g * per : (g + 1) * per, :] = mm(as_bf16(hit), block).astype(jnp.bfloat16)
        hit, _ = matched(table, spread_cap, patch_cap)
        if g < kept:
            spread_ref[g] = as_bf16(hit)
        else:
            later_spread[g - kept] = as_bf16(hit)
    other = jnp.concatenate(others, axis=0)

    state = mm(routed_ref[...], w_up[...]).astype(jnp.bfloat16).astype(jnp.float32)
    gained = (state * gain[...]).astype(jnp.bfloat16)
    scale = lax.rsqrt(jnp.mean(state * state, axis=-1, keepdims=True) + epsilon)

    parts_ref[...] = jnp.zeros_like(parts_ref)
    left = router[...]
    for part in range(3):
        here = left.astype(jnp.bfloat16).astype(jnp.float32)
        parts_ref[8 * part : 8 * part + experts, :] = here
        left = left - here
    parts = parts_ref[...].astype(jnp.bfloat16)
    deep = parts.shape[1] // 4
    logits = sum(
        mm_t(gained[:, k * deep : (k + 1) * deep], parts[:, k * deep : (k + 1) * deep])
        for k in range(4)
    )
    logits = logits * scale
    expert_of_lane = iota((1, parts_ref.shape[0]), 1) & 7
    mine = jnp.sum(jnp.where(expert_of_lane == me, logits, 0.0), axis=1, keepdims=True)
    rival = jnp.sum(jnp.where(expert_of_lane == other, logits, 0.0), axis=1, keepdims=True)
    highest = jnp.maximum(mine, rival)
    raised = jnp.exp(mine - highest)
    gate = raised / (raised + jnp.exp(rival - highest))

    hidden_share = all_hidden.shape[1]
    chunk = 256 if hidden_share % 256 == 0 else hidden_share
    for at in range(0, hidden_share, chunk):
        opened = mm(gained, w_in[:, at : at + chunk]) * scale
        upper = mm(gained, w_in[:, hidden_share + at : hidden_share + at + chunk]) * scale
        all_hidden[:, at : at + chunk] = (opened / (1.0 + jnp.exp(-opened)) * upper).astype(
            jnp.bfloat16
        )
    first = kept * per
    hidden_ref[...] = all_hidden[:first, :]
    gate_ref[...] = gate[:first]
    term = (mm(all_hidden[first:, :], w_down[...]) * gate[first:]).astype(jnp.bfloat16)
    for g in range(kept):
        give_back(term[g * per : (g + 1) * per], later_spread[g], g, outs, order)


def share_kernel(order, hidden, gate, spread, w_down, *outs):
    groups, per, _ = spread.shape
    term = (mm(hidden[...], w_down[...]) * gate[...]).astype(jnp.bfloat16)
    for g in range(groups):
        give_back(term[g * per : (g + 1) * per], spread[g], g, outs, order)


def share_shapes(sources, patch_cap, wide):
    half = jax.ShapeDtypeStruct((sources, patch_cap, wide // 2), jnp.bfloat16)
    return (half, half)


def stream(own, moved, blocks, order, patch_cap, capacity, me, w_up, gain, router, w_in, w_down):
    held, width = own.shape[-2:]
    experts, wide = router.shape
    vmem = pl.BlockSpec(memory_space=pltpu.VMEM)
    per = GROUP * capacity
    slots = 2 * len(blocks) * per
    spread = jax.ShapeDtypeStruct((len(blocks), per, GROUP * patch_cap), jnp.bfloat16)
    return pl.pallas_call(
        functools.partial(stream_kernel, patch_cap, capacity, experts, blocks * 2, order),
        out_shape=share_shapes(len(blocks) * GROUP, patch_cap, wide)
        + (
            jax.ShapeDtypeStruct((slots // 2, w_down.shape[0]), jnp.bfloat16),
            jax.ShapeDtypeStruct((slots // 2, 1), jnp.float32),
            spread,
        ),
        in_specs=[pl.BlockSpec(memory_space=pltpu.SMEM)] + [vmem] * 7,
        out_specs=(vmem,) * 5,
        scratch_shapes=[
            pltpu.VMEM((slots, w_down.shape[0]), jnp.bfloat16),
            pltpu.VMEM(spread.shape, jnp.bfloat16),
            pltpu.VMEM((slots, width), jnp.bfloat16),
            pltpu.VMEM((24, wide), jnp.float32),
        ],
        cost_estimate=cost(slots * wide * (width + w_in.shape[1]) // 4),
        compiler_params=pltpu.CompilerParams(vmem_limit_bytes=24 * 1024 * 1024),
    )(me, own, moved, w_up, gain, router, w_in, w_down)


def gated_share(hidden, gate, spread, w_down, order, patch_cap):
    groups = spread.shape[0]
    wide = w_down.shape[1]
    vmem = pl.BlockSpec(memory_space=pltpu.VMEM)
    return pl.pallas_call(
        functools.partial(share_kernel, order),
        out_shape=share_shapes(groups * GROUP, patch_cap, wide),
        in_specs=[vmem] * 4,
        out_specs=(vmem,) * 2,
        cost_estimate=cost(1000),
        compiler_params=pltpu.CompilerParams(vmem_limit_bytes=16 * 1024 * 1024),
    )(hidden, gate, spread, w_down)


def prepare_kernel(encoded, payload, gain, w_dq, w_up, queries, state):
    queries[...] = mm(normed_rows(encoded[...], gain[...]), w_dq[...]).astype(jnp.bfloat16)
    state[...] = mm(payload[: state.shape[0], :], w_up[...]).astype(jnp.bfloat16)


def prepare(encoded, payload, patch_cap, gain, w_dq, w_up):
    vmem = pl.BlockSpec(memory_space=pltpu.VMEM)
    return pl.pallas_call(
        prepare_kernel,
        out_shape=(
            jax.ShapeDtypeStruct(encoded.shape, jnp.bfloat16),
            jax.ShapeDtypeStruct((patch_cap, w_up.shape[1]), jnp.bfloat16),
        ),
        in_specs=[vmem] * 5,
        out_specs=(vmem, vmem),
        cost_estimate=cost(2 * patch_cap * w_up.size),
        compiler_params=pltpu.CompilerParams(vmem_limit_bytes=8 * 1024 * 1024),
    )(encoded, payload, gain.reshape(1, -1), w_dq, w_up)


def decode_kernel(wholes, *refs):
    state, *parts = refs[:-8]
    encoded, queries, bias, w_dkv, w_do, bytes_out, patch_out, mixed_ref = refs[-8:]
    rows, width = encoded.shape
    wide = state.shape[1] // 2
    per = (len(parts) - wholes) // 2
    pairs = 0.0
    for half in range(2):
        here = slice(half * wide, (half + 1) * wide)
        total = state[:, here].astype(jnp.float32)
        for part in parts[wholes + half * per : wholes + (half + 1) * per]:
            total = total + part[0].astype(jnp.float32)
        for part in parts[:wholes]:
            total = total + part[:, here].astype(jnp.float32)
        states = total.astype(jnp.bfloat16)
        patch_out[:, here] = states
        pairs = pairs + mm(states, w_dkv[here, :])
    pairs = pairs.astype(jnp.bfloat16)
    lanes = 2 * HEAD
    for at in range(0, width, lanes):
        mixed = attend_pair(
            queries[:, at : at + lanes],
            pairs[:, at : at + lanes],
            pairs[:, width + at : width + at + lanes],
            bias[...],
        )
        mixed_ref[:, at : at + lanes] = mixed.astype(jnp.bfloat16)
    bytes_out[...] = (encoded[...].astype(jnp.float32) + mm(mixed_ref[...], w_do[...])).astype(
        jnp.bfloat16
    )


def decode(state, wholes, halves, encoded, queries, bias, w_dkv, w_do):
    vmem = pl.BlockSpec(memory_space=pltpu.VMEM)
    parts = [*wholes, *halves[0], *halves[1]]
    return pl.pallas_call(
        functools.partial(decode_kernel, len(wholes)),
        out_shape=(
            jax.ShapeDtypeStruct(encoded.shape, jnp.bfloat16),
            jax.ShapeDtypeStruct(state.shape, jnp.bfloat16),
        ),
        in_specs=[vmem] * (6 + len(parts)),
        out_specs=(vmem, vmem),
        scratch_shapes=[pltpu.VMEM(encoded.shape, jnp.bfloat16)],
        cost_estimate=cost(4 * 256 * w_dkv.size),
        compiler_params=pltpu.CompilerParams(vmem_limit_bytes=12 * 1024 * 1024),
    )(state, *parts, encoded, queries, bias, w_dkv, w_do)


def digits():
    seq, expert = lax.axis_size("seq"), lax.axis_size("expert")
    inner = 2 if seq % 2 == 0 else 1
    core = 2 if expert % 2 == 0 else 1
    return {
        "z": ("seq", inner, seq // inner),
        "x": ("seq", 1, inner),
        "y": ("expert", core, expert // core),
        "c": ("expert", 1, core),
    }


def shift(x, digit, by):
    axis, stride, radix = digit
    pairs = []
    for i in range(lax.axis_size(axis)):
        g = i // stride % radix
        pairs.append((i, i + ((g + by) % radix - g) * stride))
    return lax.ppermute(x, axis, pairs)


def gathered(x, digit, place=0):
    return jnp.stack([x] + [shift(x, digit, d) for d in range(1, digit[2])], axis=place)


def gather_chip(x, beside):
    d = digits()
    half = x.shape[1] // 2
    x = gathered(x, d["z"])
    x, beside = lax.optimization_barrier((x, beside))
    left = gathered(gathered(x[..., :half], d["x"], 1), d["y"], 1)
    right = gathered(gathered(x[..., half:], d["y"], 1), d["x"], 2)
    return jnp.concatenate([left, right], axis=-1), beside


def summed(parts):
    total = parts[0].astype(jnp.float32)
    for part in parts[1:]:
        total = total + part.astype(jnp.float32)
    return total


def earlier_blocks(x, reach, opened):
    both_axes = ("seq", "expert")
    experts = lax.axis_size("expert")
    if reach != 2 or experts % 2:
        earlier = [passed_along(x, both_axes, by) for by in range(reach, 0, -1)]
        return jnp.zeros((1,), jnp.int32), earlier, x
    own = lax.ppermute(x, "expert", [(i, i + 1) for i in range(0, experts, 2)])
    far = lax.optimization_barrier((passed_along(x, both_axes, 2), opened))[0]
    near = lax.ppermute(far, "expert", [(i + 1, i) for i in range(0, experts, 2)])
    odd = lax.axis_index("expert").astype(jnp.int32).reshape(1) & 1
    return odd, [far, near], own


def leg(x, digit, place):
    parts = [lax.index_in_dim(x, d, place, keepdims=False) for d in range(digit[2])]
    return [parts[0]] + [shift(parts[d], digit, -d) for d in range(1, digit[2])]


def narrow(v):
    return v.astype(jnp.bfloat16)


def behind(values, *others):
    return jax.tree.map(lambda v: lax.optimization_barrier((v, others))[0], values)


def ends(legs):
    return [narrow(summed(parts)) for parts in legs]


def mixture(payload, patch_cap, capacity, w_up, moe_gain, w_router, w_in, w_down):
    d = digits()
    wide = w_up.shape[1]
    paired = w_in.reshape(w_in.shape[1], -1)
    own, paired = gather_chip(payload, paired)
    far, ys, xs = own.shape[:3]
    own = own.reshape((-1,) + own.shape[3:])
    moved = [shift(own, d["c"], by) for by in range(1, d["c"][2])]
    assert len(moved) == 1 and ys * xs % GROUP == 0
    moved = moved[0]
    me = lax.axis_index("expert").astype(jnp.int32).reshape(1)
    weights = (w_up, moe_gain.reshape(1, wide), w_router.T, paired, w_down[0])
    w_last = w_down[0]

    if far == 4:
        streams = [[2], [1, 3], [0]]
    else:
        apart = [*range(1, far), 0]
        streams = [apart[at : at + 2] for at in range(0, far, 2)]

    def blocks_of(zs):
        return [z * ys * xs + at for z in zs for at in range(0, ys * xs, GROUP)]

    def order_of(zs):
        near = len(zs)
        left, right = [], []
        for z in range(near):
            for y in range(ys):
                for x in range(xs):
                    left.append((x * ys + y) * near + z)
                    right.append((y * xs + x) * near + z)
        return left, right

    def shaped(halves, zs):
        left, right = halves
        tail = (len(zs),) + left.shape[1:]
        return [left.reshape((xs, ys) + tail), right.reshape((ys, xs) + tail)]

    def begin(zs, moved):
        got = stream(own, moved, blocks_of(zs), order_of(zs), patch_cap, capacity, me, *weights)
        sent = [shift(v, d["c"], -1) for v in shaped(got[:2], zs)]
        return sent, got

    def finish(zs, sent, hidden, gate, spread):
        kept = gated_share(hidden, gate, spread, w_last, order_of(zs), patch_cap)
        return [narrow(summed(pair)) for pair in zip(shaped(kept, zs), sent)]

    def first_leg(sums):
        return [leg(sums[0], d["x"], 0), leg(sums[1], d["y"], 0)]

    def second_leg(sums):
        return [leg(sums[0], d["y"], 0), leg(sums[1], d["x"], 0)]

    wholes = []

    def last_leg(zs, sums):
        made = []
        for at, z in enumerate(zs):
            if z:
                made.append(jnp.concatenate([v[at] for v in sums], axis=-1))
                wholes.append(shift(made[-1], d["z"], -z))
        return made

    first, second, added = None, None, None
    for zs in streams:
        sent, got = begin(zs, moved if added is None else behind(moved, added))
        hidden, gate, spread = got[2:]
        if second:
            made = last_leg(second[0], ends(behind(second[1], gate)))
            gate, second = behind(gate, made), None
        if first:
            sums = ends(behind(first[1], gate))
            gate, first, second = behind(gate, sums), None, (first[0], second_leg(sums))
        added = finish(zs, sent, hidden, gate, spread)
        first = (zs, first_leg(added))
    zs, legs = first
    sums = ends(legs)
    legs = second_leg(sums)
    if second:
        made = last_leg(second[0], ends(behind(second[1], sums)))
        legs = behind(legs, made)
    if zs != [0]:
        sums = ends(legs)
        last_leg(zs, sums)
        at = zs.index(0)
        legs = [[v[at : at + 1]] for v in sums]
    return wholes, legs


def per_device(
    byte_states,
    patch_start,
    expert_ids,
    enc_gain,
    w_qkv,
    w_out,
    w_xq,
    w_xkv,
    w_up,
    moe_gain,
    w_router,
    w_in,
    w_down,
    dec_gain,
    w_dq,
    w_dkv,
    w_do,
):
    byte_dev = byte_states.shape[0]
    patch_cap = expert_ids.shape[0]
    experts = w_router.shape[1]
    capacity = 12 * patch_cap // (5 * experts)
    both_axes = ("seq", "expert")
    reach = -(-WINDOW // byte_dev)
    place = lax.axis_index(both_axes).astype(jnp.int32).reshape(1)
    opened = opening(
        byte_states,
        patch_start,
        expert_ids,
        reach,
        capacity,
        place,
        enc_gain,
        w_qkv,
        w_out,
        w_xq,
        w_xkv,
    )
    instead, earlier, nearest = earlier_blocks(byte_states, reach, opened)
    encoded, payload = encode(instead, earlier, nearest, opened)
    wholes, halves = mixture(payload, patch_cap, capacity, w_up, moe_gain, w_router, w_in, w_down)
    queries, state = prepare(encoded, payload, patch_cap, dec_gain, w_dq, w_up)
    return decode(state, wholes, halves, encoded, queries, opened[13], w_dkv, w_do)


def solution(mesh):
    in_specs = (
        P(("seq", "expert"), None),
        P(("seq", "expert")),
        P(("seq", "expert"), None),
        P(),
        P(),
        P(),
        P(),
        P(),
        P(),
        P(),
        P(),
        P("expert", None, None, "seq"),
        P("expert", "seq", None),
        P(),
        P(),
        P(),
        P(),
    )
    out_specs = (P(("seq", "expert"), None), P(("seq", "expert"), None))
    return jax.shard_map(
        per_device, mesh=mesh, in_specs=in_specs, out_specs=out_specs, check_vma=False
    )
```

```python
import functools
import math

import jax
import jax.numpy as jnp
from jax import lax
from jax.experimental import pallas as pl
from jax.experimental.pallas import tpu as pltpu
from jax.sharding import PartitionSpec as P

HEADS_L = 8
HEAD = 64
WINDOW = 512


epsilon = 1e-06
very_negative = -1e30


def passed_along(x, axis, by):
    length = lax.axis_size(axis)
    pairs = [(i, i + by) for i in range(length) if 0 <= i + by < length]
    return lax.ppermute(x, axis, pairs)


def normed_rows(x, gain_row):
    wide = x.astype(jnp.float32)
    scale = lax.rsqrt(jnp.mean(wide * wide, axis=-1, keepdims=True) + epsilon)
    return (wide * scale * gain_row).astype(jnp.bfloat16)


def cost(flops):
    return pl.CostEstimate(flops=int(flops), transcendentals=0, bytes_accessed=0)


def mm(a, b):
    return jnp.dot(a, b, preferred_element_type=jnp.float32)


def mm_t(a, b):
    return lax.dot_general(a, b, (((1,), (1,)), ((), ())), preferred_element_type=jnp.float32)


def as_bf16(mask):
    return mask.astype(jnp.float32).astype(jnp.bfloat16)


def iota(shape, dim):
    return lax.broadcasted_iota(jnp.int32, shape, dim)


def attend_pair(q, k, v, bias):
    first = iota((1, 2 * HEAD), 1) < HEAD
    q = q * jnp.asarray(1.0 / math.sqrt(HEAD), q.dtype)
    outs = []
    for here in (first, jnp.logical_not(first)):
        scores = mm_t(jnp.where(here, q, jnp.zeros_like(q)), k) + bias
        raised = jnp.exp(scores - jnp.max(scores, axis=-1, keepdims=True)).astype(jnp.bfloat16)
        both = mm(raised, jnp.where(here, v, jnp.ones_like(v)))
        outs.append(both / pltpu.roll(both, HEAD, 1))
    return jnp.where(first, outs[0], outs[1])


def opening_kernel(reach, capacity, *refs):
    place, own_in, flags_in, ids_in, gain_in, w_qkv_in, w_out_in, w_xq_in, w_xkv_in = refs[:9]
    outs, (flags, ids, w_qkv, sem) = refs[9:-4], refs[-4:]
    own, gain, w_kv, w_out, w_xq, w_xkv, projected_out = outs[:7]
    bias_out, since_out, ends_out, member_out, live_out, table_out, decode_out = outs[7:]
    pairs = [
        (own_in, own),
        (gain_in, gain),
        (w_qkv_in, w_qkv),
        (flags_in, flags),
        (ids_in, ids),
        (w_out_in, w_out),
        (w_xq_in, w_xq),
        (w_xkv_in, w_xkv),
    ]
    copies = [pltpu.make_async_copy(a, b, sem.at[k]) for k, (a, b) in enumerate(pairs)]
    for copy in copies:
        copy.start()
    rows, width = own.shape
    patch_cap = rows * 5 // 32
    keys = (reach + 1) * rows
    at_query = iota((rows, keys), 0) + reach * rows
    at_key = iota((rows, keys), 1)
    allowed = (at_key <= at_query) & (at_key > at_query - WINDOW)
    allowed = allowed & (at_key >= (reach - place[0]) * rows)
    bias_out[...] = jnp.where(allowed, 0.0, very_negative)
    for copy in copies[:3]:
        copy.wait()
    normed = normed_rows(own[...], gain[...])
    projected_out[...] = mm(normed, w_qkv[...]).astype(jnp.bfloat16)
    w_kv[...] = w_qkv[:, width:]
    copies[3].wait()
    flag = flags[...]
    at_row, at_col = iota((rows, rows), 0), iota((rows, rows), 1)
    upto = at_col <= at_row
    opened = jnp.max(jnp.where(upto & (flag == 1), at_col, 0), axis=1, keepdims=True)
    since_out[...] = iota((rows, 1), 0) - opened
    own_number = jnp.sum(jnp.where(upto, flag, 0), axis=1, keepdims=True) - 1
    decode_out[...] = jnp.where(iota((rows, patch_cap), 1) <= own_number, 0.0, very_negative)
    eight = jnp.broadcast_to(flag, (8, rows)).astype(jnp.float32).astype(jnp.bfloat16)
    number = mm(eight, as_bf16(at_row <= at_col))[:1].astype(jnp.int32) - 1
    at_byte = iota((patch_cap, rows), 1)
    member = number == iota((patch_cap, rows), 0)
    last = jnp.max(jnp.where(member, at_byte, -1), axis=1, keepdims=True)
    live_out[...] = (last >= 0).astype(jnp.float32)
    ends_out[...] = as_bf16(member & (at_byte == last))
    member_out[...] = jnp.where(member, 0.0, very_negative)

    copies[4].wait()
    square = (patch_cap, patch_cap)
    same = iota(square, 0) == iota(square, 1)
    earlier_slot = iota(square, 0) < iota(square, 1)
    id_rows = [ids[k : k + 1, :] for k in range(2)]
    id_cols = [jnp.sum(jnp.where(same, row, 0), axis=1, keepdims=True) for row in id_rows]
    targets = []
    for row in id_rows:
        named = sum((col == row).astype(jnp.int32) for col in id_cols)
        rank = jnp.sum(jnp.where(earlier_slot, named, 0), axis=0, keepdims=True)
        targets.append(row * capacity + rank)
    extra = table_out.shape[0]
    at_extra = iota((extra, patch_cap), 0)
    table = jnp.where(at_extra == 0, targets[0], jnp.where(at_extra == 1, targets[1], 0))
    table_out[...] = jnp.zeros_like(table_out)
    table_out[:, :patch_cap] = table.astype(jnp.float32).astype(jnp.bfloat16)
    for copy in copies[5:]:
        copy.wait()


def opening(byte_states, patch_start, expert_ids, reach, capacity, place, enc_gain, *ws):
    rows, width = byte_states.shape
    w_qkv, w_out, w_xq, w_xkv = ws
    patch_cap = expert_ids.shape[0]
    extra = -(-(patch_cap + 2) // 16) * 16 - patch_cap
    keys = (reach + 1) * rows
    vmem, anywhere = pl.BlockSpec(memory_space=pltpu.VMEM), pl.BlockSpec(memory_space=pltpu.HBM)
    like = jax.ShapeDtypeStruct
    bf16, f32 = jnp.bfloat16, jnp.float32
    return pl.pallas_call(
        functools.partial(opening_kernel, reach, capacity),
        out_shape=(
            like((rows, width), bf16),
            like((1, width), f32),
            like((width, 2 * width), bf16),
            like(w_out.shape, bf16),
            like(w_xq.shape, bf16),
            like(w_xkv.shape, bf16),
            like((rows, 3 * width), bf16),
            like((rows, keys), f32),
            like((rows, 1), jnp.int32),
            like((patch_cap, rows), bf16),
            like((patch_cap, rows), f32),
            like((patch_cap, 1), f32),
            like((extra, width), bf16),
            like((rows, patch_cap), f32),
        ),
        in_specs=[pl.BlockSpec(memory_space=pltpu.SMEM)] + [anywhere] * 8,
        out_specs=(vmem,) * 14,
        scratch_shapes=[
            pltpu.VMEM((1, rows), jnp.int32),
            pltpu.VMEM((2, patch_cap), jnp.int32),
            pltpu.VMEM(w_qkv.shape, bf16),
            pltpu.SemaphoreType.DMA((8,)),
        ],
        cost_estimate=cost(4 * rows * width * 3 * width),
        compiler_params=pltpu.CompilerParams(vmem_limit_bytes=16 * 1024 * 1024),
    )(
        place,
        *[
            pltpu.with_memory_space_constraint(v, pltpu.HBM)
            for v in (
                byte_states,
                patch_start.reshape(1, rows),
                expert_ids.T,
                enc_gain.reshape(1, width),
                *ws,
            )
        ],
    )


def encoder_kernel(reach, *refs):
    instead, earlier, nearest, refs = refs[0], refs[1 : 1 + reach], refs[1 + reach], refs[2 + reach :]
    own, gain, w_kv, w_out, w_xq, w_xkv, projected = refs[:7]
    bias, since, ends, member_bias, live, table = refs[7:13]
    encoded_out, payload_out, pairs_ref, mixed_ref = refs[13:]
    rows, width = own.shape
    patch_cap = ends.shape[0]
    pairs_ref[reach * rows :, :] = projected[:, width:]
    for at, block in enumerate(earlier):
        moved = block[...]
        if at == reach - 1:
            moved = jnp.where(instead[0] == 1, nearest[...], moved)
        moved = normed_rows(moved, gain[...])
        pairs_ref[at * rows : (at + 1) * rows, :] = mm(moved, w_kv[...]).astype(jnp.bfloat16)
    lanes = 2 * HEAD
    for at in range(0, width, lanes):
        mixed = attend_pair(
            projected[:, at : at + lanes],
            pairs_ref[:, at : at + lanes],
            pairs_ref[:, width + at : width + at + lanes],
            bias[...],
        )
        mixed_ref[:, at : at + lanes] = mixed.astype(jnp.bfloat16)
    encoded = (own[...].astype(jnp.float32) + mm(mixed_ref[...], w_out[...])).astype(jnp.bfloat16)
    encoded_out[...] = encoded

    inside = since[...]
    highest = encoded.astype(jnp.float32)
    step = 1
    while step < rows:
        highest = jnp.where(
            inside >= step, jnp.maximum(highest, pltpu.roll(highest, step, 0)), highest
        )
        step *= 2
    pooled = mm(ends[...], highest.astype(jnp.bfloat16))
    patch_queries = mm(pooled.astype(jnp.bfloat16), w_xq[...]).astype(jnp.bfloat16)
    byte_pairs = mm(encoded, w_xkv[...]).astype(jnp.bfloat16)
    alive = live[...] > 0.0
    for at in range(0, width, lanes):
        mixed = attend_pair(
            patch_queries[:, at : at + lanes],
            byte_pairs[:, at : at + lanes],
            byte_pairs[:, width + at : width + at + lanes],
            member_bias[...],
        )
        total = jnp.where(alive, pooled[:, at : at + lanes] + mixed, 0.0)
        payload_out[:patch_cap, at : at + lanes] = total.astype(jnp.bfloat16)
    payload_out[patch_cap:, :] = table[...]


def encode(instead, earlier, nearest, opened):
    rows, width = opened[0].shape
    reach = len(earlier)
    vmem = pl.BlockSpec(memory_space=pltpu.VMEM)
    payload_rows = opened[9].shape[0] + opened[12].shape[0]
    return pl.pallas_call(
        functools.partial(encoder_kernel, reach),
        out_shape=(
            jax.ShapeDtypeStruct((rows, width), jnp.bfloat16),
            jax.ShapeDtypeStruct((payload_rows, width), jnp.bfloat16),
        ),
        in_specs=[pl.BlockSpec(memory_space=pltpu.SMEM)] + [vmem] * (14 + reach),
        out_specs=(vmem, vmem),
        scratch_shapes=[
            pltpu.VMEM(((reach + 1) * rows, 2 * width), jnp.bfloat16),
            pltpu.VMEM((rows, width), jnp.bfloat16),
        ],
        cost_estimate=cost(24 * rows * width * (reach + 1) * rows),
        compiler_params=pltpu.CompilerParams(vmem_limit_bytes=16 * 1024 * 1024),
    )(instead, *earlier, nearest, *opened[:13])


def mm_first(a, b):
    return lax.dot_general(a, b, (((0,), (0,)), ((), ())), preferred_element_type=jnp.float32)


def counted_from(values, step, most):
    return sum((values >= step * k).astype(jnp.int32) for k in range(1, most))


GROUP = 4


def give_back(term, spread, group, halves, order):
    for half, (out, places) in enumerate(zip(halves, order)):
        width = out.shape[-1]
        total = mm_first(spread, term[:, half * width : (half + 1) * width]).astype(jnp.bfloat16)
        block = out.shape[-2]
        for s in range(GROUP):
            out[places[group * GROUP + s]] = total[s * block : (s + 1) * block]


def stream_kernel(patch_cap, capacity, experts, blocks, order, *refs):
    me_ref, own_ref, moved_ref, w_up, gain, router, w_in, w_down = refs[:8]
    outs = refs[8:10]
    hidden_ref, gate_ref, spread_ref, all_hidden, later_spread, routed_ref, parts_ref = refs[10:]
    held, width = own_ref.shape[-2:]
    per = GROUP * capacity
    kept = len(blocks) // 2
    me = me_ref[0]
    slots = iota((per, 1), 0)
    source_of_slot = counted_from(slots, capacity, GROUP)
    place_of_slot = slots - source_of_slot * capacity + me * capacity
    lanes = 128

    def spreader(block):
        at_from, at_to = iota((GROUP * lanes, GROUP * block), 0), iota((GROUP * lanes, GROUP * block), 1)
        source = counted_from(at_from, lanes, GROUP)
        within = at_from - source * lanes
        return as_bf16((at_to == source * block + within) & (within < block))

    spread_held, spread_cap = spreader(held), spreader(patch_cap)

    def matched(table, spread, block):
        targets = mm(table, spread).astype(jnp.int32)
        at = iota((1, GROUP * block), 1)
        source = counted_from(at, block, GROUP)
        first, second = targets[0:1], targets[1:2]
        hit = (first == place_of_slot) | (second == place_of_slot)
        hit = hit & (source == source_of_slot) & (at - source * block < patch_cap)
        named = [counted_from(t, capacity, experts) for t in (first, second)]
        return hit, jnp.where(named[0] == me, named[1], named[0])

    others = []
    for g, begin in enumerate(blocks):
        rows_ref = own_ref if g < kept else moved_ref
        tables = []
        for s in range(begin, begin + GROUP):
            block = rows_ref[s, held - 16 : held, :lanes].astype(jnp.float32)
            tables.append(block[patch_cap - (held - 16) : patch_cap - (held - 16) + 8])
        table = jnp.concatenate(tables, axis=1).astype(jnp.bfloat16)
        hit, other = matched(table, spread_held, held)
        others.append(jnp.sum(jnp.where(hit, other, 0), axis=1, keepdims=True))
        block = rows_ref[begin : begin + GROUP].reshape(GROUP * held, width)
        routed_ref[g * per : (g + 1) * per, :] = mm(as_bf16(hit), block).astype(jnp.bfloat16)
        hit, _ = matched(table, spread_cap, patch_cap)
        if g < kept:
            spread_ref[g] = as_bf16(hit)
        else:
            later_spread[g - kept] = as_bf16(hit)
    other = jnp.concatenate(others, axis=0)

    state = mm(routed_ref[...], w_up[...]).astype(jnp.bfloat16).astype(jnp.float32)
    gained = (state * gain[...]).astype(jnp.bfloat16)
    scale = lax.rsqrt(jnp.mean(state * state, axis=-1, keepdims=True) + epsilon)

    parts_ref[...] = jnp.zeros_like(parts_ref)
    left = router[...]
    for part in range(3):
        here = left.astype(jnp.bfloat16).astype(jnp.float32)
        parts_ref[8 * part : 8 * part + experts, :] = here
        left = left - here
    parts = parts_ref[...].astype(jnp.bfloat16)
    deep = parts.shape[1] // 4
    logits = sum(
        mm_t(gained[:, k * deep : (k + 1) * deep], parts[:, k * deep : (k + 1) * deep])
        for k in range(4)
    )
    logits = logits * scale
    expert_of_lane = iota((1, parts_ref.shape[0]), 1) & 7
    mine = jnp.sum(jnp.where(expert_of_lane == me, logits, 0.0), axis=1, keepdims=True)
    rival = jnp.sum(jnp.where(expert_of_lane == other, logits, 0.0), axis=1, keepdims=True)
    highest = jnp.maximum(mine, rival)
    raised = jnp.exp(mine - highest)
    gate = raised / (raised + jnp.exp(rival - highest))

    hidden_share = all_hidden.shape[1]
    chunk = 256 if hidden_share % 256 == 0 else hidden_share
    for at in range(0, hidden_share, chunk):
        opened = mm(gained, w_in[:, at : at + chunk]) * scale
        upper = mm(gained, w_in[:, hidden_share + at : hidden_share + at + chunk]) * scale
        all_hidden[:, at : at + chunk] = (opened / (1.0 + jnp.exp(-opened)) * upper).astype(
            jnp.bfloat16
        )
    first = kept * per
    hidden_ref[...] = all_hidden[:first, :]
    gate_ref[...] = gate[:first]
    term = (mm(all_hidden[first:, :], w_down[...]) * gate[first:]).astype(jnp.bfloat16)
    for g in range(kept):
        give_back(term[g * per : (g + 1) * per], later_spread[g], g, outs, order)


def share_kernel(order, hidden, gate, spread, w_down, *outs):
    groups, per, _ = spread.shape
    term = (mm(hidden[...], w_down[...]) * gate[...]).astype(jnp.bfloat16)
    for g in range(groups):
        give_back(term[g * per : (g + 1) * per], spread[g], g, outs, order)


def share_shapes(sources, patch_cap, wide):
    half = jax.ShapeDtypeStruct((sources, patch_cap, wide // 2), jnp.bfloat16)
    return (half, half)


def stream(own, moved, blocks, order, patch_cap, capacity, me, w_up, gain, router, w_in, w_down):
    held, width = own.shape[-2:]
    experts, wide = router.shape
    vmem = pl.BlockSpec(memory_space=pltpu.VMEM)
    per = GROUP * capacity
    slots = 2 * len(blocks) * per
    spread = jax.ShapeDtypeStruct((len(blocks), per, GROUP * patch_cap), jnp.bfloat16)
    return pl.pallas_call(
        functools.partial(stream_kernel, patch_cap, capacity, experts, blocks * 2, order),
        out_shape=share_shapes(len(blocks) * GROUP, patch_cap, wide)
        + (
            jax.ShapeDtypeStruct((slots // 2, w_down.shape[0]), jnp.bfloat16),
            jax.ShapeDtypeStruct((slots // 2, 1), jnp.float32),
            spread,
        ),
        in_specs=[pl.BlockSpec(memory_space=pltpu.SMEM)] + [vmem] * 7,
        out_specs=(vmem,) * 5,
        scratch_shapes=[
            pltpu.VMEM((slots, w_down.shape[0]), jnp.bfloat16),
            pltpu.VMEM(spread.shape, jnp.bfloat16),
            pltpu.VMEM((slots, width), jnp.bfloat16),
            pltpu.VMEM((24, wide), jnp.float32),
        ],
        cost_estimate=cost(slots * wide * (width + w_in.shape[1]) // 4),
        compiler_params=pltpu.CompilerParams(vmem_limit_bytes=24 * 1024 * 1024),
    )(me, own, moved, w_up, gain, router, w_in, w_down)


def gated_share(hidden, gate, spread, w_down, order, patch_cap):
    groups = spread.shape[0]
    wide = w_down.shape[1]
    vmem = pl.BlockSpec(memory_space=pltpu.VMEM)
    return pl.pallas_call(
        functools.partial(share_kernel, order),
        out_shape=share_shapes(groups * GROUP, patch_cap, wide),
        in_specs=[vmem] * 4,
        out_specs=(vmem,) * 2,
        cost_estimate=cost(1000),
        compiler_params=pltpu.CompilerParams(vmem_limit_bytes=16 * 1024 * 1024),
    )(hidden, gate, spread, w_down)


def prepare_kernel(encoded, payload, gain, w_dq, w_up, queries, state):
    queries[...] = mm(normed_rows(encoded[...], gain[...]), w_dq[...]).astype(jnp.bfloat16)
    state[...] = mm(payload[: state.shape[0], :], w_up[...]).astype(jnp.bfloat16)


def prepare(encoded, payload, patch_cap, gain, w_dq, w_up):
    vmem = pl.BlockSpec(memory_space=pltpu.VMEM)
    return pl.pallas_call(
        prepare_kernel,
        out_shape=(
            jax.ShapeDtypeStruct(encoded.shape, jnp.bfloat16),
            jax.ShapeDtypeStruct((patch_cap, w_up.shape[1]), jnp.bfloat16),
        ),
        in_specs=[vmem] * 5,
        out_specs=(vmem, vmem),
        cost_estimate=cost(2 * patch_cap * w_up.size),
        compiler_params=pltpu.CompilerParams(vmem_limit_bytes=8 * 1024 * 1024),
    )(encoded, payload, gain.reshape(1, -1), w_dq, w_up)


def decode_kernel(wholes, *refs):
    state, *parts = refs[:-8]
    encoded, queries, bias, w_dkv, w_do, bytes_out, patch_out, mixed_ref = refs[-8:]
    rows, width = encoded.shape
    wide = state.shape[1] // 2
    per = (len(parts) - wholes) // 2
    pairs = 0.0
    for half in range(2):
        here = slice(half * wide, (half + 1) * wide)
        total = state[:, here].astype(jnp.float32)
        for part in parts[wholes + half * per : wholes + (half + 1) * per]:
            total = total + part[0].astype(jnp.float32)
        for part in parts[:wholes]:
            total = total + part[:, here].astype(jnp.float32)
        states = total.astype(jnp.bfloat16)
        patch_out[:, here] = states
        pairs = pairs + mm(states, w_dkv[here, :])
    pairs = pairs.astype(jnp.bfloat16)
    lanes = 2 * HEAD
    for at in range(0, width, lanes):
        mixed = attend_pair(
            queries[:, at : at + lanes],
            pairs[:, at : at + lanes],
            pairs[:, width + at : width + at + lanes],
            bias[...],
        )
        mixed_ref[:, at : at + lanes] = mixed.astype(jnp.bfloat16)
    bytes_out[...] = (encoded[...].astype(jnp.float32) + mm(mixed_ref[...], w_do[...])).astype(
        jnp.bfloat16
    )


def decode(state, wholes, halves, encoded, queries, bias, w_dkv, w_do):
    vmem = pl.BlockSpec(memory_space=pltpu.VMEM)
    parts = [*wholes, *halves[0], *halves[1]]
    return pl.pallas_call(
        functools.partial(decode_kernel, len(wholes)),
        out_shape=(
            jax.ShapeDtypeStruct(encoded.shape, jnp.bfloat16),
            jax.ShapeDtypeStruct(state.shape, jnp.bfloat16),
        ),
        in_specs=[vmem] * (6 + len(parts)),
        out_specs=(vmem, vmem),
        scratch_shapes=[pltpu.VMEM(encoded.shape, jnp.bfloat16)],
        cost_estimate=cost(4 * 256 * w_dkv.size),
        compiler_params=pltpu.CompilerParams(vmem_limit_bytes=12 * 1024 * 1024),
    )(state, *parts, encoded, queries, bias, w_dkv, w_do)


def digits():
    seq, expert = lax.axis_size("seq"), lax.axis_size("expert")
    inner = 2 if seq % 2 == 0 else 1
    core = 2 if expert % 2 == 0 else 1
    return {
        "z": ("seq", inner, seq // inner),
        "x": ("seq", 1, inner),
        "y": ("expert", core, expert // core),
        "c": ("expert", 1, core),
    }


def shift(x, digit, by):
    axis, stride, radix = digit
    pairs = []
    for i in range(lax.axis_size(axis)):
        g = i // stride % radix
        pairs.append((i, i + ((g + by) % radix - g) * stride))
    return lax.ppermute(x, axis, pairs)


def gathered(x, digit, place=0):
    return jnp.stack([x] + [shift(x, digit, d) for d in range(1, digit[2])], axis=place)


def gather_chip(x, beside):
    d = digits()
    half = x.shape[1] // 2
    x = gathered(x, d["z"])
    x, beside = lax.optimization_barrier((x, beside))
    left = gathered(gathered(x[..., :half], d["x"], 1), d["y"], 1)
    right = gathered(gathered(x[..., half:], d["y"], 1), d["x"], 2)
    return jnp.concatenate([left, right], axis=-1), beside


def summed(parts):
    total = parts[0].astype(jnp.float32)
    for part in parts[1:]:
        total = total + part.astype(jnp.float32)
    return total


def earlier_blocks(x, reach, opened):
    both_axes = ("seq", "expert")
    experts = lax.axis_size("expert")
    if reach != 2 or experts % 2:
        earlier = [passed_along(x, both_axes, by) for by in range(reach, 0, -1)]
        return jnp.zeros((1,), jnp.int32), earlier, x
    own = lax.ppermute(x, "expert", [(i, i + 1) for i in range(0, experts, 2)])
    far = lax.optimization_barrier((passed_along(x, both_axes, 2), opened))[0]
    near = lax.ppermute(far, "expert", [(i + 1, i) for i in range(0, experts, 2)])
    odd = lax.axis_index("expert").astype(jnp.int32).reshape(1) & 1
    return odd, [far, near], own


def leg(x, digit, place):
    parts = [lax.index_in_dim(x, d, place, keepdims=False) for d in range(digit[2])]
    return [parts[0]] + [shift(parts[d], digit, -d) for d in range(1, digit[2])]


def narrow(v):
    return v.astype(jnp.bfloat16)


def behind(values, *others):
    return jax.tree.map(lambda v: lax.optimization_barrier((v, others))[0], values)


def ends(legs):
    return [narrow(summed(parts)) for parts in legs]


def mixture(payload, patch_cap, capacity, w_up, moe_gain, w_router, w_in, w_down):
    d = digits()
    wide = w_up.shape[1]
    paired = w_in.reshape(w_in.shape[1], -1)
    own, paired = gather_chip(payload, paired)
    far, ys, xs = own.shape[:3]
    own = own.reshape((-1,) + own.shape[3:])
    moved = [shift(own, d["c"], by) for by in range(1, d["c"][2])]
    assert len(moved) == 1 and ys * xs % GROUP == 0
    moved = moved[0]
    me = lax.axis_index("expert").astype(jnp.int32).reshape(1)
    weights = (w_up, moe_gain.reshape(1, wide), w_router.T, paired, w_down[0])
    w_last = w_down[0]

    if far == 4:
        streams = [[2], [1, 3], [0]]
    else:
        apart = [*range(1, far), 0]
        streams = [apart[at : at + 2] for at in range(0, far, 2)]

    def blocks_of(zs):
        return [z * ys * xs + at for z in zs for at in range(0, ys * xs, GROUP)]

    def order_of(zs):
        near = len(zs)
        left, right = [], []
        for z in range(near):
            for y in range(ys):
                for x in range(xs):
                    left.append((x * ys + y) * near + z)
                    right.append((y * xs + x) * near + z)
        return left, right

    def shaped(halves, zs):
        left, right = halves
        tail = (len(zs),) + left.shape[1:]
        return [left.reshape((xs, ys) + tail), right.reshape((ys, xs) + tail)]

    def begin(zs, moved):
        got = stream(own, moved, blocks_of(zs), order_of(zs), patch_cap, capacity, me, *weights)
        sent = [shift(v, d["c"], -1) for v in shaped(got[:2], zs)]
        return sent, got

    def finish(zs, sent, hidden, gate, spread):
        kept = gated_share(hidden, gate, spread, w_last, order_of(zs), patch_cap)
        return [narrow(summed(pair)) for pair in zip(shaped(kept, zs), sent)]

    def first_leg(sums):
        return [leg(sums[0], d["x"], 0), leg(sums[1], d["y"], 0)]

    def second_leg(sums):
        return [leg(sums[0], d["y"], 0), leg(sums[1], d["x"], 0)]

    wholes = []

    def last_leg(zs, sums):
        made = []
        for at, z in enumerate(zs):
            if z:
                made.append(jnp.concatenate([v[at] for v in sums], axis=-1))
                wholes.append(shift(made[-1], d["z"], -z))
        return made

    first, second, added = None, None, None
    for zs in streams:
        sent, got = begin(zs, moved if added is None else behind(moved, added))
        hidden, gate, spread = got[2:]
        if second:
            made = last_leg(second[0], ends(behind(second[1], gate)))
            gate, second = behind(gate, made), None
        if first:
            sums = ends(behind(first[1], gate))
            gate, first, second = behind(gate, sums), None, (first[0], second_leg(sums))
        added = finish(zs, sent, hidden, gate, spread)
        first = (zs, first_leg(added))
    zs, legs = first
    if second:
        made = last_leg(second[0], ends(second[1]))
        legs = behind(legs, made)
    sums = ends(legs)
    legs = second_leg(sums)
    if zs != [0]:
        sums = ends(legs)
        last_leg(zs, sums)
        at = zs.index(0)
        legs = [[v[at : at + 1]] for v in sums]
    return wholes, legs


def per_device(
    byte_states,
    patch_start,
    expert_ids,
    enc_gain,
    w_qkv,
    w_out,
    w_xq,
    w_xkv,
    w_up,
    moe_gain,
    w_router,
    w_in,
    w_down,
    dec_gain,
    w_dq,
    w_dkv,
    w_do,
):
    byte_dev = byte_states.shape[0]
    patch_cap = expert_ids.shape[0]
    experts = w_router.shape[1]
    capacity = 12 * patch_cap // (5 * experts)
    both_axes = ("seq", "expert")
    reach = -(-WINDOW // byte_dev)
    place = lax.axis_index(both_axes).astype(jnp.int32).reshape(1)
    opened = opening(
        byte_states,
        patch_start,
        expert_ids,
        reach,
        capacity,
        place,
        enc_gain,
        w_qkv,
        w_out,
        w_xq,
        w_xkv,
    )
    instead, earlier, nearest = earlier_blocks(byte_states, reach, opened)
    encoded, payload = encode(instead, earlier, nearest, opened)
    wholes, halves = mixture(payload, patch_cap, capacity, w_up, moe_gain, w_router, w_in, w_down)
    queries, state = prepare(encoded, payload, patch_cap, dec_gain, w_dq, w_up)
    return decode(state, wholes, halves, encoded, queries, opened[13], w_dkv, w_do)


def solution(mesh):
    in_specs = (
        P(("seq", "expert"), None),
        P(("seq", "expert")),
        P(("seq", "expert"), None),
        P(),
        P(),
        P(),
        P(),
        P(),
        P(),
        P(),
        P(),
        P("expert", None, None, "seq"),
        P("expert", "seq", None),
        P(),
        P(),
        P(),
        P(),
    )
    out_specs = (P(("seq", "expert"), None), P(("seq", "expert"), None))
    return jax.shard_map(
        per_device, mesh=mesh, in_specs=in_specs, out_specs=out_specs, check_vma=False
    )
```

```python
import functools
import math

import jax
import jax.numpy as jnp
from jax import lax
from jax.experimental import pallas as pl
from jax.experimental.pallas import tpu as pltpu
from jax.sharding import PartitionSpec as P

HEADS_L = 8
HEAD = 64
WINDOW = 512


epsilon = 1e-06
very_negative = -1e30


def passed_along(x, axis, by):
    length = lax.axis_size(axis)
    pairs = [(i, i + by) for i in range(length) if 0 <= i + by < length]
    return lax.ppermute(x, axis, pairs)


def normed_rows(x, gain_row):
    wide = x.astype(jnp.float32)
    scale = lax.rsqrt(jnp.mean(wide * wide, axis=-1, keepdims=True) + epsilon)
    return (wide * scale * gain_row).astype(jnp.bfloat16)


def cost(flops):
    return pl.CostEstimate(flops=int(flops), transcendentals=0, bytes_accessed=0)


def mm(a, b):
    return jnp.dot(a, b, preferred_element_type=jnp.float32)


def mm_t(a, b):
    return lax.dot_general(a, b, (((1,), (1,)), ((), ())), preferred_element_type=jnp.float32)


def as_bf16(mask):
    return mask.astype(jnp.float32).astype(jnp.bfloat16)


def iota(shape, dim):
    return lax.broadcasted_iota(jnp.int32, shape, dim)


def attend_part(q, k, v, bias):
    first = iota((1, 2 * HEAD), 1) < HEAD
    q = q * jnp.asarray(1.0 / math.sqrt(HEAD), q.dtype)
    parts = []
    for here in (first, jnp.logical_not(first)):
        scores = mm_t(jnp.where(here, q, jnp.zeros_like(q)), k) + bias
        highest = jnp.max(scores, axis=-1, keepdims=True)
        raised = jnp.exp(scores - highest).astype(jnp.bfloat16)
        parts.append((highest, mm(raised, jnp.where(here, v, jnp.ones_like(v)))))
    return parts


def divided(sums):
    first = iota((1, 2 * HEAD), 1) < HEAD
    outs = [both / pltpu.roll(both, HEAD, 1) for both in sums]
    return jnp.where(first, outs[0], outs[1])


def attend_pair(q, k, v, bias):
    return divided([both for _, both in attend_part(q, k, v, bias)])


def attend_stacked(q, k, v, bias):
    rows, width = q.shape
    lane = iota((1, width), 1)
    heads = [(lane >= at) & (lane < at + HEAD) for at in range(0, width, HEAD)]
    scaled = q.astype(jnp.float32) * (1.0 / math.sqrt(HEAD))
    stack = jnp.concatenate([jnp.where(here, scaled, 0.0) for here in heads], axis=0)
    scores = mm_t(stack.astype(jnp.bfloat16), k) + jnp.concatenate([bias] * len(heads), axis=0)
    raised = jnp.exp(scores - jnp.max(scores, axis=-1, keepdims=True))
    mixed = mm(raised.astype(jnp.bfloat16), v) / jnp.sum(raised, axis=-1, keepdims=True)
    out = jnp.zeros((rows, width), jnp.float32)
    for number, here in enumerate(heads):
        out = jnp.where(here, mixed[number * rows : (number + 1) * rows], out)
    return out


def opening_kernel(reach, capacity, *refs):
    place, own_in, flags_in, ids_in, gain_in, w_qkv_in, w_out_in, w_xq_in, w_xkv_in = refs[:9]
    outs, (flags, ids, w_qkv, sem) = refs[9:-4], refs[-4:]
    own, gain, w_kv, w_out, w_xq, w_xkv, queries_out = outs[:7]
    bias_out, since_out, ends_out, member_out, live_out, table_out = outs[7:13]
    highest_out, sums_out, decode_out = outs[13:]
    pairs = [
        (own_in, own),
        (gain_in, gain),
        (w_qkv_in, w_qkv),
        (flags_in, flags),
        (ids_in, ids),
        (w_out_in, w_out),
        (w_xq_in, w_xq),
        (w_xkv_in, w_xkv),
    ]
    copies = [pltpu.make_async_copy(a, b, sem.at[k]) for k, (a, b) in enumerate(pairs)]
    for copy in copies:
        copy.start()
    rows, width = own.shape
    patch_cap = rows * 5 // 32
    keys = reach * rows
    at_query = iota((rows, keys), 0) + keys
    at_key = iota((rows, keys), 1)
    allowed = (at_key > at_query - WINDOW) & (at_key >= (reach - place[0]) * rows)
    bias_out[...] = jnp.where(allowed, 0.0, very_negative)
    for copy in copies[:3]:
        copy.wait()
    normed = normed_rows(own[...], gain[...])
    projected = mm(normed, w_qkv[...]).astype(jnp.bfloat16)
    queries_out[...] = projected[:, :width]
    w_kv[...] = w_qkv[:, width:]
    back = iota((rows, rows), 0) - iota((rows, rows), 1)
    own_bias = jnp.where((back >= 0) & (back < WINDOW), 0.0, very_negative)
    lanes = 2 * HEAD
    for at in range(0, width, lanes):
        parts = attend_part(
            projected[:, at : at + lanes],
            projected[:, width + at : width + at + lanes],
            projected[:, 2 * width + at : 2 * width + at + lanes],
            own_bias,
        )
        for head, (highest, both) in enumerate(parts, at // HEAD):
            highest_out[head] = jnp.broadcast_to(highest, both.shape)
            sums_out[head] = both
    copies[3].wait()
    flag = flags[...]
    at_row, at_col = iota((rows, rows), 0), iota((rows, rows), 1)
    upto = at_col <= at_row
    opened = jnp.max(jnp.where(upto & (flag == 1), at_col, 0), axis=1, keepdims=True)
    since_out[...] = iota((rows, 1), 0) - opened
    own_number = jnp.sum(jnp.where(upto, flag, 0), axis=1, keepdims=True) - 1
    decode_out[...] = jnp.where(iota((rows, patch_cap), 1) <= own_number, 0.0, very_negative)
    eight = jnp.broadcast_to(flag, (8, rows)).astype(jnp.float32).astype(jnp.bfloat16)
    number = mm(eight, as_bf16(at_row <= at_col))[:1].astype(jnp.int32) - 1
    at_byte = iota((patch_cap, rows), 1)
    member = number == iota((patch_cap, rows), 0)
    last = jnp.max(jnp.where(member, at_byte, -1), axis=1, keepdims=True)
    live_out[...] = (last >= 0).astype(jnp.float32)
    ends_out[...] = as_bf16(member & (at_byte == last))
    member_out[...] = jnp.where(member, 0.0, very_negative)

    copies[4].wait()
    square = (patch_cap, patch_cap)
    same = iota(square, 0) == iota(square, 1)
    earlier_slot = iota(square, 0) < iota(square, 1)
    id_rows = [ids[k : k + 1, :] for k in range(2)]
    id_cols = [jnp.sum(jnp.where(same, row, 0), axis=1, keepdims=True) for row in id_rows]
    targets = []
    for row in id_rows:
        named = sum((col == row).astype(jnp.int32) for col in id_cols)
        rank = jnp.sum(jnp.where(earlier_slot, named, 0), axis=0, keepdims=True)
        targets.append(row * capacity + rank)
    extra = table_out.shape[0]
    at_extra = iota((extra, patch_cap), 0)
    table = jnp.where(at_extra == 0, targets[0], jnp.where(at_extra == 1, targets[1], 0))
    table_out[...] = jnp.zeros_like(table_out)
    table_out[:, :patch_cap] = table.astype(jnp.float32).astype(jnp.bfloat16)
    for copy in copies[5:]:
        copy.wait()


def opening(byte_states, patch_start, expert_ids, reach, capacity, place, enc_gain, *ws):
    rows, width = byte_states.shape
    w_qkv, w_out, w_xq, w_xkv = ws
    patch_cap = expert_ids.shape[0]
    extra = -(-(patch_cap + 2) // 16) * 16 - patch_cap
    keys = reach * rows
    heads = width // HEAD
    vmem, anywhere = pl.BlockSpec(memory_space=pltpu.VMEM), pl.BlockSpec(memory_space=pltpu.HBM)
    like = jax.ShapeDtypeStruct
    bf16, f32 = jnp.bfloat16, jnp.float32
    return pl.pallas_call(
        functools.partial(opening_kernel, reach, capacity),
        out_shape=(
            like((rows, width), bf16),
            like((1, width), f32),
            like((width, 2 * width), bf16),
            like(w_out.shape, bf16),
            like(w_xq.shape, bf16),
            like(w_xkv.shape, bf16),
            like((rows, width), bf16),
            like((rows, keys), f32),
            like((rows, 1), jnp.int32),
            like((patch_cap, rows), bf16),
            like((patch_cap, rows), f32),
            like((patch_cap, 1), f32),
            like((extra, width), bf16),
            like((heads, rows, 2 * HEAD), f32),
            like((heads, rows, 2 * HEAD), f32),
            like((rows, patch_cap), f32),
        ),
        in_specs=[pl.BlockSpec(memory_space=pltpu.SMEM)] + [anywhere] * 8,
        out_specs=(vmem,) * 16,
        scratch_shapes=[
            pltpu.VMEM((1, rows), jnp.int32),
            pltpu.VMEM((2, patch_cap), jnp.int32),
            pltpu.VMEM(w_qkv.shape, bf16),
            pltpu.SemaphoreType.DMA((8,)),
        ],
        cost_estimate=cost(4 * rows * width * 3 * width),
        compiler_params=pltpu.CompilerParams(vmem_limit_bytes=16 * 1024 * 1024),
    )(
        place,
        *[
            pltpu.with_memory_space_constraint(v, pltpu.HBM)
            for v in (
                byte_states,
                patch_start.reshape(1, rows),
                expert_ids.T,
                enc_gain.reshape(1, width),
                *ws,
            )
        ],
    )


def encoder_kernel(reach, *refs):
    earlier, refs = refs[:reach], refs[reach:]
    own, gain, w_kv, w_out, w_xq, w_xkv, queries = refs[:7]
    bias, since, ends, member_bias, live, table, own_highest, own_sums = refs[7:15]
    encoded_out, payload_out, pairs_ref, mixed_ref = refs[15:]
    rows, width = own.shape
    patch_cap = ends.shape[0]
    for at, block in enumerate(earlier):
        moved = normed_rows(block[...], gain[...])
        pairs_ref[at * rows : (at + 1) * rows, :] = mm(moved, w_kv[...]).astype(jnp.bfloat16)
    lanes = 2 * HEAD
    for at in range(0, width, lanes):
        parts = attend_part(
            queries[:, at : at + lanes],
            pairs_ref[:, at : at + lanes],
            pairs_ref[:, width + at : width + at + lanes],
            bias[...],
        )
        sums = []
        for head, (highest, both) in enumerate(parts, at // HEAD):
            before = own_highest[head]
            top = jnp.maximum(highest, before)
            sums.append(both * jnp.exp(highest - top) + own_sums[head] * jnp.exp(before - top))
        mixed_ref[:, at : at + lanes] = divided(sums).astype(jnp.bfloat16)
    encoded = (own[...].astype(jnp.float32) + mm(mixed_ref[...], w_out[...])).astype(jnp.bfloat16)
    encoded_out[...] = encoded

    inside = since[...]
    highest = encoded.astype(jnp.float32)
    step = 1
    while step < rows:
        highest = jnp.where(
            inside >= step, jnp.maximum(highest, pltpu.roll(highest, step, 0)), highest
        )
        step *= 2
    pooled = mm(ends[...], highest.astype(jnp.bfloat16))
    patch_queries = mm(pooled.astype(jnp.bfloat16), w_xq[...]).astype(jnp.bfloat16)
    byte_pairs = mm(encoded, w_xkv[...]).astype(jnp.bfloat16)
    mixed = attend_stacked(
        patch_queries, byte_pairs[:, :width], byte_pairs[:, width:], member_bias[...]
    )
    total = jnp.where(live[...] > 0.0, pooled + mixed, 0.0)
    payload_out[:patch_cap, :] = total.astype(jnp.bfloat16)
    payload_out[patch_cap:, :] = table[...]


def encode(earlier, opened):
    rows, width = opened[0].shape
    reach = len(earlier)
    vmem = pl.BlockSpec(memory_space=pltpu.VMEM)
    payload_rows = opened[9].shape[0] + opened[12].shape[0]
    return pl.pallas_call(
        functools.partial(encoder_kernel, reach),
        out_shape=(
            jax.ShapeDtypeStruct((rows, width), jnp.bfloat16),
            jax.ShapeDtypeStruct((payload_rows, width), jnp.bfloat16),
        ),
        in_specs=[vmem] * (15 + reach),
        out_specs=(vmem, vmem),
        scratch_shapes=[
            pltpu.VMEM((reach * rows, 2 * width), jnp.bfloat16),
            pltpu.VMEM((rows, width), jnp.bfloat16),
        ],
        cost_estimate=cost(24 * rows * width * (reach + 1) * rows),
        compiler_params=pltpu.CompilerParams(vmem_limit_bytes=16 * 1024 * 1024),
    )(*earlier, *opened[:15])


def mm_first(a, b):
    return lax.dot_general(a, b, (((0,), (0,)), ((), ())), preferred_element_type=jnp.float32)


def counted_from(values, step, most):
    return sum((values >= step * k).astype(jnp.int32) for k in range(1, most))


GROUP = 4


def give_back(term, spread, group, halves, order):
    for half, (out, places) in enumerate(zip(halves, order)):
        width = out.shape[-1]
        total = mm_first(spread, term[:, half * width : (half + 1) * width]).astype(jnp.bfloat16)
        block = out.shape[-2]
        for s in range(GROUP):
            out[places[group * GROUP + s]] = total[s * block : (s + 1) * block]


def stream_kernel(patch_cap, capacity, experts, blocks, order, *refs):
    me_ref, own_ref, moved_ref, w_up, gain, router, w_in, w_down = refs[:8]
    outs = refs[8:10]
    hidden_ref, gate_ref, spread_ref, all_hidden, later_spread, routed_ref, parts_ref = refs[10:]
    held, width = own_ref.shape[-2:]
    per = GROUP * capacity
    kept = len(blocks) // 2
    me = me_ref[0]
    slots = iota((per, 1), 0)
    source_of_slot = counted_from(slots, capacity, GROUP)
    place_of_slot = slots - source_of_slot * capacity + me * capacity
    lanes = 128

    def spreader(block):
        at_from, at_to = iota((GROUP * lanes, GROUP * block), 0), iota((GROUP * lanes, GROUP * block), 1)
        source = counted_from(at_from, lanes, GROUP)
        within = at_from - source * lanes
        return as_bf16((at_to == source * block + within) & (within < block))

    spread_held, spread_cap = spreader(held), spreader(patch_cap)

    def matched(table, spread, block):
        targets = mm(table, spread).astype(jnp.int32)
        at = iota((1, GROUP * block), 1)
        source = counted_from(at, block, GROUP)
        first, second = targets[0:1], targets[1:2]
        hit = (first == place_of_slot) | (second == place_of_slot)
        hit = hit & (source == source_of_slot) & (at - source * block < patch_cap)
        named = [counted_from(t, capacity, experts) for t in (first, second)]
        return hit, jnp.where(named[0] == me, named[1], named[0])

    others = []
    for g, begin in enumerate(blocks):
        rows_ref = own_ref if g < kept else moved_ref
        tables = []
        for s in range(begin, begin + GROUP):
            block = rows_ref[s, held - 16 : held, :lanes].astype(jnp.float32)
            tables.append(block[patch_cap - (held - 16) : patch_cap - (held - 16) + 8])
        table = jnp.concatenate(tables, axis=1).astype(jnp.bfloat16)
        hit, other = matched(table, spread_held, held)
        others.append(jnp.sum(jnp.where(hit, other, 0), axis=1, keepdims=True))
        block = rows_ref[begin : begin + GROUP].reshape(GROUP * held, width)
        routed_ref[g * per : (g + 1) * per, :] = mm(as_bf16(hit), block).astype(jnp.bfloat16)
        hit, _ = matched(table, spread_cap, patch_cap)
        if g < kept:
            spread_ref[g] = as_bf16(hit)
        else:
            later_spread[g - kept] = as_bf16(hit)
    other = jnp.concatenate(others, axis=0)

    state = mm(routed_ref[...], w_up[...]).astype(jnp.bfloat16).astype(jnp.float32)
    gained = (state * gain[...]).astype(jnp.bfloat16)
    scale = lax.rsqrt(jnp.mean(state * state, axis=-1, keepdims=True) + epsilon)

    parts_ref[...] = jnp.zeros_like(parts_ref)
    left = router[...]
    for part in range(3):
        here = left.astype(jnp.bfloat16).astype(jnp.float32)
        parts_ref[8 * part : 8 * part + experts, :] = here
        left = left - here
    parts = parts_ref[...].astype(jnp.bfloat16)
    deep = parts.shape[1] // 4
    logits = sum(
        mm_t(gained[:, k * deep : (k + 1) * deep], parts[:, k * deep : (k + 1) * deep])
        for k in range(4)
    )
    logits = logits * scale
    expert_of_lane = iota((1, parts_ref.shape[0]), 1) & 7
    mine = jnp.sum(jnp.where(expert_of_lane == me, logits, 0.0), axis=1, keepdims=True)
    rival = jnp.sum(jnp.where(expert_of_lane == other, logits, 0.0), axis=1, keepdims=True)
    highest = jnp.maximum(mine, rival)
    raised = jnp.exp(mine - highest)
    gate = raised / (raised + jnp.exp(rival - highest))

    hidden_share = all_hidden.shape[1]
    chunk = 256 if hidden_share % 256 == 0 else hidden_share
    for at in range(0, hidden_share, chunk):
        opened = mm(gained, w_in[:, at : at + chunk]) * scale
        upper = mm(gained, w_in[:, hidden_share + at : hidden_share + at + chunk]) * scale
        all_hidden[:, at : at + chunk] = (opened / (1.0 + jnp.exp(-opened)) * upper).astype(
            jnp.bfloat16
        )
    first = kept * per
    hidden_ref[...] = all_hidden[:first, :]
    gate_ref[...] = gate[:first]
    term = (mm(all_hidden[first:, :], w_down[...]) * gate[first:]).astype(jnp.bfloat16)
    for g in range(kept):
        give_back(term[g * per : (g + 1) * per], later_spread[g], g, outs, order)


def share_kernel(order, hidden, gate, spread, w_down, *outs):
    groups, per, _ = spread.shape
    term = (mm(hidden[...], w_down[...]) * gate[...]).astype(jnp.bfloat16)
    for g in range(groups):
        give_back(term[g * per : (g + 1) * per], spread[g], g, outs, order)


def share_shapes(sources, patch_cap, wide):
    half = jax.ShapeDtypeStruct((sources, patch_cap, wide // 2), jnp.bfloat16)
    return (half, half)


def stream(own, moved, blocks, order, patch_cap, capacity, me, w_up, gain, router, w_in, w_down):
    held, width = own.shape[-2:]
    experts, wide = router.shape
    vmem = pl.BlockSpec(memory_space=pltpu.VMEM)
    per = GROUP * capacity
    slots = 2 * len(blocks) * per
    spread = jax.ShapeDtypeStruct((len(blocks), per, GROUP * patch_cap), jnp.bfloat16)
    return pl.pallas_call(
        functools.partial(stream_kernel, patch_cap, capacity, experts, blocks * 2, order),
        out_shape=share_shapes(len(blocks) * GROUP, patch_cap, wide)
        + (
            jax.ShapeDtypeStruct((slots // 2, w_down.shape[0]), jnp.bfloat16),
            jax.ShapeDtypeStruct((slots // 2, 1), jnp.float32),
            spread,
        ),
        in_specs=[pl.BlockSpec(memory_space=pltpu.SMEM)] + [vmem] * 7,
        out_specs=(vmem,) * 5,
        scratch_shapes=[
            pltpu.VMEM((slots, w_down.shape[0]), jnp.bfloat16),
            pltpu.VMEM(spread.shape, jnp.bfloat16),
            pltpu.VMEM((slots, width), jnp.bfloat16),
            pltpu.VMEM((24, wide), jnp.float32),
        ],
        cost_estimate=cost(slots * wide * (width + w_in.shape[1]) // 4),
        compiler_params=pltpu.CompilerParams(vmem_limit_bytes=24 * 1024 * 1024),
    )(me, own, moved, w_up, gain, router, w_in, w_down)


def gated_share(hidden, gate, spread, w_down, order, patch_cap):
    groups = spread.shape[0]
    wide = w_down.shape[1]
    vmem = pl.BlockSpec(memory_space=pltpu.VMEM)
    return pl.pallas_call(
        functools.partial(share_kernel, order),
        out_shape=share_shapes(groups * GROUP, patch_cap, wide),
        in_specs=[vmem] * 4,
        out_specs=(vmem,) * 2,
        cost_estimate=cost(1000),
        compiler_params=pltpu.CompilerParams(vmem_limit_bytes=16 * 1024 * 1024),
    )(hidden, gate, spread, w_down)


def prepare_kernel(encoded, payload, gain, w_dq, w_up, queries, state):
    queries[...] = mm(normed_rows(encoded[...], gain[...]), w_dq[...]).astype(jnp.bfloat16)
    state[...] = mm(payload[: state.shape[0], :], w_up[...]).astype(jnp.bfloat16)


def prepare(encoded, payload, patch_cap, gain, w_dq, w_up):
    vmem = pl.BlockSpec(memory_space=pltpu.VMEM)
    return pl.pallas_call(
        prepare_kernel,
        out_shape=(
            jax.ShapeDtypeStruct(encoded.shape, jnp.bfloat16),
            jax.ShapeDtypeStruct((patch_cap, w_up.shape[1]), jnp.bfloat16),
        ),
        in_specs=[vmem] * 5,
        out_specs=(vmem, vmem),
        cost_estimate=cost(2 * patch_cap * w_up.size),
        compiler_params=pltpu.CompilerParams(vmem_limit_bytes=8 * 1024 * 1024),
    )(encoded, payload, gain.reshape(1, -1), w_dq, w_up)


def decode_kernel(wholes, *refs):
    state, *parts = refs[:-8]
    encoded, queries, bias, w_dkv, w_do, bytes_out, patch_out, mixed_ref = refs[-8:]
    rows, width = encoded.shape
    wide = state.shape[1] // 2
    per = (len(parts) - wholes) // 2
    pairs = 0.0
    for half in range(2):
        here = slice(half * wide, (half + 1) * wide)
        total = state[:, here].astype(jnp.float32)
        for part in parts[wholes + half * per : wholes + (half + 1) * per]:
            total = total + part[0].astype(jnp.float32)
        for part in parts[:wholes]:
            total = total + part[:, here].astype(jnp.float32)
        states = total.astype(jnp.bfloat16)
        patch_out[:, here] = states
        pairs = pairs + mm(states, w_dkv[here, :])
    pairs = pairs.astype(jnp.bfloat16)
    lanes = 2 * HEAD
    for at in range(0, width, lanes):
        mixed = attend_pair(
            queries[:, at : at + lanes],
            pairs[:, at : at + lanes],
            pairs[:, width + at : width + at + lanes],
            bias[...],
        )
        mixed_ref[:, at : at + lanes] = mixed.astype(jnp.bfloat16)
    bytes_out[...] = (encoded[...].astype(jnp.float32) + mm(mixed_ref[...], w_do[...])).astype(
        jnp.bfloat16
    )


def decode(state, wholes, halves, encoded, queries, bias, w_dkv, w_do):
    vmem = pl.BlockSpec(memory_space=pltpu.VMEM)
    parts = [*wholes, *halves[0], *halves[1]]
    return pl.pallas_call(
        functools.partial(decode_kernel, len(wholes)),
        out_shape=(
            jax.ShapeDtypeStruct(encoded.shape, jnp.bfloat16),
            jax.ShapeDtypeStruct(state.shape, jnp.bfloat16),
        ),
        in_specs=[vmem] * (6 + len(parts)),
        out_specs=(vmem, vmem),
        scratch_shapes=[pltpu.VMEM(encoded.shape, jnp.bfloat16)],
        cost_estimate=cost(4 * 256 * w_dkv.size),
        compiler_params=pltpu.CompilerParams(vmem_limit_bytes=12 * 1024 * 1024),
    )(state, *parts, encoded, queries, bias, w_dkv, w_do)


def digits():
    seq, expert = lax.axis_size("seq"), lax.axis_size("expert")
    inner = 2 if seq % 2 == 0 else 1
    core = 2 if expert % 2 == 0 else 1
    return {
        "z": ("seq", inner, seq // inner),
        "x": ("seq", 1, inner),
        "y": ("expert", core, expert // core),
        "c": ("expert", 1, core),
    }


def shift(x, digit, by):
    axis, stride, radix = digit
    pairs = []
    for i in range(lax.axis_size(axis)):
        g = i // stride % radix
        pairs.append((i, i + ((g + by) % radix - g) * stride))
    return lax.ppermute(x, axis, pairs)


def gathered(x, digit, place=0):
    return jnp.stack([x] + [shift(x, digit, d) for d in range(1, digit[2])], axis=place)


def gather_chip(x, beside):
    d = digits()
    half = x.shape[1] // 2
    x = gathered(x, d["z"])
    x, beside = lax.optimization_barrier((x, beside))
    left = gathered(gathered(x[..., :half], d["x"], 1), d["y"], 1)
    right = gathered(gathered(x[..., half:], d["y"], 1), d["x"], 2)
    return jnp.concatenate([left, right], axis=-1), beside


def summed(parts):
    total = parts[0].astype(jnp.float32)
    for part in parts[1:]:
        total = total + part.astype(jnp.float32)
    return total


def leg(x, digit, place):
    parts = [lax.index_in_dim(x, d, place, keepdims=False) for d in range(digit[2])]
    return [parts[0]] + [shift(parts[d], digit, -d) for d in range(1, digit[2])]


def narrow(v):
    return v.astype(jnp.bfloat16)


def behind(values, *others):
    return jax.tree.map(lambda v: lax.optimization_barrier((v, others))[0], values)


def ends(legs):
    return [narrow(summed(parts)) for parts in legs]


def mixture(payload, patch_cap, capacity, w_up, moe_gain, w_router, w_in, w_down):
    d = digits()
    wide = w_up.shape[1]
    paired = w_in.reshape(w_in.shape[1], -1)
    own, paired = gather_chip(payload, paired)
    far, ys, xs = own.shape[:3]
    own = own.reshape((-1,) + own.shape[3:])
    moved = [shift(own, d["c"], by) for by in range(1, d["c"][2])]
    assert len(moved) == 1 and ys * xs % GROUP == 0
    moved = moved[0]
    me = lax.axis_index("expert").astype(jnp.int32).reshape(1)
    weights = (w_up, moe_gain.reshape(1, wide), w_router.T, paired, w_down[0])
    w_last = w_down[0]

    if far == 4:
        streams = [[2], [1, 3], [0]]
    else:
        apart = [*range(1, far), 0]
        streams = [apart[at : at + 2] for at in range(0, far, 2)]

    def blocks_of(zs):
        return [z * ys * xs + at for z in zs for at in range(0, ys * xs, GROUP)]

    def order_of(zs):
        near = len(zs)
        left, right = [], []
        for z in range(near):
            for y in range(ys):
                for x in range(xs):
                    left.append((x * ys + y) * near + z)
                    right.append((y * xs + x) * near + z)
        return left, right

    def shaped(halves, zs):
        left, right = halves
        tail = (len(zs),) + left.shape[1:]
        return [left.reshape((xs, ys) + tail), right.reshape((ys, xs) + tail)]

    def begin(zs, moved):
        got = stream(own, moved, blocks_of(zs), order_of(zs), patch_cap, capacity, me, *weights)
        sent = [shift(v, d["c"], -1) for v in shaped(got[:2], zs)]
        return sent, got

    def finish(zs, sent, hidden, gate, spread):
        kept = gated_share(hidden, gate, spread, w_last, order_of(zs), patch_cap)
        return [narrow(summed(pair)) for pair in zip(shaped(kept, zs), sent)]

    def first_leg(sums):
        return [leg(sums[0], d["x"], 0), leg(sums[1], d["y"], 0)]

    def second_leg(sums):
        return [leg(sums[0], d["y"], 0), leg(sums[1], d["x"], 0)]

    wholes = []

    def last_leg(zs, sums):
        made = []
        for at, z in enumerate(zs):
            if z:
                made.append(jnp.concatenate([v[at] for v in sums], axis=-1))
                wholes.append(shift(made[-1], d["z"], -z))
        return made

    first, second, added = None, None, None
    for zs in streams:
        sent, got = begin(zs, moved if added is None else behind(moved, added))
        hidden, gate, spread = got[2:]
        if second:
            made = last_leg(second[0], ends(behind(second[1], gate)))
            gate, second = behind(gate, made), None
        if first:
            sums = ends(behind(first[1], gate))
            gate, first, second = behind(gate, sums), None, (first[0], second_leg(sums))
        added = finish(zs, sent, hidden, gate, spread)
        first = (zs, first_leg(added))
    zs, legs = first
    if second:
        made = last_leg(second[0], ends(second[1]))
        legs = behind(legs, made)
    sums = ends(legs)
    legs = second_leg(sums)
    if zs != [0]:
        sums = ends(legs)
        last_leg(zs, sums)
        at = zs.index(0)
        legs = [[v[at : at + 1]] for v in sums]
    return wholes, legs


def per_device(
    byte_states,
    patch_start,
    expert_ids,
    enc_gain,
    w_qkv,
    w_out,
    w_xq,
    w_xkv,
    w_up,
    moe_gain,
    w_router,
    w_in,
    w_down,
    dec_gain,
    w_dq,
    w_dkv,
    w_do,
):
    byte_dev = byte_states.shape[0]
    patch_cap = expert_ids.shape[0]
    experts = w_router.shape[1]
    capacity = 12 * patch_cap // (5 * experts)
    both_axes = ("seq", "expert")
    reach = -(-WINDOW // byte_dev)
    place = lax.axis_index(both_axes).astype(jnp.int32).reshape(1)
    opened = opening(
        byte_states,
        patch_start,
        expert_ids,
        reach,
        capacity,
        place,
        enc_gain,
        w_qkv,
        w_out,
        w_xq,
        w_xkv,
    )
    earlier = [passed_along(byte_states, both_axes, by) for by in range(reach, 0, -1)]
    encoded, payload = encode(earlier, opened)
    wholes, halves = mixture(payload, patch_cap, capacity, w_up, moe_gain, w_router, w_in, w_down)
    queries, state = prepare(encoded, payload, patch_cap, dec_gain, w_dq, w_up)
    return decode(state, wholes, halves, encoded, queries, opened[15], w_dkv, w_do)


def solution(mesh):
    in_specs = (
        P(("seq", "expert"), None),
        P(("seq", "expert")),
        P(("seq", "expert"), None),
        P(),
        P(),
        P(),
        P(),
        P(),
        P(),
        P(),
        P(),
        P("expert", None, None, "seq"),
        P("expert", "seq", None),
        P(),
        P(),
        P(),
        P(),
    )
    out_specs = (P(("seq", "expert"), None), P(("seq", "expert"), None))
    return jax.shard_map(
        per_device, mesh=mesh, in_specs=in_specs, out_specs=out_specs, check_vma=False
    )
```

```python
import functools
import math

import jax
import jax.numpy as jnp
from jax import lax
from jax.experimental import pallas as pl
from jax.experimental.pallas import tpu as pltpu
from jax.sharding import PartitionSpec as P

HEADS_L = 8
HEAD = 64
WINDOW = 512


epsilon = 1e-06
very_negative = -1e30


def passed_along(x, axis, by):
    length = lax.axis_size(axis)
    pairs = [(i, i + by) for i in range(length) if 0 <= i + by < length]
    return lax.ppermute(x, axis, pairs)


def normed_rows(x, gain_row):
    wide = x.astype(jnp.float32)
    scale = lax.rsqrt(jnp.mean(wide * wide, axis=-1, keepdims=True) + epsilon)
    return (wide * scale * gain_row).astype(jnp.bfloat16)


def cost(flops):
    return pl.CostEstimate(flops=int(flops), transcendentals=0, bytes_accessed=0)


def mm(a, b):
    return jnp.dot(a, b, preferred_element_type=jnp.float32)


def mm_t(a, b):
    return lax.dot_general(a, b, (((1,), (1,)), ((), ())), preferred_element_type=jnp.float32)


def as_bf16(mask):
    return mask.astype(jnp.float32).astype(jnp.bfloat16)


def iota(shape, dim):
    return lax.broadcasted_iota(jnp.int32, shape, dim)


def attend_part(q, k, v, bias):
    first = iota((1, 2 * HEAD), 1) < HEAD
    q = q * jnp.asarray(1.0 / math.sqrt(HEAD), q.dtype)
    parts = []
    for here in (first, jnp.logical_not(first)):
        scores = mm_t(jnp.where(here, q, jnp.zeros_like(q)), k) + bias
        highest = jnp.max(scores, axis=-1, keepdims=True)
        raised = jnp.exp(scores - highest).astype(jnp.bfloat16)
        parts.append((highest, mm(raised, jnp.where(here, v, jnp.ones_like(v)))))
    return parts


def divided(sums):
    first = iota((1, 2 * HEAD), 1) < HEAD
    outs = [both / pltpu.roll(both, HEAD, 1) for both in sums]
    return jnp.where(first, outs[0], outs[1])


def head_lanes(width):
    lane = iota((1, width), 1)
    return [(lane >= at) & (lane < at + HEAD) for at in range(0, width, HEAD)]


def stacked(x):
    blocks = [jnp.where(here, x, 0.0) for here in head_lanes(x.shape[1])]
    return jnp.concatenate(blocks, axis=0).astype(jnp.bfloat16)


def attend_columns(q, k, v, bias):
    keys, width = k.shape
    scaled = k.astype(jnp.float32) * (1.0 / math.sqrt(HEAD))
    scores = mm_t(stacked(scaled), q).reshape(width // HEAD, keys, q.shape[0]) + bias[None]
    raised = jnp.exp(scores - jnp.max(scores, axis=1, keepdims=True))
    weights = raised / jnp.sum(raised, axis=1, keepdims=True)
    weights = weights.reshape(-1, q.shape[0]).astype(jnp.bfloat16)
    return mm_first(weights, stacked(v.astype(jnp.float32)))


def attend_stacked(q, k, v, bias):
    rows, width = q.shape
    heads = head_lanes(width)
    scaled = q.astype(jnp.float32) * (1.0 / math.sqrt(HEAD))
    scores = mm_t(stacked(scaled), k) + jnp.concatenate([bias] * len(heads), axis=0)
    raised = jnp.exp(scores - jnp.max(scores, axis=-1, keepdims=True))
    mixed = mm(raised.astype(jnp.bfloat16), v) / jnp.sum(raised, axis=-1, keepdims=True)
    out = jnp.zeros((rows, width), jnp.float32)
    for number, here in enumerate(heads):
        out = jnp.where(here, mixed[number * rows : (number + 1) * rows], out)
    return out


def opening_kernel(reach, capacity, *refs):
    place, own_in, flags_in, ids_in, gain_in, w_qkv_in, w_out_in, w_xq_in, w_xkv_in = refs[:9]
    outs, (flags, ids, w_qkv, sem) = refs[9:-4], refs[-4:]
    own, gain, w_kv, w_out, w_xq, w_xkv, queries_out = outs[:7]
    bias_out, since_out, ends_out, member_out, live_out, table_out = outs[7:13]
    highest_out, sums_out, decode_out = outs[13:]
    pairs = [
        (own_in, own),
        (gain_in, gain),
        (w_qkv_in, w_qkv),
        (flags_in, flags),
        (ids_in, ids),
        (w_out_in, w_out),
        (w_xq_in, w_xq),
        (w_xkv_in, w_xkv),
    ]
    copies = [pltpu.make_async_copy(a, b, sem.at[k]) for k, (a, b) in enumerate(pairs)]
    for copy in copies:
        copy.start()
    rows, width = own.shape
    patch_cap = rows * 5 // 32
    keys = reach * rows
    at_query = iota((rows, keys), 0) + keys
    at_key = iota((rows, keys), 1)
    allowed = (at_key > at_query - WINDOW) & (at_key >= (reach - place[0]) * rows)
    bias_out[...] = jnp.where(allowed, 0.0, very_negative)
    for copy in copies[:3]:
        copy.wait()
    normed = normed_rows(own[...], gain[...])
    projected = mm(normed, w_qkv[...]).astype(jnp.bfloat16)
    queries_out[...] = projected[:, :width]
    w_kv[...] = w_qkv[:, width:]
    back = iota((rows, rows), 0) - iota((rows, rows), 1)
    own_bias = jnp.where((back >= 0) & (back < WINDOW), 0.0, very_negative)
    lanes = 2 * HEAD
    for at in range(0, width, lanes):
        parts = attend_part(
            projected[:, at : at + lanes],
            projected[:, width + at : width + at + lanes],
            projected[:, 2 * width + at : 2 * width + at + lanes],
            own_bias,
        )
        for head, (highest, both) in enumerate(parts, at // HEAD):
            highest_out[head] = jnp.broadcast_to(highest, both.shape)
            sums_out[head] = both
    copies[3].wait()
    flag = flags[...]
    at_row, at_col = iota((rows, rows), 0), iota((rows, rows), 1)
    upto = at_col <= at_row
    opened = jnp.max(jnp.where(upto & (flag == 1), at_col, 0), axis=1, keepdims=True)
    since_out[...] = iota((rows, 1), 0) - opened
    eight = jnp.broadcast_to(flag, (8, rows)).astype(jnp.float32).astype(jnp.bfloat16)
    number = mm(eight, as_bf16(at_row <= at_col))[:1].astype(jnp.int32) - 1
    at_byte = iota((patch_cap, rows), 1)
    member = number == iota((patch_cap, rows), 0)
    decode_out[...] = jnp.where(iota((patch_cap, rows), 0) <= number, 0.0, very_negative)
    last = jnp.max(jnp.where(member, at_byte, -1), axis=1, keepdims=True)
    live_out[...] = (last >= 0).astype(jnp.float32)
    ends_out[...] = as_bf16(member & (at_byte == last))
    member_out[...] = jnp.where(member, 0.0, very_negative)

    copies[4].wait()
    square = (patch_cap, patch_cap)
    same = iota(square, 0) == iota(square, 1)
    earlier_slot = iota(square, 0) < iota(square, 1)
    id_rows = [ids[k : k + 1, :] for k in range(2)]
    id_cols = [jnp.sum(jnp.where(same, row, 0), axis=1, keepdims=True) for row in id_rows]
    targets = []
    for row in id_rows:
        named = sum((col == row).astype(jnp.int32) for col in id_cols)
        rank = jnp.sum(jnp.where(earlier_slot, named, 0), axis=0, keepdims=True)
        targets.append(row * capacity + rank)
    extra = table_out.shape[0]
    at_extra = iota((extra, patch_cap), 0)
    table = jnp.where(at_extra == 0, targets[0], jnp.where(at_extra == 1, targets[1], 0))
    table_out[...] = jnp.zeros_like(table_out)
    table_out[:, :patch_cap] = table.astype(jnp.float32).astype(jnp.bfloat16)
    for copy in copies[5:]:
        copy.wait()


def opening(byte_states, patch_start, expert_ids, reach, capacity, place, enc_gain, *ws):
    rows, width = byte_states.shape
    w_qkv, w_out, w_xq, w_xkv = ws
    patch_cap = expert_ids.shape[0]
    extra = -(-(patch_cap + 2) // 16) * 16 - patch_cap
    keys = reach * rows
    heads = width // HEAD
    vmem, anywhere = pl.BlockSpec(memory_space=pltpu.VMEM), pl.BlockSpec(memory_space=pltpu.HBM)
    like = jax.ShapeDtypeStruct
    bf16, f32 = jnp.bfloat16, jnp.float32
    return pl.pallas_call(
        functools.partial(opening_kernel, reach, capacity),
        out_shape=(
            like((rows, width), bf16),
            like((1, width), f32),
            like((width, 2 * width), bf16),
            like(w_out.shape, bf16),
            like(w_xq.shape, bf16),
            like(w_xkv.shape, bf16),
            like((rows, width), bf16),
            like((rows, keys), f32),
            like((rows, 1), jnp.int32),
            like((patch_cap, rows), bf16),
            like((patch_cap, rows), f32),
            like((patch_cap, 1), f32),
            like((extra, width), bf16),
            like((heads, rows, 2 * HEAD), f32),
            like((heads, rows, 2 * HEAD), f32),
            like((patch_cap, rows), f32),
        ),
        in_specs=[pl.BlockSpec(memory_space=pltpu.SMEM)] + [anywhere] * 8,
        out_specs=(vmem,) * 16,
        scratch_shapes=[
            pltpu.VMEM((1, rows), jnp.int32),
            pltpu.VMEM((2, patch_cap), jnp.int32),
            pltpu.VMEM(w_qkv.shape, bf16),
            pltpu.SemaphoreType.DMA((8,)),
        ],
        cost_estimate=cost(4 * rows * width * 3 * width),
        compiler_params=pltpu.CompilerParams(vmem_limit_bytes=16 * 1024 * 1024),
    )(
        place,
        *[
            pltpu.with_memory_space_constraint(v, pltpu.HBM)
            for v in (
                byte_states,
                patch_start.reshape(1, rows),
                expert_ids.T,
                enc_gain.reshape(1, width),
                *ws,
            )
        ],
    )


def encoder_kernel(reach, *refs):
    earlier, refs = refs[:reach], refs[reach:]
    own, gain, w_kv, w_out, w_xq, w_xkv, queries = refs[:7]
    bias, since, ends, member_bias, live, table, own_highest, own_sums = refs[7:15]
    encoded_out, payload_out, pairs_ref, mixed_ref = refs[15:]
    rows, width = own.shape
    patch_cap = ends.shape[0]
    for at, block in enumerate(earlier):
        moved = normed_rows(block[...], gain[...])
        pairs_ref[at * rows : (at + 1) * rows, :] = mm(moved, w_kv[...]).astype(jnp.bfloat16)
    lanes = 2 * HEAD
    for at in range(0, width, lanes):
        parts = attend_part(
            queries[:, at : at + lanes],
            pairs_ref[:, at : at + lanes],
            pairs_ref[:, width + at : width + at + lanes],
            bias[...],
        )
        sums = []
        for head, (highest, both) in enumerate(parts, at // HEAD):
            before = own_highest[head]
            top = jnp.maximum(highest, before)
            sums.append(both * jnp.exp(highest - top) + own_sums[head] * jnp.exp(before - top))
        mixed_ref[:, at : at + lanes] = divided(sums).astype(jnp.bfloat16)
    encoded = (own[...].astype(jnp.float32) + mm(mixed_ref[...], w_out[...])).astype(jnp.bfloat16)
    encoded_out[...] = encoded

    inside = since[...]
    highest = encoded.astype(jnp.float32)
    step = 1
    while step < rows:
        highest = jnp.where(
            inside >= step, jnp.maximum(highest, pltpu.roll(highest, step, 0)), highest
        )
        step *= 2
    pooled = mm(ends[...], highest.astype(jnp.bfloat16))
    patch_queries = mm(pooled.astype(jnp.bfloat16), w_xq[...]).astype(jnp.bfloat16)
    byte_pairs = mm(encoded, w_xkv[...]).astype(jnp.bfloat16)
    mixed = attend_stacked(
        patch_queries, byte_pairs[:, :width], byte_pairs[:, width:], member_bias[...]
    )
    total = jnp.where(live[...] > 0.0, pooled + mixed, 0.0)
    payload_out[:patch_cap, :] = total.astype(jnp.bfloat16)
    payload_out[patch_cap:, :] = table[...]


def encode(earlier, opened):
    rows, width = opened[0].shape
    reach = len(earlier)
    vmem = pl.BlockSpec(memory_space=pltpu.VMEM)
    payload_rows = opened[9].shape[0] + opened[12].shape[0]
    return pl.pallas_call(
        functools.partial(encoder_kernel, reach),
        out_shape=(
            jax.ShapeDtypeStruct((rows, width), jnp.bfloat16),
            jax.ShapeDtypeStruct((payload_rows, width), jnp.bfloat16),
        ),
        in_specs=[vmem] * (15 + reach),
        out_specs=(vmem, vmem),
        scratch_shapes=[
            pltpu.VMEM((reach * rows, 2 * width), jnp.bfloat16),
            pltpu.VMEM((rows, width), jnp.bfloat16),
        ],
        cost_estimate=cost(24 * rows * width * (reach + 1) * rows),
        compiler_params=pltpu.CompilerParams(vmem_limit_bytes=16 * 1024 * 1024),
    )(*earlier, *opened[:15])


def mm_first(a, b):
    return lax.dot_general(a, b, (((0,), (0,)), ((), ())), preferred_element_type=jnp.float32)


def counted_from(values, step, most):
    return sum((values >= step * k).astype(jnp.int32) for k in range(1, most))


GROUP = 4


def give_back(term, spread, group, halves, order):
    for half, (out, places) in enumerate(zip(halves, order)):
        width = out.shape[-1]
        total = mm_first(spread, term[:, half * width : (half + 1) * width]).astype(jnp.bfloat16)
        block = out.shape[-2]
        for s in range(GROUP):
            out[places[group * GROUP + s]] = total[s * block : (s + 1) * block]


def stream_kernel(patch_cap, capacity, experts, blocks, order, *refs):
    me_ref, own_ref, moved_ref, w_up, gain, router, w_in, w_down = refs[:8]
    outs = refs[8:10]
    hidden_ref, gate_ref, spread_ref, all_hidden, later_spread, routed_ref, parts_ref = refs[10:]
    held, width = own_ref.shape[-2:]
    per = GROUP * capacity
    kept = len(blocks) // 2
    me = me_ref[0]
    slots = iota((per, 1), 0)
    source_of_slot = counted_from(slots, capacity, GROUP)
    place_of_slot = slots - source_of_slot * capacity + me * capacity
    lanes = 128

    def spreader(block):
        at_from, at_to = iota((GROUP * lanes, GROUP * block), 0), iota((GROUP * lanes, GROUP * block), 1)
        source = counted_from(at_from, lanes, GROUP)
        within = at_from - source * lanes
        return as_bf16((at_to == source * block + within) & (within < block))

    spread_held, spread_cap = spreader(held), spreader(patch_cap)

    def matched(table, spread, block):
        targets = mm(table, spread).astype(jnp.int32)
        at = iota((1, GROUP * block), 1)
        source = counted_from(at, block, GROUP)
        first, second = targets[0:1], targets[1:2]
        hit = (first == place_of_slot) | (second == place_of_slot)
        hit = hit & (source == source_of_slot) & (at - source * block < patch_cap)
        named = [counted_from(t, capacity, experts) for t in (first, second)]
        return hit, jnp.where(named[0] == me, named[1], named[0])

    others = []
    for g, begin in enumerate(blocks):
        rows_ref = own_ref if g < kept else moved_ref
        tables = []
        for s in range(begin, begin + GROUP):
            block = rows_ref[s, held - 16 : held, :lanes].astype(jnp.float32)
            tables.append(block[patch_cap - (held - 16) : patch_cap - (held - 16) + 8])
        table = jnp.concatenate(tables, axis=1).astype(jnp.bfloat16)
        hit, other = matched(table, spread_held, held)
        others.append(jnp.sum(jnp.where(hit, other, 0), axis=1, keepdims=True))
        block = rows_ref[begin : begin + GROUP].reshape(GROUP * held, width)
        routed_ref[g * per : (g + 1) * per, :] = mm(as_bf16(hit), block).astype(jnp.bfloat16)
        hit, _ = matched(table, spread_cap, patch_cap)
        if g < kept:
            spread_ref[g] = as_bf16(hit)
        else:
            later_spread[g - kept] = as_bf16(hit)
    other = jnp.concatenate(others, axis=0)

    state = mm(routed_ref[...], w_up[...]).astype(jnp.bfloat16).astype(jnp.float32)
    gained = (state * gain[...]).astype(jnp.bfloat16)
    scale = lax.rsqrt(jnp.mean(state * state, axis=-1, keepdims=True) + epsilon)

    parts_ref[...] = jnp.zeros_like(parts_ref)
    left = router[...]
    for part in range(3):
        here = left.astype(jnp.bfloat16).astype(jnp.float32)
        parts_ref[8 * part : 8 * part + experts, :] = here
        left = left - here
    parts = parts_ref[...].astype(jnp.bfloat16)
    deep = parts.shape[1] // 4
    logits = sum(
        mm_t(gained[:, k * deep : (k + 1) * deep], parts[:, k * deep : (k + 1) * deep])
        for k in range(4)
    )
    logits = logits * scale
    expert_of_lane = iota((1, parts_ref.shape[0]), 1) & 7
    mine = jnp.sum(jnp.where(expert_of_lane == me, logits, 0.0), axis=1, keepdims=True)
    rival = jnp.sum(jnp.where(expert_of_lane == other, logits, 0.0), axis=1, keepdims=True)
    highest = jnp.maximum(mine, rival)
    raised = jnp.exp(mine - highest)
    gate = raised / (raised + jnp.exp(rival - highest))

    hidden_share = all_hidden.shape[1]
    chunk = 256 if hidden_share % 256 == 0 else hidden_share
    for at in range(0, hidden_share, chunk):
        opened = mm(gained, w_in[:, at : at + chunk]) * scale
        upper = mm(gained, w_in[:, hidden_share + at : hidden_share + at + chunk]) * scale
        all_hidden[:, at : at + chunk] = (opened / (1.0 + jnp.exp(-opened)) * upper).astype(
            jnp.bfloat16
        )
    first = kept * per
    hidden_ref[...] = all_hidden[:first, :]
    gate_ref[...] = gate[:first]
    term = (mm(all_hidden[first:, :], w_down[...]) * gate[first:]).astype(jnp.bfloat16)
    for g in range(kept):
        give_back(term[g * per : (g + 1) * per], later_spread[g], g, outs, order)


def share_kernel(order, hidden, gate, spread, w_down, *outs):
    groups, per, _ = spread.shape
    term = (mm(hidden[...], w_down[...]) * gate[...]).astype(jnp.bfloat16)
    for g in range(groups):
        give_back(term[g * per : (g + 1) * per], spread[g], g, outs, order)


def share_shapes(sources, patch_cap, wide):
    half = jax.ShapeDtypeStruct((sources, patch_cap, wide // 2), jnp.bfloat16)
    return (half, half)


def stream(own, moved, blocks, order, patch_cap, capacity, me, w_up, gain, router, w_in, w_down):
    held, width = own.shape[-2:]
    experts, wide = router.shape
    vmem = pl.BlockSpec(memory_space=pltpu.VMEM)
    per = GROUP * capacity
    slots = 2 * len(blocks) * per
    spread = jax.ShapeDtypeStruct((len(blocks), per, GROUP * patch_cap), jnp.bfloat16)
    return pl.pallas_call(
        functools.partial(stream_kernel, patch_cap, capacity, experts, blocks * 2, order),
        out_shape=share_shapes(len(blocks) * GROUP, patch_cap, wide)
        + (
            jax.ShapeDtypeStruct((slots // 2, w_down.shape[0]), jnp.bfloat16),
            jax.ShapeDtypeStruct((slots // 2, 1), jnp.float32),
            spread,
        ),
        in_specs=[pl.BlockSpec(memory_space=pltpu.SMEM)] + [vmem] * 7,
        out_specs=(vmem,) * 5,
        scratch_shapes=[
            pltpu.VMEM((slots, w_down.shape[0]), jnp.bfloat16),
            pltpu.VMEM(spread.shape, jnp.bfloat16),
            pltpu.VMEM((slots, width), jnp.bfloat16),
            pltpu.VMEM((24, wide), jnp.float32),
        ],
        cost_estimate=cost(slots * wide * (width + w_in.shape[1]) // 4),
        compiler_params=pltpu.CompilerParams(vmem_limit_bytes=24 * 1024 * 1024),
    )(me, own, moved, w_up, gain, router, w_in, w_down)


def gated_share(hidden, gate, spread, w_down, order, patch_cap):
    groups = spread.shape[0]
    wide = w_down.shape[1]
    vmem = pl.BlockSpec(memory_space=pltpu.VMEM)
    return pl.pallas_call(
        functools.partial(share_kernel, order),
        out_shape=share_shapes(groups * GROUP, patch_cap, wide),
        in_specs=[vmem] * 4,
        out_specs=(vmem,) * 2,
        cost_estimate=cost(1000),
        compiler_params=pltpu.CompilerParams(vmem_limit_bytes=16 * 1024 * 1024),
    )(hidden, gate, spread, w_down)


def prepare_kernel(encoded, payload, gain, w_dq, w_up, queries, state):
    queries[...] = mm(normed_rows(encoded[...], gain[...]), w_dq[...]).astype(jnp.bfloat16)
    state[...] = mm(payload[: state.shape[0], :], w_up[...]).astype(jnp.bfloat16)


def prepare(encoded, payload, patch_cap, gain, w_dq, w_up):
    vmem = pl.BlockSpec(memory_space=pltpu.VMEM)
    return pl.pallas_call(
        prepare_kernel,
        out_shape=(
            jax.ShapeDtypeStruct(encoded.shape, jnp.bfloat16),
            jax.ShapeDtypeStruct((patch_cap, w_up.shape[1]), jnp.bfloat16),
        ),
        in_specs=[vmem] * 5,
        out_specs=(vmem, vmem),
        cost_estimate=cost(2 * patch_cap * w_up.size),
        compiler_params=pltpu.CompilerParams(vmem_limit_bytes=8 * 1024 * 1024),
    )(encoded, payload, gain.reshape(1, -1), w_dq, w_up)


def decode_kernel(wholes, *refs):
    state, *parts = refs[:-7]
    encoded, queries, bias, w_dkv, w_do, bytes_out, patch_out = refs[-7:]
    width = encoded.shape[1]
    wide = state.shape[1] // 2
    per = (len(parts) - wholes) // 2
    pairs = 0.0
    for half in range(2):
        here = slice(half * wide, (half + 1) * wide)
        total = state[:, here].astype(jnp.float32)
        for part in parts[wholes + half * per : wholes + (half + 1) * per]:
            total = total + part[0].astype(jnp.float32)
        for part in parts[:wholes]:
            total = total + part[:, here].astype(jnp.float32)
        states = total.astype(jnp.bfloat16)
        patch_out[:, here] = states
        pairs = pairs + mm(states, w_dkv[here, :])
    pairs = pairs.astype(jnp.bfloat16)
    mixed = attend_columns(queries[...], pairs[:, :width], pairs[:, width:], bias[...])
    bytes_out[...] = (
        encoded[...].astype(jnp.float32) + mm(mixed.astype(jnp.bfloat16), w_do[...])
    ).astype(jnp.bfloat16)


def decode(state, wholes, halves, encoded, queries, bias, w_dkv, w_do):
    vmem = pl.BlockSpec(memory_space=pltpu.VMEM)
    parts = [*wholes, *halves[0], *halves[1]]
    return pl.pallas_call(
        functools.partial(decode_kernel, len(wholes)),
        out_shape=(
            jax.ShapeDtypeStruct(encoded.shape, jnp.bfloat16),
            jax.ShapeDtypeStruct(state.shape, jnp.bfloat16),
        ),
        in_specs=[vmem] * (6 + len(parts)),
        out_specs=(vmem, vmem),
        cost_estimate=cost(4 * 256 * w_dkv.size),
        compiler_params=pltpu.CompilerParams(vmem_limit_bytes=12 * 1024 * 1024),
    )(state, *parts, encoded, queries, bias, w_dkv, w_do)


def digits():
    seq, expert = lax.axis_size("seq"), lax.axis_size("expert")
    inner = 2 if seq % 2 == 0 else 1
    core = 2 if expert % 2 == 0 else 1
    return {
        "z": ("seq", inner, seq // inner),
        "x": ("seq", 1, inner),
        "y": ("expert", core, expert // core),
        "c": ("expert", 1, core),
    }


def shift(x, digit, by):
    axis, stride, radix = digit
    pairs = []
    for i in range(lax.axis_size(axis)):
        g = i // stride % radix
        pairs.append((i, i + ((g + by) % radix - g) * stride))
    return lax.ppermute(x, axis, pairs)


def gathered(x, digit, place=0):
    return jnp.stack([x] + [shift(x, digit, d) for d in range(1, digit[2])], axis=place)


def gather_chip(x, beside):
    d = digits()
    half = x.shape[1] // 2
    x = gathered(x, d["z"])
    x, beside = lax.optimization_barrier((x, beside))
    left = gathered(gathered(x[..., :half], d["x"], 1), d["y"], 1)
    right = gathered(gathered(x[..., half:], d["y"], 1), d["x"], 2)
    return jnp.concatenate([left, right], axis=-1), beside


def summed(parts):
    total = parts[0].astype(jnp.float32)
    for part in parts[1:]:
        total = total + part.astype(jnp.float32)
    return total


def leg(x, digit, place):
    parts = [lax.index_in_dim(x, d, place, keepdims=False) for d in range(digit[2])]
    return [parts[0]] + [shift(parts[d], digit, -d) for d in range(1, digit[2])]


def narrow(v):
    return v.astype(jnp.bfloat16)


def behind(values, *others):
    return jax.tree.map(lambda v: lax.optimization_barrier((v, others))[0], values)


def ends(legs):
    return [narrow(summed(parts)) for parts in legs]


def mixture(payload, patch_cap, capacity, w_up, moe_gain, w_router, w_in, w_down):
    d = digits()
    wide = w_up.shape[1]
    paired = w_in.reshape(w_in.shape[1], -1)
    own, paired = gather_chip(payload, paired)
    far, ys, xs = own.shape[:3]
    own = own.reshape((-1,) + own.shape[3:])
    moved = [shift(own, d["c"], by) for by in range(1, d["c"][2])]
    assert len(moved) == 1 and ys * xs % GROUP == 0
    moved = moved[0]
    me = lax.axis_index("expert").astype(jnp.int32).reshape(1)
    weights = (w_up, moe_gain.reshape(1, wide), w_router.T, paired, w_down[0])
    w_last = w_down[0]

    if far == 4:
        streams = [[2], [1, 3], [0]]
    else:
        apart = [*range(1, far), 0]
        streams = [apart[at : at + 2] for at in range(0, far, 2)]

    def blocks_of(zs):
        return [z * ys * xs + at for z in zs for at in range(0, ys * xs, GROUP)]

    def order_of(zs):
        near = len(zs)
        left, right = [], []
        for z in range(near):
            for y in range(ys):
                for x in range(xs):
                    left.append((x * ys + y) * near + z)
                    right.append((y * xs + x) * near + z)
        return left, right

    def shaped(halves, zs):
        left, right = halves
        tail = (len(zs),) + left.shape[1:]
        return [left.reshape((xs, ys) + tail), right.reshape((ys, xs) + tail)]

    def begin(zs, moved):
        got = stream(own, moved, blocks_of(zs), order_of(zs), patch_cap, capacity, me, *weights)
        sent = [shift(v, d["c"], -1) for v in shaped(got[:2], zs)]
        return sent, got

    def finish(zs, sent, hidden, gate, spread):
        kept = gated_share(hidden, gate, spread, w_last, order_of(zs), patch_cap)
        return [narrow(summed(pair)) for pair in zip(shaped(kept, zs), sent)]

    def first_leg(sums):
        return [leg(sums[0], d["x"], 0), leg(sums[1], d["y"], 0)]

    def second_leg(sums):
        return [leg(sums[0], d["y"], 0), leg(sums[1], d["x"], 0)]

    wholes = []

    def last_leg(zs, sums):
        made = []
        for at, z in enumerate(zs):
            if z:
                made.append(jnp.concatenate([v[at] for v in sums], axis=-1))
                wholes.append(shift(made[-1], d["z"], -z))
        return made

    first, second, added = None, None, None
    for zs in streams:
        sent, got = begin(zs, moved if added is None else behind(moved, added))
        hidden, gate, spread = got[2:]
        if second:
            made = last_leg(second[0], ends(behind(second[1], gate)))
            gate, second = behind(gate, made), None
        if first:
            sums = ends(behind(first[1], gate))
            gate, first, second = behind(gate, sums), None, (first[0], second_leg(sums))
        added = finish(zs, sent, hidden, gate, spread)
        first = (zs, first_leg(added))
    zs, legs = first
    if second:
        made = last_leg(second[0], ends(second[1]))
        legs = behind(legs, made)
    sums = ends(legs)
    legs = second_leg(sums)
    if zs != [0]:
        sums = ends(legs)
        last_leg(zs, sums)
        at = zs.index(0)
        legs = [[v[at : at + 1]] for v in sums]
    return wholes, legs


def per_device(
    byte_states,
    patch_start,
    expert_ids,
    enc_gain,
    w_qkv,
    w_out,
    w_xq,
    w_xkv,
    w_up,
    moe_gain,
    w_router,
    w_in,
    w_down,
    dec_gain,
    w_dq,
    w_dkv,
    w_do,
):
    byte_dev = byte_states.shape[0]
    patch_cap = expert_ids.shape[0]
    experts = w_router.shape[1]
    capacity = 12 * patch_cap // (5 * experts)
    both_axes = ("seq", "expert")
    reach = -(-WINDOW // byte_dev)
    place = lax.axis_index(both_axes).astype(jnp.int32).reshape(1)
    opened = opening(
        byte_states,
        patch_start,
        expert_ids,
        reach,
        capacity,
        place,
        enc_gain,
        w_qkv,
        w_out,
        w_xq,
        w_xkv,
    )
    earlier = [passed_along(byte_states, both_axes, by) for by in range(reach, 0, -1)]
    encoded, payload = encode(earlier, opened)
    wholes, halves = mixture(payload, patch_cap, capacity, w_up, moe_gain, w_router, w_in, w_down)
    queries, state = prepare(encoded, payload, patch_cap, dec_gain, w_dq, w_up)
    return decode(state, wholes, halves, encoded, queries, opened[15], w_dkv, w_do)


def solution(mesh):
    in_specs = (
        P(("seq", "expert"), None),
        P(("seq", "expert")),
        P(("seq", "expert"), None),
        P(),
        P(),
        P(),
        P(),
        P(),
        P(),
        P(),
        P(),
        P("expert", None, None, "seq"),
        P("expert", "seq", None),
        P(),
        P(),
        P(),
        P(),
    )
    out_specs = (P(("seq", "expert"), None), P(("seq", "expert"), None))
    return jax.shard_map(
        per_device, mesh=mesh, in_specs=in_specs, out_specs=out_specs, check_vma=False
    )
```

```python
import functools
import math

import jax
import jax.numpy as jnp
from jax import lax
from jax.experimental import pallas as pl
from jax.experimental.pallas import tpu as pltpu
from jax.sharding import PartitionSpec as P

HEADS_L = 8
HEAD = 64
WINDOW = 512


epsilon = 1e-06
very_negative = -1e30


def passed_along(x, axis, by):
    length = lax.axis_size(axis)
    pairs = [(i, i + by) for i in range(length) if 0 <= i + by < length]
    return lax.ppermute(x, axis, pairs)


def normed_rows(x, gain_row):
    wide = x.astype(jnp.float32)
    scale = lax.rsqrt(jnp.mean(wide * wide, axis=-1, keepdims=True) + epsilon)
    return (wide * scale * gain_row).astype(jnp.bfloat16)


def cost(flops):
    return pl.CostEstimate(flops=int(flops), transcendentals=0, bytes_accessed=0)


def mm(a, b):
    return jnp.dot(a, b, preferred_element_type=jnp.float32)


def mm_t(a, b):
    return lax.dot_general(a, b, (((1,), (1,)), ((), ())), preferred_element_type=jnp.float32)


def as_bf16(mask):
    return mask.astype(jnp.float32).astype(jnp.bfloat16)


def iota(shape, dim):
    return lax.broadcasted_iota(jnp.int32, shape, dim)


def attend_part(q, k, v, bias):
    first = iota((1, 2 * HEAD), 1) < HEAD
    q = q * jnp.asarray(1.0 / math.sqrt(HEAD), q.dtype)
    parts = []
    for here in (first, jnp.logical_not(first)):
        scores = mm_t(jnp.where(here, q, jnp.zeros_like(q)), k) + bias
        highest = jnp.max(scores, axis=-1, keepdims=True)
        raised = jnp.exp(scores - highest).astype(jnp.bfloat16)
        parts.append((highest, mm(raised, jnp.where(here, v, jnp.ones_like(v)))))
    return parts


def divided(sums):
    first = iota((1, 2 * HEAD), 1) < HEAD
    outs = [both / pltpu.roll(both, HEAD, 1) for both in sums]
    return jnp.where(first, outs[0], outs[1])


def head_lanes(width):
    lane = iota((1, width), 1)
    return [(lane >= at) & (lane < at + HEAD) for at in range(0, width, HEAD)]


def stacked(x):
    blocks = [jnp.where(here, x, 0.0) for here in head_lanes(x.shape[1])]
    return jnp.concatenate(blocks, axis=0).astype(jnp.bfloat16)


def attend_columns(q, k, v, bias):
    keys, width = k.shape
    scaled = k.astype(jnp.float32) * (1.0 / math.sqrt(HEAD))
    scores = mm_t(stacked(scaled), q).reshape(width // HEAD, keys, q.shape[0]) + bias[None]
    raised = jnp.exp(scores - jnp.max(scores, axis=1, keepdims=True))
    weights = raised / jnp.sum(raised, axis=1, keepdims=True)
    weights = weights.reshape(-1, q.shape[0]).astype(jnp.bfloat16)
    return mm_first(weights, stacked(v.astype(jnp.float32)))


def attend_stacked(q, k, v, bias):
    rows, width = q.shape
    heads = head_lanes(width)
    scaled = q.astype(jnp.float32) * (1.0 / math.sqrt(HEAD))
    scores = mm_t(stacked(scaled), k) + jnp.concatenate([bias] * len(heads), axis=0)
    raised = jnp.exp(scores - jnp.max(scores, axis=-1, keepdims=True))
    mixed = mm(raised.astype(jnp.bfloat16), v) / jnp.sum(raised, axis=-1, keepdims=True)
    out = jnp.zeros((rows, width), jnp.float32)
    for number, here in enumerate(heads):
        out = jnp.where(here, mixed[number * rows : (number + 1) * rows], out)
    return out


def opening_kernel(reach, capacity, *refs):
    place, own_in, flags_in, ids_in, gain_in, w_qkv_in, w_out_in, w_xq_in, w_xkv_in = refs[:9]
    outs, (flags, ids, w_qkv, sem) = refs[9:-4], refs[-4:]
    own, gain, w_kv, w_out, w_xq, w_xkv, queries_out = outs[:7]
    bias_out, since_out, ends_out, member_out, live_out, table_out = outs[7:13]
    highest_out, sums_out, decode_out = outs[13:]
    pairs = [
        (own_in, own),
        (gain_in, gain),
        (w_qkv_in, w_qkv),
        (flags_in, flags),
        (ids_in, ids),
        (w_out_in, w_out),
        (w_xq_in, w_xq),
        (w_xkv_in, w_xkv),
    ]
    copies = [pltpu.make_async_copy(a, b, sem.at[k]) for k, (a, b) in enumerate(pairs)]
    for copy in copies:
        copy.start()
    rows, width = own.shape
    patch_cap = rows * 5 // 32
    keys = reach * rows
    at_query = iota((rows, keys), 0) + keys
    at_key = iota((rows, keys), 1)
    allowed = (at_key > at_query - WINDOW) & (at_key >= (reach - place[0]) * rows)
    bias_out[...] = jnp.where(allowed, 0.0, very_negative)
    for copy in copies[:3]:
        copy.wait()
    normed = normed_rows(own[...], gain[...])
    projected = mm(normed, w_qkv[...]).astype(jnp.bfloat16)
    queries_out[...] = projected[:, :width]
    w_kv[...] = w_qkv[:, width:]
    back = iota((rows, rows), 0) - iota((rows, rows), 1)
    own_bias = jnp.where((back >= 0) & (back < WINDOW), 0.0, very_negative)
    lanes = 2 * HEAD
    for at in range(0, width, lanes):
        parts = attend_part(
            projected[:, at : at + lanes],
            projected[:, width + at : width + at + lanes],
            projected[:, 2 * width + at : 2 * width + at + lanes],
            own_bias,
        )
        for head, (highest, both) in enumerate(parts, at // HEAD):
            highest_out[head] = jnp.broadcast_to(highest, both.shape)
            sums_out[head] = both
    copies[3].wait()
    flag = flags[...]
    at_row, at_col = iota((rows, rows), 0), iota((rows, rows), 1)
    upto = at_col <= at_row
    opened = jnp.max(jnp.where(upto & (flag == 1), at_col, 0), axis=1, keepdims=True)
    since_out[...] = iota((rows, 1), 0) - opened
    eight = jnp.broadcast_to(flag, (8, rows)).astype(jnp.float32).astype(jnp.bfloat16)
    number = mm(eight, as_bf16(at_row <= at_col))[:1].astype(jnp.int32) - 1
    at_byte = iota((patch_cap, rows), 1)
    member = number == iota((patch_cap, rows), 0)
    decode_out[...] = jnp.where(iota((patch_cap, rows), 0) <= number, 0.0, very_negative)
    last = jnp.max(jnp.where(member, at_byte, -1), axis=1, keepdims=True)
    live_out[...] = (last >= 0).astype(jnp.float32)
    ends_out[...] = as_bf16(member & (at_byte == last))
    member_out[...] = jnp.where(member, 0.0, very_negative)

    copies[4].wait()
    square = (patch_cap, patch_cap)
    same = iota(square, 0) == iota(square, 1)
    earlier_slot = iota(square, 0) < iota(square, 1)
    id_rows = [ids[k : k + 1, :] for k in range(2)]
    id_cols = [jnp.sum(jnp.where(same, row, 0), axis=1, keepdims=True) for row in id_rows]
    targets = []
    for row in id_rows:
        named = sum((col == row).astype(jnp.int32) for col in id_cols)
        rank = jnp.sum(jnp.where(earlier_slot, named, 0), axis=0, keepdims=True)
        targets.append(row * capacity + rank)
    extra = table_out.shape[0]
    at_extra = iota((extra, patch_cap), 0)
    table = jnp.where(at_extra == 0, targets[0], jnp.where(at_extra == 1, targets[1], 0))
    table_out[...] = jnp.zeros_like(table_out)
    table_out[:, :patch_cap] = table.astype(jnp.float32).astype(jnp.bfloat16)
    for copy in copies[5:]:
        copy.wait()


def opening(byte_states, patch_start, expert_ids, reach, capacity, place, enc_gain, *ws):
    rows, width = byte_states.shape
    w_qkv, w_out, w_xq, w_xkv = ws
    patch_cap = expert_ids.shape[0]
    extra = -(-(patch_cap + 2) // 16) * 16 - patch_cap
    keys = reach * rows
    heads = width // HEAD
    vmem, anywhere = pl.BlockSpec(memory_space=pltpu.VMEM), pl.BlockSpec(memory_space=pltpu.HBM)
    like = jax.ShapeDtypeStruct
    bf16, f32 = jnp.bfloat16, jnp.float32
    return pl.pallas_call(
        functools.partial(opening_kernel, reach, capacity),
        out_shape=(
            like((rows, width), bf16),
            like((1, width), f32),
            like((width, 2 * width), bf16),
            like(w_out.shape, bf16),
            like(w_xq.shape, bf16),
            like(w_xkv.shape, bf16),
            like((rows, width), bf16),
            like((rows, keys), f32),
            like((rows, 1), jnp.int32),
            like((patch_cap, rows), bf16),
            like((patch_cap, rows), f32),
            like((patch_cap, 1), f32),
            like((extra, width), bf16),
            like((heads, rows, 2 * HEAD), f32),
            like((heads, rows, 2 * HEAD), f32),
            like((patch_cap, rows), f32),
        ),
        in_specs=[pl.BlockSpec(memory_space=pltpu.SMEM)] + [anywhere] * 8,
        out_specs=(vmem,) * 16,
        scratch_shapes=[
            pltpu.VMEM((1, rows), jnp.int32),
            pltpu.VMEM((2, patch_cap), jnp.int32),
            pltpu.VMEM(w_qkv.shape, bf16),
            pltpu.SemaphoreType.DMA((8,)),
        ],
        cost_estimate=cost(4 * rows * width * 3 * width),
        compiler_params=pltpu.CompilerParams(vmem_limit_bytes=16 * 1024 * 1024),
    )(
        place,
        *[
            pltpu.with_memory_space_constraint(v, pltpu.HBM)
            for v in (
                byte_states,
                patch_start.reshape(1, rows),
                expert_ids.T,
                enc_gain.reshape(1, width),
                *ws,
            )
        ],
    )


def encoder_kernel(reach, *refs):
    earlier, refs = refs[:reach], refs[reach:]
    own, gain, w_kv, w_out, w_xq, w_xkv, queries = refs[:7]
    bias, since, ends, member_bias, live, table, own_highest, own_sums = refs[7:15]
    encoded_out, payload_out, pairs_ref, mixed_ref = refs[15:]
    rows, width = own.shape
    patch_cap = ends.shape[0]
    for at, block in enumerate(earlier):
        moved = normed_rows(block[...], gain[...])
        pairs_ref[at * rows : (at + 1) * rows, :] = mm(moved, w_kv[...]).astype(jnp.bfloat16)
    lanes = 2 * HEAD
    for at in range(0, width, lanes):
        parts = attend_part(
            queries[:, at : at + lanes],
            pairs_ref[:, at : at + lanes],
            pairs_ref[:, width + at : width + at + lanes],
            bias[...],
        )
        sums = []
        for head, (highest, both) in enumerate(parts, at // HEAD):
            before = own_highest[head]
            top = jnp.maximum(highest, before)
            sums.append(both * jnp.exp(highest - top) + own_sums[head] * jnp.exp(before - top))
        mixed_ref[:, at : at + lanes] = divided(sums).astype(jnp.bfloat16)
    encoded = (own[...].astype(jnp.float32) + mm(mixed_ref[...], w_out[...])).astype(jnp.bfloat16)
    encoded_out[...] = encoded

    inside = since[...]
    highest = encoded.astype(jnp.float32)
    step = 1
    while step < rows:
        highest = jnp.where(
            inside >= step, jnp.maximum(highest, pltpu.roll(highest, step, 0)), highest
        )
        step *= 2
    pooled = mm(ends[...], highest.astype(jnp.bfloat16))
    patch_queries = mm(pooled.astype(jnp.bfloat16), w_xq[...]).astype(jnp.bfloat16)
    byte_pairs = mm(encoded, w_xkv[...]).astype(jnp.bfloat16)
    mixed = attend_stacked(
        patch_queries, byte_pairs[:, :width], byte_pairs[:, width:], member_bias[...]
    )
    total = jnp.where(live[...] > 0.0, pooled + mixed, 0.0)
    payload_out[:patch_cap, :] = total.astype(jnp.bfloat16)
    payload_out[patch_cap:, :] = table[...]


def encode(earlier, opened):
    rows, width = opened[0].shape
    reach = len(earlier)
    vmem = pl.BlockSpec(memory_space=pltpu.VMEM)
    payload_rows = opened[9].shape[0] + opened[12].shape[0]
    return pl.pallas_call(
        functools.partial(encoder_kernel, reach),
        out_shape=(
            jax.ShapeDtypeStruct((rows, width), jnp.bfloat16),
            jax.ShapeDtypeStruct((payload_rows, width), jnp.bfloat16),
        ),
        in_specs=[vmem] * (15 + reach),
        out_specs=(vmem, vmem),
        scratch_shapes=[
            pltpu.VMEM((reach * rows, 2 * width), jnp.bfloat16),
            pltpu.VMEM((rows, width), jnp.bfloat16),
        ],
        cost_estimate=cost(24 * rows * width * (reach + 1) * rows),
        compiler_params=pltpu.CompilerParams(vmem_limit_bytes=16 * 1024 * 1024),
    )(*earlier, *opened[:15])


def mm_first(a, b):
    return lax.dot_general(a, b, (((0,), (0,)), ((), ())), preferred_element_type=jnp.float32)


def counted_from(values, step, most):
    return sum((values >= step * k).astype(jnp.int32) for k in range(1, most))


GROUP = 4


def give_back(term, spread, group, halves, order):
    for half, (out, places) in enumerate(zip(halves, order)):
        width = out.shape[-1]
        total = mm_first(spread, term[:, half * width : (half + 1) * width]).astype(jnp.bfloat16)
        block = out.shape[-2]
        for s in range(GROUP):
            out[places[group * GROUP + s]] = total[s * block : (s + 1) * block]


def stream_kernel(patch_cap, capacity, experts, blocks, order, *refs):
    me_ref, *rows_refs, w_up, gain, router, w_in, w_down = refs[:10]
    outs = refs[10:12]
    hidden_ref, gate_ref, spread_ref, all_hidden, later_spread, routed_ref, parts_ref = refs[12:]
    held = rows_refs[0].shape[1]
    per = GROUP * capacity
    kept = len(blocks) // 2
    me = me_ref[0]
    slots = iota((per, 1), 0)
    source_of_slot = counted_from(slots, capacity, GROUP)
    place_of_slot = slots - source_of_slot * capacity + me * capacity
    lanes = 128

    def spreader(block):
        at_from, at_to = iota((GROUP * lanes, GROUP * block), 0), iota((GROUP * lanes, GROUP * block), 1)
        source = counted_from(at_from, lanes, GROUP)
        within = at_from - source * lanes
        return as_bf16((at_to == source * block + within) & (within < block))

    spread_held, spread_cap = spreader(held), spreader(patch_cap)

    def matched(table, spread, block):
        targets = mm(table, spread).astype(jnp.int32)
        at = iota((1, GROUP * block), 1)
        source = counted_from(at, block, GROUP)
        first, second = targets[0:1], targets[1:2]
        hit = (first == place_of_slot) | (second == place_of_slot)
        hit = hit & (source == source_of_slot) & (at - source * block < patch_cap)
        named = [counted_from(t, capacity, experts) for t in (first, second)]
        return hit, jnp.where(named[0] == me, named[1], named[0])

    others = []
    for g, begin in enumerate(blocks):
        left_ref, right_ref = rows_refs[:2] if g < kept else rows_refs[2:]
        tables = []
        for s in range(begin, begin + GROUP):
            block = left_ref[s, held - 16 : held, :lanes].astype(jnp.float32)
            tables.append(block[patch_cap - (held - 16) : patch_cap - (held - 16) + 8])
        table = jnp.concatenate(tables, axis=1).astype(jnp.bfloat16)
        hit, other = matched(table, spread_held, held)
        others.append(jnp.sum(jnp.where(hit, other, 0), axis=1, keepdims=True))
        half = left_ref.shape[2]
        for at, ref in ((0, left_ref), (half, right_ref)):
            block = ref[begin : begin + GROUP].reshape(GROUP * held, half)
            routed_ref[g * per : (g + 1) * per, at : at + half] = mm(as_bf16(hit), block).astype(
                jnp.bfloat16
            )
        hit, _ = matched(table, spread_cap, patch_cap)
        if g < kept:
            spread_ref[g] = as_bf16(hit)
        else:
            later_spread[g - kept] = as_bf16(hit)
    other = jnp.concatenate(others, axis=0)

    state = mm(routed_ref[...], w_up[...]).astype(jnp.bfloat16).astype(jnp.float32)
    gained = (state * gain[...]).astype(jnp.bfloat16)
    scale = lax.rsqrt(jnp.mean(state * state, axis=-1, keepdims=True) + epsilon)

    parts_ref[...] = jnp.zeros_like(parts_ref)
    left = router[...]
    for part in range(3):
        here = left.astype(jnp.bfloat16).astype(jnp.float32)
        parts_ref[8 * part : 8 * part + experts, :] = here
        left = left - here
    parts = parts_ref[...].astype(jnp.bfloat16)
    deep = parts.shape[1] // 4
    logits = sum(
        mm_t(gained[:, k * deep : (k + 1) * deep], parts[:, k * deep : (k + 1) * deep])
        for k in range(4)
    )
    logits = logits * scale
    expert_of_lane = iota((1, parts_ref.shape[0]), 1) & 7
    mine = jnp.sum(jnp.where(expert_of_lane == me, logits, 0.0), axis=1, keepdims=True)
    rival = jnp.sum(jnp.where(expert_of_lane == other, logits, 0.0), axis=1, keepdims=True)
    highest = jnp.maximum(mine, rival)
    raised = jnp.exp(mine - highest)
    gate = raised / (raised + jnp.exp(rival - highest))

    hidden_share = all_hidden.shape[1]
    chunk = 256 if hidden_share % 256 == 0 else hidden_share
    for at in range(0, hidden_share, chunk):
        opened = mm(gained, w_in[:, at : at + chunk]) * scale
        upper = mm(gained, w_in[:, hidden_share + at : hidden_share + at + chunk]) * scale
        all_hidden[:, at : at + chunk] = (opened / (1.0 + jnp.exp(-opened)) * upper).astype(
            jnp.bfloat16
        )
    first = kept * per
    hidden_ref[...] = all_hidden[:first, :]
    gate_ref[...] = gate[:first]
    term = (mm(all_hidden[first:, :], w_down[...]) * gate[first:]).astype(jnp.bfloat16)
    for g in range(kept):
        give_back(term[g * per : (g + 1) * per], later_spread[g], g, outs, order)


def share_kernel(order, hidden, gate, spread, w_down, *outs):
    groups, per, _ = spread.shape
    term = (mm(hidden[...], w_down[...]) * gate[...]).astype(jnp.bfloat16)
    for g in range(groups):
        give_back(term[g * per : (g + 1) * per], spread[g], g, outs, order)


def share_shapes(sources, patch_cap, wide):
    half = jax.ShapeDtypeStruct((sources, patch_cap, wide // 2), jnp.bfloat16)
    return (half, half)


def stream(own, moved, blocks, order, patch_cap, capacity, me, w_up, gain, router, w_in, w_down):
    width = w_up.shape[0]
    experts, wide = router.shape
    vmem = pl.BlockSpec(memory_space=pltpu.VMEM)
    per = GROUP * capacity
    slots = 2 * len(blocks) * per
    spread = jax.ShapeDtypeStruct((len(blocks), per, GROUP * patch_cap), jnp.bfloat16)
    return pl.pallas_call(
        functools.partial(stream_kernel, patch_cap, capacity, experts, blocks * 2, order),
        out_shape=share_shapes(len(blocks) * GROUP, patch_cap, wide)
        + (
            jax.ShapeDtypeStruct((slots // 2, w_down.shape[0]), jnp.bfloat16),
            jax.ShapeDtypeStruct((slots // 2, 1), jnp.float32),
            spread,
        ),
        in_specs=[pl.BlockSpec(memory_space=pltpu.SMEM)] + [vmem] * 9,
        out_specs=(vmem,) * 5,
        scratch_shapes=[
            pltpu.VMEM((slots, w_down.shape[0]), jnp.bfloat16),
            pltpu.VMEM(spread.shape, jnp.bfloat16),
            pltpu.VMEM((slots, width), jnp.bfloat16),
            pltpu.VMEM((24, wide), jnp.float32),
        ],
        cost_estimate=cost(slots * wide * (width + w_in.shape[1]) // 4),
        compiler_params=pltpu.CompilerParams(vmem_limit_bytes=24 * 1024 * 1024),
    )(me, *own, *moved, w_up, gain, router, w_in, w_down)


def gated_share(hidden, gate, spread, w_down, order, patch_cap):
    groups = spread.shape[0]
    wide = w_down.shape[1]
    vmem = pl.BlockSpec(memory_space=pltpu.VMEM)
    return pl.pallas_call(
        functools.partial(share_kernel, order),
        out_shape=share_shapes(groups * GROUP, patch_cap, wide),
        in_specs=[vmem] * 4,
        out_specs=(vmem,) * 2,
        cost_estimate=cost(1000),
        compiler_params=pltpu.CompilerParams(vmem_limit_bytes=16 * 1024 * 1024),
    )(hidden, gate, spread, w_down)


def prepare_kernel(encoded, payload, gain, w_dq, w_up, queries, state):
    queries[...] = mm(normed_rows(encoded[...], gain[...]), w_dq[...]).astype(jnp.bfloat16)
    state[...] = mm(payload[: state.shape[0], :], w_up[...]).astype(jnp.bfloat16)


def prepare(encoded, payload, patch_cap, gain, w_dq, w_up):
    vmem = pl.BlockSpec(memory_space=pltpu.VMEM)
    return pl.pallas_call(
        prepare_kernel,
        out_shape=(
            jax.ShapeDtypeStruct(encoded.shape, jnp.bfloat16),
            jax.ShapeDtypeStruct((patch_cap, w_up.shape[1]), jnp.bfloat16),
        ),
        in_specs=[vmem] * 5,
        out_specs=(vmem, vmem),
        cost_estimate=cost(2 * patch_cap * w_up.size),
        compiler_params=pltpu.CompilerParams(vmem_limit_bytes=8 * 1024 * 1024),
    )(encoded, payload, gain.reshape(1, -1), w_dq, w_up)


def decode_kernel(wholes, *refs):
    state, *parts = refs[:-7]
    encoded, queries, bias, w_dkv, w_do, bytes_out, patch_out = refs[-7:]
    width = encoded.shape[1]
    wide = state.shape[1] // 2
    per = (len(parts) - wholes) // 2
    pairs = 0.0
    for half in range(2):
        here = slice(half * wide, (half + 1) * wide)
        total = state[:, here].astype(jnp.float32)
        for part in parts[wholes + half * per : wholes + (half + 1) * per]:
            total = total + part[0].astype(jnp.float32)
        for part in parts[:wholes]:
            total = total + part[:, here].astype(jnp.float32)
        states = total.astype(jnp.bfloat16)
        patch_out[:, here] = states
        pairs = pairs + mm(states, w_dkv[here, :])
    pairs = pairs.astype(jnp.bfloat16)
    mixed = attend_columns(queries[...], pairs[:, :width], pairs[:, width:], bias[...])
    bytes_out[...] = (
        encoded[...].astype(jnp.float32) + mm(mixed.astype(jnp.bfloat16), w_do[...])
    ).astype(jnp.bfloat16)


def decode(state, wholes, halves, encoded, queries, bias, w_dkv, w_do):
    vmem = pl.BlockSpec(memory_space=pltpu.VMEM)
    parts = [*wholes, *halves[0], *halves[1]]
    return pl.pallas_call(
        functools.partial(decode_kernel, len(wholes)),
        out_shape=(
            jax.ShapeDtypeStruct(encoded.shape, jnp.bfloat16),
            jax.ShapeDtypeStruct(state.shape, jnp.bfloat16),
        ),
        in_specs=[vmem] * (6 + len(parts)),
        out_specs=(vmem, vmem),
        cost_estimate=cost(4 * 256 * w_dkv.size),
        compiler_params=pltpu.CompilerParams(vmem_limit_bytes=12 * 1024 * 1024),
    )(state, *parts, encoded, queries, bias, w_dkv, w_do)


def digits():
    seq, expert = lax.axis_size("seq"), lax.axis_size("expert")
    inner = 2 if seq % 2 == 0 else 1
    core = 2 if expert % 2 == 0 else 1
    return {
        "z": ("seq", inner, seq // inner),
        "x": ("seq", 1, inner),
        "y": ("expert", core, expert // core),
        "c": ("expert", 1, core),
    }


def shift(x, digit, by):
    axis, stride, radix = digit
    pairs = []
    for i in range(lax.axis_size(axis)):
        g = i // stride % radix
        pairs.append((i, i + ((g + by) % radix - g) * stride))
    return lax.ppermute(x, axis, pairs)


def gathered(x, digit, place=0):
    return jnp.stack([x] + [shift(x, digit, d) for d in range(1, digit[2])], axis=place)


def gather_chip(x, beside):
    d = digits()
    half = x.shape[1] // 2
    x = gathered(x, d["z"])
    x, beside = lax.optimization_barrier((x, beside))
    left = gathered(gathered(x[..., :half], d["x"], 1), d["y"], 1)
    right = gathered(gathered(x[..., half:], d["y"], 1), d["x"], 2)
    return left, right, beside


def summed(parts):
    total = parts[0].astype(jnp.float32)
    for part in parts[1:]:
        total = total + part.astype(jnp.float32)
    return total


def leg(x, digit, place):
    parts = [lax.index_in_dim(x, d, place, keepdims=False) for d in range(digit[2])]
    return [parts[0]] + [shift(parts[d], digit, -d) for d in range(1, digit[2])]


def narrow(v):
    return v.astype(jnp.bfloat16)


def behind(values, *others):
    return jax.tree.map(lambda v: lax.optimization_barrier((v, others))[0], values)


def ends(legs):
    return [narrow(summed(parts)) for parts in legs]


def mixture(payload, patch_cap, capacity, w_up, moe_gain, w_router, w_in, w_down):
    d = digits()
    wide = w_up.shape[1]
    paired = w_in.reshape(w_in.shape[1], -1)
    *own, paired = gather_chip(payload, paired)
    far, ys, xs = own[0].shape[:3]
    own = [v.reshape((-1,) + v.shape[3:]) for v in own]
    assert d["c"][2] == 2 and ys * xs % GROUP == 0
    moved = [shift(v, d["c"], 1) for v in own]
    me = lax.axis_index("expert").astype(jnp.int32).reshape(1)
    weights = (w_up, moe_gain.reshape(1, wide), w_router.T, paired, w_down[0])
    w_last = w_down[0]

    if far == 4:
        streams = [[2], [1, 3], [0]]
    else:
        apart = [*range(1, far), 0]
        streams = [apart[at : at + 2] for at in range(0, far, 2)]

    def blocks_of(zs):
        return [z * ys * xs + at for z in zs for at in range(0, ys * xs, GROUP)]

    def order_of(zs):
        near = len(zs)
        left, right = [], []
        for z in range(near):
            for y in range(ys):
                for x in range(xs):
                    left.append((x * ys + y) * near + z)
                    right.append((y * xs + x) * near + z)
        return left, right

    def shaped(halves, zs):
        left, right = halves
        tail = (len(zs),) + left.shape[1:]
        return [left.reshape((xs, ys) + tail), right.reshape((ys, xs) + tail)]

    def begin(zs, moved):
        got = stream(own, moved, blocks_of(zs), order_of(zs), patch_cap, capacity, me, *weights)
        sent = [shift(v, d["c"], -1) for v in shaped(got[:2], zs)]
        return sent, got

    def finish(zs, sent, hidden, gate, spread):
        kept = gated_share(hidden, gate, spread, w_last, order_of(zs), patch_cap)
        return [narrow(summed(pair)) for pair in zip(shaped(kept, zs), sent)]

    def first_leg(sums):
        return [leg(sums[0], d["x"], 0), leg(sums[1], d["y"], 0)]

    def second_leg(sums):
        return [leg(sums[0], d["y"], 0), leg(sums[1], d["x"], 0)]

    wholes = []

    def last_leg(zs, sums):
        made = []
        for at, z in enumerate(zs):
            if z:
                made.append(jnp.concatenate([v[at] for v in sums], axis=-1))
                wholes.append(shift(made[-1], d["z"], -z))
        return made

    first, second, added = None, None, None
    for zs in streams:
        sent, got = begin(zs, moved if added is None else behind(moved, added))
        hidden, gate, spread = got[2:]
        if second:
            made = last_leg(second[0], ends(behind(second[1], gate)))
            gate, second = behind(gate, made), None
        if first:
            sums = ends(behind(first[1], gate))
            gate, first, second = behind(gate, sums), None, (first[0], second_leg(sums))
        added = finish(zs, sent, hidden, gate, spread)
        first = (zs, first_leg(added))
    zs, legs = first
    if second:
        made = last_leg(second[0], ends(second[1]))
        legs = behind(legs, made)
    sums = ends(legs)
    legs = second_leg(sums)
    if zs != [0]:
        sums = ends(legs)
        last_leg(zs, sums)
        at = zs.index(0)
        legs = [[v[at : at + 1]] for v in sums]
    return wholes, legs


def per_device(
    byte_states,
    patch_start,
    expert_ids,
    enc_gain,
    w_qkv,
    w_out,
    w_xq,
    w_xkv,
    w_up,
    moe_gain,
    w_router,
    w_in,
    w_down,
    dec_gain,
    w_dq,
    w_dkv,
    w_do,
):
    byte_dev = byte_states.shape[0]
    patch_cap = expert_ids.shape[0]
    experts = w_router.shape[1]
    capacity = 12 * patch_cap // (5 * experts)
    both_axes = ("seq", "expert")
    reach = -(-WINDOW // byte_dev)
    place = lax.axis_index(both_axes).astype(jnp.int32).reshape(1)
    opened = opening(
        byte_states,
        patch_start,
        expert_ids,
        reach,
        capacity,
        place,
        enc_gain,
        w_qkv,
        w_out,
        w_xq,
        w_xkv,
    )
    earlier = [passed_along(byte_states, both_axes, by) for by in range(reach, 0, -1)]
    encoded, payload = encode(earlier, opened)
    wholes, halves = mixture(payload, patch_cap, capacity, w_up, moe_gain, w_router, w_in, w_down)
    queries, state = prepare(encoded, payload, patch_cap, dec_gain, w_dq, w_up)
    return decode(state, wholes, halves, encoded, queries, opened[15], w_dkv, w_do)


def solution(mesh):
    in_specs = (
        P(("seq", "expert"), None),
        P(("seq", "expert")),
        P(("seq", "expert"), None),
        P(),
        P(),
        P(),
        P(),
        P(),
        P(),
        P(),
        P(),
        P("expert", None, None, "seq"),
        P("expert", "seq", None),
        P(),
        P(),
        P(),
        P(),
    )
    out_specs = (P(("seq", "expert"), None), P(("seq", "expert"), None))
    return jax.shard_map(
        per_device, mesh=mesh, in_specs=in_specs, out_specs=out_specs, check_vma=False
    )
```
